32 devices in a mesh: parts: 2 (over x), sta: 16 (over z, y, core).
Axes of the slice: x: 2, y: 2, z: 4, core: 2. Of those that a mesh axis runs over, the one named last changes fastest.
Arguments:
- raw_traces: bfloat16 [512, 16384], P('parts', 'sta'), parts along dimension 0, may hold values from -6 to 6
- filter_taps: bfloat16 [256], replicated, may hold values from -0.375 to 0.375
- station_order: int32 [512], P('parts'), parts along dimension 0, may hold values from 0 to 255, each once
- window_starts: int32 [32], P('parts'), parts along dimension 0, may hold values from 0 to 2048, as said below
- pairing: int32 [4, 16], replicated, may hold values from 0 to 15, as said below
Outputs:
- correlation: float32 [4, 512, 16, 256], P(None, ('parts', 'sta')), parts along dimension 1
The draws below stay inside these ranges and needn't reach their ends.
There are 2 independent parts, one for each index of `parts`. The reference program is written for one: setup_inputs(seed, part) draws one part's arguments, and reference() takes and returns one part's arrays. A program takes and returns all parts, laid end to end along the dimension named above; an argument that names none is the same for every part. Nothing has to cross between parts.
Inputs may be any that keep to these rules, and one draw needn't show every extreme that they name: Each station appears once; block b holds the stations station_order[b * 16 + j], j < 16. `window_starts`: starts never fall; the first is 0 and the last is 2048; consecutive starts differ by at most 273. Row r is one round of a single round-robin tournament over the 16 blocks: pairing[r, pairing[r, b]] = b, pairing[r, b] != b, and no two rows pair the same two blocks.
All inputs are finite; a program needn't handle non-finite values.
Results may differ from the reference program's by a relative error of at most 0.0049.
Values may be sent and summed in bfloat16 or wider, within the bound.
A program may use at most 128 MiB of HBM per device.

```python
import math
import jax
import jax.numpy as jnp
from jax import lax

SB = 16
NW = 16
DEC = 4
TAPS = 256
SEG = 2048
BAND = 64
LAGS = 256
ROUNDS = 4
BINS = 1024
BLOCKS = 16
STATIONS = 256
TIME = 16384
SAMPLES = 4096


def draw_window_starts(key, part):
    free_room = SAMPLES - SEG
    stride = free_room // (NW - 1)
    window_index = jnp.arange(NW, dtype=jnp.int32)
    anchor = window_index * free_room // (NW - 1)
    jitter = jax.random.randint(key, (NW,), 0, stride + 1, dtype=jnp.int32) * (window_index > 0).astype(jnp.int32)
    return jnp.minimum(anchor + jitter, free_room).astype(jnp.int32)


def draw_pairing(key, part):
    relabel = jax.random.permutation(jax.random.fold_in(key, 7), BLOCKS).astype(jnp.int32)
    inverse = jnp.argsort(relabel).astype(jnp.int32)
    rounds_col = jnp.arange(1, ROUNDS + 1, dtype=jnp.int32)[:, None]
    labels = relabel[None, :]
    mirror = (2 * rounds_col - labels) % (BLOCKS - 1)
    partner_label = jnp.where(labels == BLOCKS - 1, rounds_col % (BLOCKS - 1), jnp.where(mirror == labels, BLOCKS - 1, mirror))
    return jnp.take(inverse, partner_label).astype(jnp.int32)


def shard_levels(own_key, dims, split, least, largest):
    loudness = 1.0
    for position, parts in split:
        heights = jax.random.uniform(jax.random.fold_in(jax.random.fold_in(own_key, 6), position), (parts,), jnp.float32, least / len(split), largest / len(split))
        loudness = loudness * jnp.repeat(jnp.exp(heights), dims[position] // parts).reshape((-1,) + (1,) * (len(dims) - 1 - position))
    return loudness


def centred(stream_key, dims, width, limit, cuts=(), kind=jnp.bfloat16):
    factor_of = shard_levels(stream_key, dims, cuts, -0.22, 0.18) if cuts else 1.0
    entries = jax.random.normal(stream_key, dims, jnp.float32) * width * factor_of
    return jnp.minimum(jnp.maximum(entries, -limit), limit).astype(kind)


def setup_inputs(seed: int = 0, part: int = 0) -> dict:
    key_of = jax.random.split(jax.random.key(seed), 6)
    part_splits = jax.random.split(jax.random.fold_in(key_of[5], part), 6)
    raw_traces = centred(part_splits[0], (STATIONS, TIME), 1.0, 6.0, ((1, 16),))
    filter_taps = centred(key_of[1], (TAPS,), TAPS ** -0.5, 0.375)
    station_order = jax.random.permutation(part_splits[2], STATIONS).astype(jnp.int32)
    window_starts = draw_window_starts(jax.random.fold_in(jax.random.fold_in(key_of[5], part), 71), part)
    pairing = draw_pairing(jax.random.fold_in(key_of[5], 71), part)
    return {"raw_traces": raw_traces, "filter_taps": filter_taps, "station_order": station_order, "window_starts": window_starts, "pairing": pairing}


def decimate(signal, leading, filter_taps, factor):
    row_count, length = signal.shape
    outputs = length // factor
    per_tile = math.gcd(outputs, 128)
    tile_span = per_tile * factor
    margin = leading.shape[1]
    pieces = 1 + (margin + tile_span - 1) // tile_span
    tile_count = outputs // per_tile
    padded = jnp.concatenate([leading, signal, jnp.zeros((row_count, (pieces - 1) * tile_span - margin), signal.dtype)], axis=1)
    tap_count = filter_taps.shape[0]
    positions = jnp.arange(pieces * tile_span, dtype=jnp.int32)[:, None]
    column = jnp.arange(per_tile, dtype=jnp.int32)[None, :]
    tap_index = column * factor + tap_count - 1 - positions
    inside = (tap_index >= 0) & (tap_index < tap_count)
    banded = jnp.where(inside, jnp.take(filter_taps, jnp.clip(tap_index, 0, tap_count - 1)), jnp.zeros((), filter_taps.dtype))
    summed = jnp.zeros((row_count, tile_count, per_tile), jnp.float32)
    for section_index in range(pieces):
        segment = padded[:, section_index * tile_span:section_index * tile_span + length].reshape(row_count, tile_count, tile_span)
        summed = summed + jnp.einsum('rtu,ui->rti', segment.astype(jnp.float32), banded[section_index * tile_span:(section_index + 1) * tile_span].astype(jnp.float32), precision=lax.Precision.HIGHEST)
    return summed.reshape(row_count, outputs)

def dft_matrix(seg_length, bin_count):
    sample = jnp.arange(seg_length, dtype=jnp.int32)
    frequency = jnp.arange(bin_count, dtype=jnp.int32)
    angles = (frequency[:, None] * sample[None, :] % seg_length).astype(jnp.float32) * (2.0 * math.pi / seg_length)
    taper_curve = 0.5 - 0.5 * jnp.cos(sample.astype(jnp.float32) * (2.0 * math.pi / seg_length))
    joined = jnp.concatenate([jnp.cos(angles) * taper_curve[None, :], -jnp.sin(angles) * taper_curve[None, :]], axis=0)
    return joined.astype(jnp.bfloat16)

def lag_matrix(seg_length, bin_count, lag_count, window_count):
    frequency = jnp.arange(bin_count, dtype=jnp.int32)
    lag_offset = jnp.arange(lag_count, dtype=jnp.int32) - lag_count // 2 + seg_length
    angles = (frequency[:, None] * lag_offset[None, :] % seg_length).astype(jnp.float32) * (2.0 * math.pi / seg_length)
    normalizer = 1.0 / math.sqrt(bin_count * window_count)
    return jnp.stack([jnp.cos(angles) * normalizer, -jnp.sin(angles) * normalizer]).astype(jnp.bfloat16)

def whiten(spectrum, band_width):
    halves, bin_count, station_count, window_count = spectrum.shape
    grouped = spectrum.reshape(halves, bin_count // band_width, band_width, station_count, window_count)
    band_level = lax.optimization_barrier(jnp.sum(grouped * grouped, axis=(0, 2))) / (2 * band_width)
    scaled = grouped * (1.0 / jnp.sqrt(band_level + 1e-06))[None, :, None]
    return scaled.reshape(spectrum.shape).astype(jnp.bfloat16)

def cross_spectra(left_spec, right_spec):
    left_wide = left_spec.astype(jnp.float32)
    right_wide = right_spec.astype(jnp.float32)
    turned = jnp.stack([right_wide, jnp.stack([-right_wide[1], right_wide[0]])])
    return jnp.einsum('cfsw,kcftw->kfst', left_wide, turned, precision=lax.Precision.HIGHEST)

def reference(raw_traces, filter_taps, station_order, window_starts, pairing):
    ordered = jnp.take(raw_traces, station_order, axis=0)
    leading = jnp.zeros((STATIONS, TAPS - DEC), raw_traces.dtype)
    low_rate = lax.optimization_barrier(decimate(ordered, leading, filter_taps, DEC).astype(jnp.bfloat16))
    dft_table = lax.optimization_barrier(dft_matrix(SEG, BINS)).astype(jnp.float32)

    def block_spectra(block_rows):
        windows = jax.vmap(lambda first_sample: lax.dynamic_slice_in_dim(block_rows, first_sample, SEG, 1))(window_starts)
        spectrum = jnp.einsum('kl,wsl->ksw', dft_table, windows.astype(jnp.float32), precision=lax.Precision.HIGHEST)
        return lax.optimization_barrier(whiten(spectrum.reshape(2, BINS, SB, NW), BAND))
    whitened = lax.map(block_spectra, low_rate.reshape(BLOCKS, SB, SAMPLES))
    lag_table = lax.optimization_barrier(lag_matrix(SEG, BINS, LAGS, NW)).astype(jnp.float32)

    def one_round(partners):

        def one_block(block_index):
            own_spec = whitened[block_index]
            theirs = whitened[partners[block_index]]
            cross_spec = lax.optimization_barrier(cross_spectra(own_spec, theirs).astype(jnp.bfloat16))
            flattened = cross_spec.astype(jnp.float32).reshape(2, BINS, SB * SB)
            return jnp.einsum('kfp,kfl->pl', flattened, lag_table, precision=lax.Precision.HIGHEST).reshape(SB, SB, LAGS)
        return lax.map(one_block, jnp.arange(BLOCKS, dtype=jnp.int32)).reshape(BLOCKS * SB, SB, LAGS)
    return lax.map(one_round, pairing)
```

```python
import functools
import math

import jax
import jax.numpy as jnp
import ml_dtypes
import numpy as np
from jax import lax
from jax.experimental import pallas as pl
from jax.experimental.pallas import tpu as pltpu
from jax.sharding import PartitionSpec as P

SB = 16
DEC = 4
TAPS = 256
SEG = 2048
BAND = 64
LAGS = 256
ROUNDS = 4
BINS = 1024
LANE = 128
SPAN = LANE * DEC + TAPS
GROUPS = ROUNDS + 1
ROWS = GROUPS * SB
THEIRS = ROUNDS * SB
FOLD = SEG // 2
FT = 256
TILES = BINS // FT
PACK = 8
NT = (((1,), (1,)), ((), ()))
QUAD = 4
MESH = pl.DeviceIdType.MESH


def dft_table():
    sample = np.arange(FOLD)
    frequency = np.arange(BINS)
    angles = (sample[None, :] * frequency[:, None] % SEG) * (2.0 * math.pi / SEG)
    taper = (0.5 - 0.5 * np.cos(sample * (2.0 * math.pi / SEG)))[None, :]
    both = np.stack([np.cos(angles) * taper, -np.sin(angles) * taper])
    both[0, :, 0] = 1.0 - 2.0 * (frequency % 2)
    return both.astype(np.float32).astype(ml_dtypes.bfloat16)


def lag_table(window_count):
    frequency = np.arange(BINS)
    offset = np.arange(LAGS) - LAGS // 2 + SEG
    angles = (frequency[None, :] * offset[:, None] % SEG) * (2.0 * math.pi / SEG)
    scale = 1.0 / math.sqrt(BINS * window_count)
    both = np.stack([np.cos(angles) * scale, -np.sin(angles) * scale])
    return both.astype(np.float32).astype(ml_dtypes.bfloat16)


def gather_kernel(members, raw_ref, taps_ref, order_ref, out_ref, halo, low, halo_sems, own_sem, send_sems, recv_sems):
    me = lax.axis_index("sta")
    stations, local_time = raw_ref.shape
    line = members // QUAD
    rank, lead = me // QUAD, me % QUAD
    far = [lax.rem(rank + k, line) * QUAD + lead for k in range(1, line)]
    across = rank * QUAD + lax.rem(lead + 2, QUAD)
    twin = me + 1 - 2 * lax.rem(me, 2)
    after, before = lax.rem(me + 1, members), lax.rem(me + members - 1, members)

    barrier = pltpu.get_barrier_semaphore()
    greeted = far + [across, twin, after, before]
    for peer in greeted:
        pl.semaphore_signal(barrier, inc=1, device_id={"sta": peer}, device_id_type=MESH)
    pl.semaphore_wait(barrier, len(greeted))

    halo_copy = pltpu.make_async_remote_copy(
        src_ref=raw_ref.at[:, local_time - TAPS :],
        dst_ref=halo,
        send_sem=halo_sems.at[0],
        recv_sem=halo_sems.at[1],
        device_id={"sta": after},
        device_id_type=MESH,
    )

    @pl.when(me < members - 1)
    def _():
        halo_copy.start()

    banded = jnp.broadcast_to(taps_ref[...], (LANE, SPAN))
    banded = pltpu.roll(banded, 0, 1, stride=DEC, stride_axis=0).astype(jnp.bfloat16)
    picks = (lax.broadcasted_iota(jnp.int32, (stations, stations), 1) == order_ref[...]).astype(
        jnp.float32
    ).astype(jnp.bfloat16)
    dims = (((1,), (1,)), ((), ()))

    def filtered(piece, samples):
        summed = lax.dot_general(samples, banded, dims, preferred_element_type=jnp.float32)
        ordered = jnp.dot(picks, summed.astype(jnp.bfloat16), preferred_element_type=jnp.float32)
        low[piece] = ordered.astype(jnp.bfloat16)

    for piece in range(1, low.shape[0]):
        first = piece * LANE * DEC - TAPS
        filtered(piece, raw_ref[:, first : first + SPAN])

    @pl.when(me > 0)
    def _():
        halo_copy.wait_recv()

    @pl.when(me == 0)
    def _():
        halo[...] = jnp.zeros_like(halo)

    filtered(0, jnp.concatenate([halo[...], raw_ref[:, : LANE * DEC]], axis=1))

    sent = []

    def send(source, slot, peer):
        n = len(sent)
        copy = pltpu.make_async_remote_copy(
            src_ref=source,
            dst_ref=out_ref.at[slot],
            send_sem=send_sems.at[n],
            recv_sem=recv_sems.at[slot],
            device_id={"sta": peer},
            device_id_type=MESH,
        )
        copy.start()
        sent.append(copy)

    def arrived(slot):
        pltpu.make_async_remote_copy(
            src_ref=low,
            dst_ref=out_ref.at[slot],
            send_sem=send_sems.at[0],
            recv_sem=recv_sems.at[slot],
            device_id={"sta": twin},
            device_id_type=MESH,
        ).wait_recv()

    order = sorted(range(line - 1), key=lambda k: min(k + 1, line - 1 - k))
    for k in order:
        send(low, me, far[k])
    send(low, me, across)
    send(low, me, twin)
    own = pltpu.make_async_copy(low, out_ref.at[me], own_sem)
    own.start()
    shift = across - me
    arrived(me + shift)
    send(out_ref.at[me + shift], me + shift, twin)
    for k in order:
        arrived(far[k])
        send(out_ref.at[far[k]], far[k], across)
        send(out_ref.at[far[k]], far[k], twin)
    for k in order:
        arrived(far[k] + shift)
        send(out_ref.at[far[k] + shift], far[k] + shift, twin)
    turn = twin - me
    for slot in [me] + [far[k] for k in order]:
        arrived(slot + turn)
        arrived(slot + shift + turn)
    own.wait()
    for copy in sent:
        copy.wait_send()

    @pl.when(me < members - 1)
    def _():
        halo_copy.wait_send()


def correlate_kernel(
    starts_ref,
    groups_ref,
    low_ref,
    dft_ref,
    lag_ref,
    out_ref,
    rows,
    ahead,
    back,
    even_theirs,
    odd_theirs,
    even_own,
    odd_own,
    real_theirs,
    imag_theirs,
    white_own,
    left,
    right,
    cross_real,
    cross_imag,
    sems,
):
    tile = pl.program_id(0)
    planes = low_ref.shape[0]
    window_count = starts_ref.shape[0]
    lane = lax.broadcasted_iota(jnp.int32, (1, LANE), 1)

    @pl.when(tile == 0)
    def _():
        copies = []
        for g in range(GROUPS):
            first = pl.multiple_of(groups_ref[g] * SB, SB)
            copy = pltpu.make_async_copy(
                low_ref.at[:, pl.ds(first, SB), :], rows.at[:, pl.ds(g * SB, SB), :], sems.at[g]
            )
            copy.start()
            copies.append(copy)
        for copy in copies:
            copy.wait()
        mirror = (
            lax.broadcasted_iota(jnp.int32, (LANE, LANE), 0) + lax.broadcasted_iota(jnp.int32, (LANE, LANE), 1)
            == LANE - 1
        ).astype(jnp.float32).astype(jnp.bfloat16)
        back[0] = jnp.zeros((ROWS, LANE), jnp.float32)

        def one_plane(n, carry):
            samples = rows[n]
            ahead[n] = samples.astype(jnp.float32)
            back[planes - n] = jnp.dot(samples, mirror, preferred_element_type=jnp.float32)
            return carry

        lax.fori_loop(0, planes, one_plane, 0, unroll=4)

        def one_window(w, carry):
            def shifted(ref, first):
                plane = first // LANE
                keep = LANE - first % LANE
                shift = keep % LANE
                now = pltpu.roll(ref[plane], shift, 1)
                pieces = []
                for piece in range(FOLD // LANE):
                    later = pltpu.roll(ref[plane + piece + 1], shift, 1)
                    pieces.append(jnp.where(lane < keep, now, later))
                    now = later
                return pieces, now

            start = starts_ref[w]
            forward, middle = shifted(ahead, start)
            backward, _ = shifted(back, planes * LANE - 1 - FOLD * 2 + LANE - start)
            theirs = pl.ds(pl.multiple_of(w * THEIRS, SB), THEIRS)
            own = pl.ds(pl.multiple_of(w * SB, SB), SB)
            for piece, (a, b) in enumerate(zip(forward, backward)):
                at = slice(piece * LANE, (piece + 1) * LANE)
                even, odd = a + b, a - b
                if piece == 0:
                    even = jnp.where(lane == 0, middle, even)
                even, odd = even.astype(jnp.bfloat16), odd.astype(jnp.bfloat16)
                even_theirs[theirs, at] = even[:THEIRS]
                odd_theirs[theirs, at] = odd[:THEIRS]
                even_own[own, at] = even[THEIRS:]
                odd_own[own, at] = odd[THEIRS:]
            return carry

        lax.fori_loop(0, window_count, one_window, 0)

    def dot_nt(a, b):
        return lax.dot_general(a, b, NT, preferred_element_type=jnp.float32)

    half = LANE // 2
    pairs = window_count // 2
    real_theirs[...] = dot_nt(dft_ref[0], even_theirs[...])
    imag_theirs[...] = dot_nt(dft_ref[1], odd_theirs[...])

    def one_band(n, carry):
        at = pl.ds(pl.multiple_of(n * BAND, BAND), BAND)
        for pair in range(pairs):
            lanes = slice(pair * LANE, (pair + 1) * LANE)
            real, imag = real_theirs[at, lanes], imag_theirs[at, lanes]
            level = jnp.sum(real * real + imag * imag, axis=0, keepdims=True)
            scale = lax.rsqrt(level * (1.0 / (2 * BAND)) + 1e-06)
            real, imag = real * scale, imag * scale
            real_turned, imag_turned = pltpu.roll(real, half, 1), pltpu.roll(imag, half, 1)
            first = lane < half
            blocks = (
                (jnp.where(first, real, -imag_turned), jnp.where(first, real_turned, -imag)),
                (jnp.where(first, imag, real_turned), jnp.where(first, imag_turned, real)),
            )
            for c, block in enumerate(blocks):
                both = [x.reshape(BAND // PACK, 1, PACK, LANE) for x in block]
                both = jnp.concatenate(both, axis=1).reshape(BAND // PACK, 2 * PACK, LANE)
                right[
                    pl.ds(n * (BAND // PACK), BAND // PACK),
                    pl.ds((c * pairs + pair) * 2 * PACK, 2 * PACK),
                    :,
                ] = both.astype(jnp.bfloat16)
        return carry

    lax.fori_loop(0, FT // BAND, one_band, 0)

    real, imag = dot_nt(even_own[...], dft_ref[0]), dot_nt(odd_own[...], dft_ref[1])
    power = (real * real + imag * imag).astype(jnp.bfloat16)
    same = (
        lax.broadcasted_iota(jnp.int32, (FT, FT), 0) // BAND == lax.broadcasted_iota(jnp.int32, (FT, FT), 1) // BAND
    ).astype(jnp.float32).astype(jnp.bfloat16)
    level = jnp.dot(power, same, preferred_element_type=jnp.float32)
    scale = lax.rsqrt(level * (1.0 / (2 * BAND)) + 1e-06)
    white_own[0] = real * scale
    white_own[1] = imag * scale

    slots = LANE // PACK
    for part in range(FT // LANE):
        for c in range(2):
            moved = [[], []]
            for pair in range(pairs):
                x = [
                    white_own[c, (2 * pair + k) * SB : (2 * pair + k + 1) * SB, part * LANE : (part + 1) * LANE]
                    for k in range(2)
                ]
                low_slot = lane // PACK % 2 == 0
                y = (
                    jnp.where(low_slot, x[0], pltpu.roll(x[1], PACK, 1)),
                    jnp.where(low_slot, pltpu.roll(x[0], LANE - PACK, 1), x[1]),
                )
                for k in range(2):
                    moved[k].append(pltpu.roll(y[k], 2 * PACK * pair, 1) if pair else y[k])
            for slot in range(slots):
                turn, k = slot // 2, slot % 2
                joined = moved[k][0]
                for pair in range(1, pairs):
                    joined = jnp.where(lane // (2 * PACK) == (turn + pair) % (slots // 2), moved[k][pair], joined)
                if turn:
                    joined = pltpu.roll(joined, LANE - 2 * PACK * turn, 1)
                left[part * slots + slot, c] = joined.astype(jnp.bfloat16)

    own_bin = lax.broadcasted_iota(jnp.int32, (PACK * SB, LANE), 0) // SB
    mask = (own_bin == lax.broadcasted_iota(jnp.int32, (PACK * SB, LANE), 1) % PACK).astype(jnp.float32).astype(
        jnp.bfloat16
    )

    def one_group(n, carry):
        masked = jnp.concatenate([jnp.concatenate([left[n, c]] * PACK, axis=0) * mask for c in range(2)], axis=1)
        product = jnp.dot(masked, right[n], preferred_element_type=jnp.float32)
        product = product.reshape(PACK, 2, SB // 2, LANE)
        first = lane < half
        a, b = product[:, 0].reshape(PACK * SB // 2, LANE), product[:, 1].reshape(PACK * SB // 2, LANE)
        a_turned, b_turned = pltpu.roll(a, half, 1), pltpu.roll(b, half, 1)
        at = pl.ds(pl.multiple_of((tile * (FT // PACK) + n) * PACK * SB // 2, PACK * SB // 2), PACK * SB // 2)
        cross_real[at, :] = jnp.where(first, a, b_turned)
        cross_imag[at, :] = jnp.where(first, a_turned, b)
        return carry

    lax.fori_loop(0, FT // PACK, one_group, 0, unroll=4)

    @pl.when(tile == pl.num_programs(0) - 1)
    def _():
        def two_stations(n, carry):
            summed = None
            for k, cross in enumerate((cross_real, cross_imag)):
                columns = jnp.concatenate(
                    [cross[pl.ds(2 * n + m, BINS, stride=SB // 2), :].astype(jnp.bfloat16) for m in range(2)], axis=1
                )
                term = jnp.dot(lag_ref[k], columns, preferred_element_type=jnp.float32)
                summed = term if summed is None else summed + term
            turned = summed.T
            for m in range(2):
                for h in range(2):
                    i = h * (SB // 2) + 2 * n + m
                    for r in range(ROUNDS):
                        first = ((m * 2 + h) * ROUNDS + r) * SB
                        out_ref[r, pl.ds(pl.multiple_of(i * SB, SB), SB), :] = turned[first : first + SB]
            return carry

        lax.fori_loop(0, SB // 4, two_stations, 0)


def correlate(window_starts, groups, low, dft, lag):
    window_count = window_starts.shape[0]
    planes = low.shape[0]
    grid_spec = pltpu.PrefetchScalarGridSpec(
        num_scalar_prefetch=2,
        grid=(TILES,),
        in_specs=[
            pl.BlockSpec(memory_space=pl.ANY),
            pl.BlockSpec((2, FT, FOLD), lambda n, *_: (0, n, 0)),
            pl.BlockSpec((2, LAGS, BINS), lambda n, *_: (0, 0, 0)),
        ],
        out_specs=pl.BlockSpec((ROUNDS, SB * SB, LAGS), lambda n, *_: (0, 0, 0)),
        scratch_shapes=[
            pltpu.VMEM((planes, ROWS, LANE), jnp.bfloat16),
            pltpu.VMEM((planes, ROWS, LANE), jnp.float32),
            pltpu.VMEM((planes + 1, ROWS, LANE), jnp.float32),
            pltpu.VMEM((window_count * THEIRS, FOLD), jnp.bfloat16),
            pltpu.VMEM((window_count * THEIRS, FOLD), jnp.bfloat16),
            pltpu.VMEM((window_count * SB, FOLD), jnp.bfloat16),
            pltpu.VMEM((window_count * SB, FOLD), jnp.bfloat16),
            pltpu.VMEM((FT, window_count * THEIRS), jnp.float32),
            pltpu.VMEM((FT, window_count * THEIRS), jnp.float32),
            pltpu.VMEM((2, window_count * SB, FT), jnp.float32),
            pltpu.VMEM((FT // PACK, 2, SB, LANE), jnp.bfloat16),
            pltpu.VMEM((FT // PACK, 2 * LANE, LANE), jnp.bfloat16),
            pltpu.VMEM((BINS * SB // 2, LANE), jnp.float32),
            pltpu.VMEM((BINS * SB // 2, LANE), jnp.float32),
            pltpu.SemaphoreType.DMA((GROUPS,)),
        ],
    )
    return pl.pallas_call(
        correlate_kernel,
        grid_spec=grid_spec,
        out_shape=jax.ShapeDtypeStruct((ROUNDS, SB * SB, LAGS), jnp.float32),
        compiler_params=pltpu.CompilerParams(vmem_limit_bytes=56 * 2**20),
    )(window_starts, groups, low, dft, lag)


def body(raw_traces, filter_taps, station_order, window_starts, pairing):
    members = lax.axis_size("sta")
    me = lax.axis_index("sta")
    stations, local_time = raw_traces.shape
    window_count = window_starts.shape[0]
    pieces = local_time // (LANE * DEC)
    taps = jnp.pad(filter_taps.astype(jnp.float32)[::-1], (DEC, SPAN - TAPS - DEC)).reshape(1, SPAN)
    in_vmem = pl.BlockSpec(memory_space=pltpu.VMEM)
    low = pl.pallas_call(
        functools.partial(gather_kernel, members),
        out_shape=jax.ShapeDtypeStruct((members, pieces, stations, LANE), jnp.bfloat16),
        in_specs=[in_vmem] * 3,
        out_specs=pl.BlockSpec(memory_space=pl.ANY),
        scratch_shapes=[
            pltpu.VMEM((stations, TAPS), jnp.bfloat16),
            pltpu.VMEM((pieces, stations, LANE), jnp.bfloat16),
            pltpu.SemaphoreType.DMA((2,)),
            pltpu.SemaphoreType.DMA,
            pltpu.SemaphoreType.DMA((members,)),
            pltpu.SemaphoreType.DMA((members,)),
        ],
        compiler_params=pltpu.CompilerParams(
            collective_id=0, has_side_effects=True, vmem_limit_bytes=40 * 2**20
        ),
    )(raw_traces, taps, station_order.reshape(stations, 1))
    low = low.reshape(members * pieces, stations, LANE)
    groups = jnp.concatenate([lax.dynamic_slice_in_dim(pairing, me, 1, 1)[:, 0], me[None].astype(jnp.int32)])
    correlated = correlate(
        window_starts,
        groups,
        low,
        jnp.asarray(dft_table()),
        jnp.asarray(lag_table(window_count)),
    )
    return correlated.reshape(ROUNDS, SB, SB, LAGS)


def solution(mesh):
    return jax.shard_map(
        body,
        mesh=mesh,
        in_specs=(P("parts", "sta"), P(), P("parts"), P("parts"), P()),
        out_specs=P(None, ("parts", "sta"), None, None),
        check_vma=False,
    )
```

```python
import functools
import math

import jax
import jax.numpy as jnp
import ml_dtypes
import numpy as np
from jax import lax
from jax.experimental import pallas as pl
from jax.experimental.pallas import tpu as pltpu
from jax.sharding import PartitionSpec as P

SB = 16
DEC = 4
TAPS = 256
SEG = 2048
BAND = 64
LAGS = 256
ROUNDS = 4
BINS = 1024
LANE = 128
SPAN = LANE * DEC + TAPS
GROUPS = ROUNDS + 1
ROWS = GROUPS * SB
THEIRS = ROUNDS * SB
FOLD = SEG // 2
FT = 256
TILES = BINS // FT
PACK = 8
NT = (((1,), (1,)), ((), ()))
QUAD = 4
MESH = pl.DeviceIdType.MESH


def dft_table():
    sample = np.arange(FOLD)
    frequency = np.arange(BINS)
    angles = (sample[None, :] * frequency[:, None] % SEG) * (2.0 * math.pi / SEG)
    taper = (0.5 - 0.5 * np.cos(sample * (2.0 * math.pi / SEG)))[None, :]
    both = np.stack([np.cos(angles) * taper, -np.sin(angles) * taper])
    both[0, :, 0] = 1.0 - 2.0 * (frequency % 2)
    return both.astype(np.float32).astype(ml_dtypes.bfloat16)


def lag_table(window_count):
    frequency = np.arange(BINS)
    offset = np.arange(LAGS) - LAGS // 2 + SEG
    angles = (frequency[None, :] * offset[:, None] % SEG) * (2.0 * math.pi / SEG)
    scale = 1.0 / math.sqrt(BINS * window_count)
    both = np.stack([np.cos(angles) * scale, -np.sin(angles) * scale])
    return both.astype(np.float32).astype(ml_dtypes.bfloat16)


def gather_kernel(members, raw_ref, taps_ref, order_ref, out_ref, halo, low, halo_sems, own_sem, send_sems, recv_sems):
    me = lax.axis_index("sta")
    stations, local_time = raw_ref.shape
    line = members // QUAD
    rank, lead = me // QUAD, me % QUAD
    far = [lax.rem(rank + k, line) * QUAD + lead for k in range(1, line)]
    across = rank * QUAD + lax.rem(lead + 2, QUAD)
    twin = me + 1 - 2 * lax.rem(me, 2)
    after, before = lax.rem(me + 1, members), lax.rem(me + members - 1, members)

    barrier = pltpu.get_barrier_semaphore()
    greeted = far + [across, twin, after, before]
    for peer in greeted:
        pl.semaphore_signal(barrier, inc=1, device_id={"sta": peer}, device_id_type=MESH)
    pl.semaphore_wait(barrier, len(greeted))

    halo_copy = pltpu.make_async_remote_copy(
        src_ref=raw_ref.at[:, local_time - TAPS :],
        dst_ref=halo,
        send_sem=halo_sems.at[0],
        recv_sem=halo_sems.at[1],
        device_id={"sta": after},
        device_id_type=MESH,
    )

    @pl.when(me < members - 1)
    def _():
        halo_copy.start()

    banded = jnp.broadcast_to(taps_ref[...], (LANE, SPAN))
    banded = pltpu.roll(banded, 0, 1, stride=DEC, stride_axis=0).astype(jnp.bfloat16)
    picks = (lax.broadcasted_iota(jnp.int32, (stations, stations), 1) == order_ref[...]).astype(
        jnp.float32
    ).astype(jnp.bfloat16)
    dims = (((1,), (1,)), ((), ()))

    def filtered(piece, samples):
        summed = lax.dot_general(samples, banded, dims, preferred_element_type=jnp.float32)
        ordered = jnp.dot(picks, summed.astype(jnp.bfloat16), preferred_element_type=jnp.float32)
        low[piece] = ordered.astype(jnp.bfloat16)

    for piece in range(1, low.shape[0]):
        first = piece * LANE * DEC - TAPS
        filtered(piece, raw_ref[:, first : first + SPAN])

    @pl.when(me > 0)
    def _():
        halo_copy.wait_recv()

    @pl.when(me == 0)
    def _():
        halo[...] = jnp.zeros_like(halo)

    filtered(0, jnp.concatenate([halo[...], raw_ref[:, : LANE * DEC]], axis=1))

    sent = []

    def send(source, slot, peer):
        n = len(sent)
        copy = pltpu.make_async_remote_copy(
            src_ref=source,
            dst_ref=out_ref.at[slot],
            send_sem=send_sems.at[n],
            recv_sem=recv_sems.at[slot],
            device_id={"sta": peer},
            device_id_type=MESH,
        )
        copy.start()
        sent.append(copy)

    def arrived(slot):
        pltpu.make_async_remote_copy(
            src_ref=low,
            dst_ref=out_ref.at[slot],
            send_sem=send_sems.at[0],
            recv_sem=recv_sems.at[slot],
            device_id={"sta": twin},
            device_id_type=MESH,
        ).wait_recv()

    order = sorted(range(line - 1), key=lambda k: min(k + 1, line - 1 - k))
    for k in order:
        send(low, me, far[k])
    send(low, me, across)
    send(low, me, twin)
    own = pltpu.make_async_copy(low, out_ref.at[me], own_sem)
    own.start()
    shift = across - me
    arrived(me + shift)
    send(out_ref.at[me + shift], me + shift, twin)
    for k in order:
        arrived(far[k])
        send(out_ref.at[far[k]], far[k], across)
        send(out_ref.at[far[k]], far[k], twin)
    for k in order:
        arrived(far[k] + shift)
        send(out_ref.at[far[k] + shift], far[k] + shift, twin)
    turn = twin - me
    for slot in [me] + [far[k] for k in order]:
        arrived(slot + turn)
        arrived(slot + shift + turn)
    own.wait()
    for copy in sent:
        copy.wait_send()

    @pl.when(me < members - 1)
    def _():
        halo_copy.wait_send()


def correlate_kernel(
    starts_ref,
    groups_ref,
    low_ref,
    dft_ref,
    lag_ref,
    out_ref,
    rows,
    ahead,
    back,
    even_theirs,
    odd_theirs,
    even_own,
    odd_own,
    white_own,
    left,
    right,
    cross_real,
    cross_imag,
    sems,
):
    tile = pl.program_id(0)
    planes = low_ref.shape[0]
    window_count = starts_ref.shape[0]
    lane = lax.broadcasted_iota(jnp.int32, (1, LANE), 1)

    @pl.when(tile == 0)
    def _():
        copies = []
        for g in range(GROUPS):
            first = pl.multiple_of(groups_ref[g] * SB, SB)
            copy = pltpu.make_async_copy(
                low_ref.at[:, pl.ds(first, SB), :], rows.at[:, pl.ds(g * SB, SB), :], sems.at[g]
            )
            copy.start()
            copies.append(copy)
        for copy in copies:
            copy.wait()
        mirror = (
            lax.broadcasted_iota(jnp.int32, (LANE, LANE), 0) + lax.broadcasted_iota(jnp.int32, (LANE, LANE), 1)
            == LANE - 1
        ).astype(jnp.float32).astype(jnp.bfloat16)
        back[0] = jnp.zeros((ROWS, LANE), jnp.float32)

        def one_plane(n, carry):
            samples = rows[n]
            ahead[n] = samples.astype(jnp.float32)
            back[planes - n] = jnp.dot(samples, mirror, preferred_element_type=jnp.float32)
            return carry

        lax.fori_loop(0, planes, one_plane, 0, unroll=8)

        def one_window(w, carry):
            def shifted(ref, first):
                plane = first // LANE
                keep = LANE - first % LANE
                shift = keep % LANE
                now = pltpu.roll(ref[plane], shift, 1)
                pieces = []
                for piece in range(FOLD // LANE):
                    later = pltpu.roll(ref[plane + piece + 1], shift, 1)
                    pieces.append(jnp.where(lane < keep, now, later))
                    now = later
                return pieces, now

            start = starts_ref[w]
            forward, middle = shifted(ahead, start)
            backward, _ = shifted(back, planes * LANE - 1 - FOLD * 2 + LANE - start)
            theirs = pl.ds(pl.multiple_of(w * THEIRS, SB), THEIRS)
            own = pl.ds(pl.multiple_of(w * SB, SB), SB)
            for piece, (a, b) in enumerate(zip(forward, backward)):
                at = slice(piece * LANE, (piece + 1) * LANE)
                even, odd = a + b, a - b
                if piece == 0:
                    even = jnp.where(lane == 0, middle, even)
                even, odd = even.astype(jnp.bfloat16), odd.astype(jnp.bfloat16)
                even_theirs[theirs, at] = even[:THEIRS]
                odd_theirs[theirs, at] = odd[:THEIRS]
                even_own[own, at] = even[THEIRS:]
                odd_own[own, at] = odd[THEIRS:]
            return carry

        lax.fori_loop(0, window_count, one_window, 0, unroll=2)

    def dot_nt(a, b):
        return lax.dot_general(a, b, NT, preferred_element_type=jnp.float32)

    half = LANE // 2
    pairs = window_count // 2
    wide = 2 * LANE
    first = lane < half
    for tile_pair in range(window_count * THEIRS // wide):
        at = slice(tile_pair * wide, (tile_pair + 1) * wide)
        reals = dot_nt(dft_ref[0], even_theirs[at, :])
        imags = dot_nt(dft_ref[1], odd_theirs[at, :])
        for n in range(FT // BAND):
            for inner in range(wide // LANE):
                pair = tile_pair * (wide // LANE) + inner
                real, imag = (
                    x[n * BAND : (n + 1) * BAND, inner * LANE : (inner + 1) * LANE] for x in (reals, imags)
                )
                level = jnp.sum(real * real + imag * imag, axis=0, keepdims=True)
                scale = lax.rsqrt(level * (1.0 / (2 * BAND)) + 1e-06)
                real, imag = real * scale, imag * scale
                real_turned, imag_turned = pltpu.roll(real, half, 1), pltpu.roll(imag, half, 1)
                blocks = (
                    (jnp.where(first, real, -imag_turned), jnp.where(first, real_turned, -imag)),
                    (jnp.where(first, imag, real_turned), jnp.where(first, imag_turned, real)),
                )
                for c, block in enumerate(blocks):
                    both = [x.reshape(BAND // PACK, 1, PACK, LANE) for x in block]
                    both = jnp.concatenate(both, axis=1).reshape(BAND // PACK, 2 * PACK, LANE)
                    row = (c * pairs + pair) * 2 * PACK
                    right[n * (BAND // PACK) : (n + 1) * (BAND // PACK), row : row + 2 * PACK, :] = both.astype(
                        jnp.bfloat16
                    )

    real, imag = dot_nt(even_own[...], dft_ref[0]), dot_nt(odd_own[...], dft_ref[1])
    power = (real * real + imag * imag).astype(jnp.bfloat16)
    same = (
        lax.broadcasted_iota(jnp.int32, (FT, FT), 0) // BAND == lax.broadcasted_iota(jnp.int32, (FT, FT), 1) // BAND
    ).astype(jnp.float32).astype(jnp.bfloat16)
    level = jnp.dot(power, same, preferred_element_type=jnp.float32)
    scale = lax.rsqrt(level * (1.0 / (2 * BAND)) + 1e-06)
    white_own[0] = real * scale
    white_own[1] = imag * scale

    slots = LANE // PACK
    for part in range(FT // LANE):
        for c in range(2):
            moved = [[], []]
            for pair in range(pairs):
                x = [
                    white_own[c, (2 * pair + k) * SB : (2 * pair + k + 1) * SB, part * LANE : (part + 1) * LANE]
                    for k in range(2)
                ]
                low_slot = lane // PACK % 2 == 0
                y = (
                    jnp.where(low_slot, x[0], pltpu.roll(x[1], PACK, 1)),
                    jnp.where(low_slot, pltpu.roll(x[0], LANE - PACK, 1), x[1]),
                )
                for k in range(2):
                    moved[k].append(pltpu.roll(y[k], 2 * PACK * pair, 1) if pair else y[k])
            for slot in range(slots):
                turn, k = slot // 2, slot % 2
                joined = moved[k][0]
                for pair in range(1, pairs):
                    joined = jnp.where(lane // (2 * PACK) == (turn + pair) % (slots // 2), moved[k][pair], joined)
                if turn:
                    joined = pltpu.roll(joined, LANE - 2 * PACK * turn, 1)
                left[part * slots + slot, c] = joined.astype(jnp.bfloat16)

    own_bin = lax.broadcasted_iota(jnp.int32, (PACK * SB, LANE), 0) // SB
    mask = (own_bin == lax.broadcasted_iota(jnp.int32, (PACK * SB, LANE), 1) % PACK).astype(jnp.float32).astype(
        jnp.bfloat16
    )

    def one_group(n, carry):
        masked = jnp.concatenate([jnp.concatenate([left[n, c]] * PACK, axis=0) * mask for c in range(2)], axis=1)
        product = jnp.dot(masked, right[n], preferred_element_type=jnp.float32)
        product = product.reshape(PACK, 2, SB // 2, LANE)
        first = lane < half
        a, b = product[:, 0].reshape(PACK * SB // 2, LANE), product[:, 1].reshape(PACK * SB // 2, LANE)
        a_turned, b_turned = pltpu.roll(a, half, 1), pltpu.roll(b, half, 1)
        at = pl.ds(pl.multiple_of((tile * (FT // PACK) + n) * PACK * SB // 2, PACK * SB // 2), PACK * SB // 2)
        cross_real[at, :] = jnp.where(first, a, b_turned)
        cross_imag[at, :] = jnp.where(first, a_turned, b)
        return carry

    lax.fori_loop(0, FT // PACK, one_group, 0, unroll=16)

    @pl.when(tile == pl.num_programs(0) - 1)
    def _():
        def two_stations(n, carry):
            summed = None
            for k, cross in enumerate((cross_real, cross_imag)):
                columns = jnp.concatenate(
                    [cross[pl.ds(2 * n + m, BINS, stride=SB // 2), :].astype(jnp.bfloat16) for m in range(2)], axis=1
                )
                term = jnp.dot(lag_ref[k], columns, preferred_element_type=jnp.float32)
                summed = term if summed is None else summed + term
            turned = summed.T
            for m in range(2):
                for h in range(2):
                    i = h * (SB // 2) + 2 * n + m
                    for r in range(ROUNDS):
                        first = ((m * 2 + h) * ROUNDS + r) * SB
                        out_ref[r, pl.ds(pl.multiple_of(i * SB, SB), SB), :] = turned[first : first + SB]
            return carry

        lax.fori_loop(0, SB // 4, two_stations, 0, unroll=True)


def correlate(window_starts, groups, low, dft, lag):
    window_count = window_starts.shape[0]
    planes = low.shape[0]
    grid_spec = pltpu.PrefetchScalarGridSpec(
        num_scalar_prefetch=2,
        grid=(TILES,),
        in_specs=[
            pl.BlockSpec(memory_space=pl.ANY),
            pl.BlockSpec((2, FT, FOLD), lambda n, *_: (0, n, 0)),
            pl.BlockSpec((2, LAGS, BINS), lambda n, *_: (0, 0, 0)),
        ],
        out_specs=pl.BlockSpec((ROUNDS, SB * SB, LAGS), lambda n, *_: (0, 0, 0)),
        scratch_shapes=[
            pltpu.VMEM((planes, ROWS, LANE), jnp.bfloat16),
            pltpu.VMEM((planes, ROWS, LANE), jnp.float32),
            pltpu.VMEM((planes + 1, ROWS, LANE), jnp.float32),
            pltpu.VMEM((window_count * THEIRS, FOLD), jnp.bfloat16),
            pltpu.VMEM((window_count * THEIRS, FOLD), jnp.bfloat16),
            pltpu.VMEM((window_count * SB, FOLD), jnp.bfloat16),
            pltpu.VMEM((window_count * SB, FOLD), jnp.bfloat16),
            pltpu.VMEM((2, window_count * SB, FT), jnp.float32),
            pltpu.VMEM((FT // PACK, 2, SB, LANE), jnp.bfloat16),
            pltpu.VMEM((FT // PACK, 2 * LANE, LANE), jnp.bfloat16),
            pltpu.VMEM((BINS * SB // 2, LANE), jnp.float32),
            pltpu.VMEM((BINS * SB // 2, LANE), jnp.float32),
            pltpu.SemaphoreType.DMA((GROUPS,)),
        ],
    )
    return pl.pallas_call(
        correlate_kernel,
        grid_spec=grid_spec,
        out_shape=jax.ShapeDtypeStruct((ROUNDS, SB * SB, LAGS), jnp.float32),
        compiler_params=pltpu.CompilerParams(vmem_limit_bytes=56 * 2**20),
    )(window_starts, groups, low, dft, lag)


def body(raw_traces, filter_taps, station_order, window_starts, pairing):
    members = lax.axis_size("sta")
    me = lax.axis_index("sta")
    stations, local_time = raw_traces.shape
    window_count = window_starts.shape[0]
    pieces = local_time // (LANE * DEC)
    taps = jnp.pad(filter_taps.astype(jnp.float32)[::-1], (DEC, SPAN - TAPS - DEC)).reshape(1, SPAN)
    in_vmem = pl.BlockSpec(memory_space=pltpu.VMEM)
    low = pl.pallas_call(
        functools.partial(gather_kernel, members),
        out_shape=jax.ShapeDtypeStruct((members, pieces, stations, LANE), jnp.bfloat16),
        in_specs=[in_vmem] * 3,
        out_specs=pl.BlockSpec(memory_space=pl.ANY),
        scratch_shapes=[
            pltpu.VMEM((stations, TAPS), jnp.bfloat16),
            pltpu.VMEM((pieces, stations, LANE), jnp.bfloat16),
            pltpu.SemaphoreType.DMA((2,)),
            pltpu.SemaphoreType.DMA,
            pltpu.SemaphoreType.DMA((members,)),
            pltpu.SemaphoreType.DMA((members,)),
        ],
        compiler_params=pltpu.CompilerParams(
            collective_id=0, has_side_effects=True, vmem_limit_bytes=40 * 2**20
        ),
    )(raw_traces, taps, station_order.reshape(stations, 1))
    low = low.reshape(members * pieces, stations, LANE)
    groups = jnp.concatenate([lax.dynamic_slice_in_dim(pairing, me, 1, 1)[:, 0], me[None].astype(jnp.int32)])
    correlated = correlate(
        window_starts,
        groups,
        low,
        jnp.asarray(dft_table()),
        jnp.asarray(lag_table(window_count)),
    )
    return correlated.reshape(ROUNDS, SB, SB, LAGS)


def solution(mesh):
    return jax.shard_map(
        body,
        mesh=mesh,
        in_specs=(P("parts", "sta"), P(), P("parts"), P("parts"), P()),
        out_specs=P(None, ("parts", "sta"), None, None),
        check_vma=False,
    )
```

```python
import functools
import math

import jax
import jax.numpy as jnp
import ml_dtypes
import numpy as np
from jax import lax
from jax.experimental import pallas as pl
from jax.experimental.pallas import tpu as pltpu
from jax.sharding import PartitionSpec as P

SB = 16
DEC = 4
TAPS = 256
SEG = 2048
BAND = 64
LAGS = 256
ROUNDS = 4
BINS = 1024
LANE = 128
SPAN = LANE * DEC + TAPS
GROUPS = ROUNDS + 1
ROWS = GROUPS * SB
THEIRS = ROUNDS * SB
FOLD = SEG // 2
FT = 256
TILES = BINS // FT
PACK = 8
NT = (((1,), (1,)), ((), ()))
QUAD = 4
MESH = pl.DeviceIdType.MESH


def dft_table():
    sample = np.arange(FOLD)
    frequency = np.arange(BINS)
    angles = (sample[None, :] * frequency[:, None] % SEG) * (2.0 * math.pi / SEG)
    taper = (0.5 - 0.5 * np.cos(sample * (2.0 * math.pi / SEG)))[None, :]
    both = np.stack([np.cos(angles) * taper, -np.sin(angles) * taper])
    both[0, :, 0] = 1.0 - 2.0 * (frequency % 2)
    return both.astype(np.float32).astype(ml_dtypes.bfloat16)


def lag_table(window_count):
    frequency = np.arange(BINS)
    offset = np.arange(LAGS) - LAGS // 2 + SEG
    angles = (frequency[None, :] * offset[:, None] % SEG) * (2.0 * math.pi / SEG)
    scale = 1.0 / math.sqrt(BINS * window_count)
    both = np.stack([np.cos(angles) * scale, -np.sin(angles) * scale])
    return both.astype(np.float32).astype(ml_dtypes.bfloat16)


def gather_kernel(
    members,
    raw_ref,
    taps_ref,
    order_ref,
    pairing_ref,
    out_ref,
    raw,
    halo,
    column,
    private,
    picked,
    raw_sem,
    halo_sems,
    line_send,
    line_recv,
    pick_send,
    pick_recv,
):
    me = lax.axis_index("sta")
    stations, local_time = raw_ref.shape
    line, pieces = column.shape[:2]
    rank, lead = me // QUAD, me % QUAD
    turn = 1 - 2 * lax.rem(me, 2)
    twin = me + turn
    across = rank * QUAD + lax.rem(lead + 2, QUAD)
    others = (across, across + turn, twin)
    after, before = lax.rem(me + 1, members), lax.rem(me + members - 1, members)

    def nearest(n):
        chosen = None
        for r in range(line):
            order = sorted((x for x in range(line) if x != r), key=lambda x: abs(x - r))
            chosen = order[n] if chosen is None else jnp.where(rank == r, order[n], chosen)
        return chosen

    line_order = [nearest(n) for n in range(line - 1)]

    raw_copy = pltpu.make_async_copy(raw_ref, raw, raw_sem)
    raw_copy.start()

    barrier = pltpu.get_barrier_semaphore()
    greeted = [r * QUAD + lead for r in line_order] + list(others) + [after, before]
    for peer in greeted:
        pl.semaphore_signal(barrier, inc=1, device_id={"sta": peer}, device_id_type=MESH)

    mirror = (
        lax.broadcasted_iota(jnp.int32, (TAPS, TAPS), 0) + lax.broadcasted_iota(jnp.int32, (TAPS, TAPS), 1) == TAPS - 1
    ).astype(jnp.float32).astype(jnp.bfloat16)
    taps = jnp.broadcast_to(taps_ref[...].astype(jnp.float32), (SB, TAPS)).astype(jnp.bfloat16)
    taps = jnp.dot(taps, mirror, preferred_element_type=jnp.float32)[:1]
    banded = jnp.concatenate([taps, jnp.zeros((1, SPAN - TAPS), jnp.float32)], axis=1)
    banded = jnp.broadcast_to(banded, (LANE, SPAN))
    banded = pltpu.roll(banded, DEC, 1, stride=DEC, stride_axis=0).astype(jnp.bfloat16)
    picks = (lax.broadcasted_iota(jnp.int32, (stations, stations), 0) == order_ref[...]).astype(jnp.float32)
    picks = picks.T.astype(jnp.bfloat16)

    pl.semaphore_wait(barrier, len(greeted))

    halo_copy = pltpu.make_async_remote_copy(
        src_ref=raw_ref.at[:, local_time - TAPS :],
        dst_ref=halo,
        send_sem=halo_sems.at[0],
        recv_sem=halo_sems.at[1],
        device_id={"sta": after},
        device_id_type=MESH,
    )

    @pl.when(me < members - 1)
    def _():
        halo_copy.start()

    def line_copy(source, piece, n, peer):
        return pltpu.make_async_remote_copy(
            src_ref=column.at[source, piece],
            dst_ref=column.at[source, piece],
            send_sem=line_send.at[piece * line + n],
            recv_sem=line_recv.at[source * pieces + piece],
            device_id={"sta": peer * QUAD + lead},
            device_id_type=MESH,
        )

    at_end = (rank == 0) | (rank == line - 1)
    beside_end = (rank == 1) | (rank == line - 2)
    far_end = jnp.where(rank == 1, 0, line - 1)
    relayed = line > 3
    picks_sent = []

    def share(source, piece, samples):
        private[...] = samples.reshape(private.shape)
        plane = (source * QUAD + lead) * pieces + piece
        for k, peer in enumerate(others + (me,)):
            blocks = [pairing_ref[r, peer] for r in range(ROUNDS)] + [peer]
            slot = len(picks_sent)
            for g, block in enumerate(blocks):
                chosen = private[block]
                if k < len(others):
                    picked[slot, g * SB : (g + 1) * SB, :] = chosen
                else:
                    out_ref[plane, g * SB : (g + 1) * SB, :] = chosen
            if k < len(others):
                copy = pltpu.make_async_remote_copy(
                    src_ref=picked.at[slot],
                    dst_ref=out_ref.at[plane],
                    send_sem=pick_send.at[slot],
                    recv_sem=pick_recv.at[plane],
                    device_id={"sta": peer},
                    device_id_type=MESH,
                )
                copy.start()
                picks_sent.append(copy)

    dims = (((1,), (1,)), ((), ()))

    def filtered(piece, samples):
        summed = lax.dot_general(samples, banded, dims, preferred_element_type=jnp.float32)
        ordered = jnp.dot(picks, summed.astype(jnp.bfloat16), preferred_element_type=jnp.float32).astype(jnp.bfloat16)
        column[rank, piece] = ordered
        for n, peer in enumerate(line_order):
            if n == line - 2 and relayed:

                @pl.when(jnp.logical_not(at_end))
                def _():
                    line_copy(rank, piece, n, peer).start()
            else:
                line_copy(rank, piece, n, peer).start()
        share(rank, piece, ordered)

    raw_copy.wait()
    for piece in range(pieces - 1, 0, -1):
        first = piece * LANE * DEC - TAPS
        filtered(piece, raw[:, first : first + SPAN])

    @pl.when(me > 0)
    def _():
        halo_copy.wait_recv()

    @pl.when(me == 0)
    def _():
        halo[...] = jnp.zeros_like(halo)

    filtered(0, jnp.concatenate([halo[...], raw[:, : LANE * DEC]], axis=1))

    for n, source in enumerate(line_order):
        for piece in range(pieces - 1, -1, -1):
            line_copy(source, piece, n, source).wait_recv()
            if n == line - 2 and relayed:

                @pl.when(beside_end)
                def _():
                    line_copy(source, piece, line - 1, far_end).start()

            share(source, piece, column[source, piece])

    for source in range(line):
        for piece in range(pieces):
            for peer in others:
                plane = peer - rank * QUAD + source * QUAD
                plane = plane * pieces + piece
                pltpu.make_async_remote_copy(
                    src_ref=picked.at[0],
                    dst_ref=out_ref.at[plane],
                    send_sem=pick_send.at[0],
                    recv_sem=pick_recv.at[plane],
                    device_id={"sta": twin},
                    device_id_type=MESH,
                ).wait_recv()
    for copy in picks_sent:
        copy.wait_send()
    for piece in range(pieces):
        for n, peer in enumerate(line_order):
            if n == line - 2 and relayed:

                @pl.when(jnp.logical_not(at_end))
                def _():
                    line_copy(rank, piece, n, peer).wait_send()
            else:
                line_copy(rank, piece, n, peer).wait_send()
        if relayed:

            @pl.when(beside_end)
            def _():
                line_copy(line_order[-1], piece, line - 1, far_end).wait_send()

    @pl.when(me < members - 1)
    def _():
        halo_copy.wait_send()


def correlate_kernel(
    starts_ref,
    low_ref,
    dft_ref,
    lag_ref,
    out_ref,
    ahead,
    back,
    even_theirs,
    odd_theirs,
    even_own,
    odd_own,
    white_own,
    left,
    right,
    cross_real,
    cross_imag,
):
    tile = pl.program_id(0)
    planes = low_ref.shape[0]
    window_count = starts_ref.shape[0]
    lane = lax.broadcasted_iota(jnp.int32, (1, LANE), 1)

    @pl.when(tile == 0)
    def _():
        mirror = (
            lax.broadcasted_iota(jnp.int32, (LANE, LANE), 0) + lax.broadcasted_iota(jnp.int32, (LANE, LANE), 1)
            == LANE - 1
        ).astype(jnp.float32).astype(jnp.bfloat16)
        back[0] = jnp.zeros((ROWS, LANE), jnp.float32)

        def one_plane(n, carry):
            samples = low_ref[n]
            ahead[n] = samples.astype(jnp.float32)
            back[planes - n] = jnp.dot(samples, mirror, preferred_element_type=jnp.float32)
            return carry

        lax.fori_loop(0, planes, one_plane, 0, unroll=8)

        def one_window(w, carry):
            def shifted(ref, first):
                plane = first // LANE
                keep = LANE - first % LANE
                shift = keep % LANE
                now = pltpu.roll(ref[plane], shift, 1)
                pieces = []
                for piece in range(FOLD // LANE):
                    later = pltpu.roll(ref[plane + piece + 1], shift, 1)
                    pieces.append(jnp.where(lane < keep, now, later))
                    now = later
                return pieces, now

            start = starts_ref[w]
            forward, middle = shifted(ahead, start)
            backward, _ = shifted(back, planes * LANE - 1 - FOLD * 2 + LANE - start)
            theirs = pl.ds(pl.multiple_of(w * THEIRS, SB), THEIRS)
            own = pl.ds(pl.multiple_of(w * SB, SB), SB)
            for piece, (a, b) in enumerate(zip(forward, backward)):
                at = slice(piece * LANE, (piece + 1) * LANE)
                even, odd = a + b, a - b
                if piece == 0:
                    even = jnp.where(lane == 0, middle, even)
                even, odd = even.astype(jnp.bfloat16), odd.astype(jnp.bfloat16)
                even_theirs[theirs, at] = even[:THEIRS]
                odd_theirs[theirs, at] = odd[:THEIRS]
                even_own[own, at] = even[THEIRS:]
                odd_own[own, at] = odd[THEIRS:]
            return carry

        lax.fori_loop(0, window_count, one_window, 0, unroll=2)

    def dot_nt(a, b):
        return lax.dot_general(a, b, NT, preferred_element_type=jnp.float32)

    half = LANE // 2
    pairs = window_count // 2
    wide = 2 * LANE
    first = lane < half
    for tile_pair in range(window_count * THEIRS // wide):
        at = slice(tile_pair * wide, (tile_pair + 1) * wide)
        reals = dot_nt(dft_ref[0], even_theirs[at, :])
        imags = dot_nt(dft_ref[1], odd_theirs[at, :])
        for n in range(FT // BAND):
            for inner in range(wide // LANE):
                pair = tile_pair * (wide // LANE) + inner
                real, imag = (
                    x[n * BAND : (n + 1) * BAND, inner * LANE : (inner + 1) * LANE] for x in (reals, imags)
                )
                level = jnp.sum(real * real + imag * imag, axis=0, keepdims=True)
                scale = lax.rsqrt(level * (1.0 / (2 * BAND)) + 1e-06)
                real, imag = real * scale, imag * scale
                real_turned, imag_turned = pltpu.roll(real, half, 1), pltpu.roll(imag, half, 1)
                blocks = (
                    (jnp.where(first, real, -imag_turned), jnp.where(first, real_turned, -imag)),
                    (jnp.where(first, imag, real_turned), jnp.where(first, imag_turned, real)),
                )
                for c, block in enumerate(blocks):
                    both = [x.reshape(BAND // PACK, 1, PACK, LANE) for x in block]
                    both = jnp.concatenate(both, axis=1).reshape(BAND // PACK, 2 * PACK, LANE)
                    row = (c * pairs + pair) * 2 * PACK
                    right[n * (BAND // PACK) : (n + 1) * (BAND // PACK), row : row + 2 * PACK, :] = both.astype(
                        jnp.bfloat16
                    )

    real, imag = dot_nt(even_own[...], dft_ref[0]), dot_nt(odd_own[...], dft_ref[1])
    power = (real * real + imag * imag).astype(jnp.bfloat16)
    same = (
        lax.broadcasted_iota(jnp.int32, (FT, FT), 0) // BAND == lax.broadcasted_iota(jnp.int32, (FT, FT), 1) // BAND
    ).astype(jnp.float32).astype(jnp.bfloat16)
    level = jnp.dot(power, same, preferred_element_type=jnp.float32)
    scale = lax.rsqrt(level * (1.0 / (2 * BAND)) + 1e-06)
    white_own[0] = real * scale
    white_own[1] = imag * scale

    slots = LANE // PACK
    for part in range(FT // LANE):
        for c in range(2):
            moved = [[], []]
            for pair in range(pairs):
                x = [
                    white_own[c, (2 * pair + k) * SB : (2 * pair + k + 1) * SB, part * LANE : (part + 1) * LANE]
                    for k in range(2)
                ]
                low_slot = lane // PACK % 2 == 0
                y = (
                    jnp.where(low_slot, x[0], pltpu.roll(x[1], PACK, 1)),
                    jnp.where(low_slot, pltpu.roll(x[0], LANE - PACK, 1), x[1]),
                )
                for k in range(2):
                    moved[k].append(pltpu.roll(y[k], 2 * PACK * pair, 1) if pair else y[k])
            for slot in range(slots):
                turn, k = slot // 2, slot % 2
                joined = moved[k][0]
                for pair in range(1, pairs):
                    joined = jnp.where(lane // (2 * PACK) == (turn + pair) % (slots // 2), moved[k][pair], joined)
                if turn:
                    joined = pltpu.roll(joined, LANE - 2 * PACK * turn, 1)
                left[part * slots + slot, c] = joined.astype(jnp.bfloat16)

    own_bin = lax.broadcasted_iota(jnp.int32, (PACK * SB, LANE), 0) // SB
    mask = (own_bin == lax.broadcasted_iota(jnp.int32, (PACK * SB, LANE), 1) % PACK).astype(jnp.float32).astype(
        jnp.bfloat16
    )

    def one_group(n, carry):
        masked = jnp.concatenate([jnp.concatenate([left[n, c]] * PACK, axis=0) * mask for c in range(2)], axis=1)
        product = jnp.dot(masked, right[n], preferred_element_type=jnp.float32)
        product = product.reshape(PACK, 2, SB // 2, LANE)
        first = lane < half
        a, b = product[:, 0].reshape(PACK * SB // 2, LANE), product[:, 1].reshape(PACK * SB // 2, LANE)
        a_turned, b_turned = pltpu.roll(a, half, 1), pltpu.roll(b, half, 1)
        at = pl.ds(pl.multiple_of((tile * (FT // PACK) + n) * PACK * SB // 2, PACK * SB // 2), PACK * SB // 2)
        cross_real[at, :] = jnp.where(first, a, b_turned)
        cross_imag[at, :] = jnp.where(first, a_turned, b)
        return carry

    lax.fori_loop(0, FT // PACK, one_group, 0, unroll=16)

    @pl.when(tile == pl.num_programs(0) - 1)
    def _():
        def two_stations(n, carry):
            summed = None
            for k, cross in enumerate((cross_real, cross_imag)):
                columns = jnp.concatenate(
                    [cross[pl.ds(2 * n + m, BINS, stride=SB // 2), :].astype(jnp.bfloat16) for m in range(2)], axis=1
                )
                term = jnp.dot(lag_ref[k], columns, preferred_element_type=jnp.float32)
                summed = term if summed is None else summed + term
            turned = summed.T
            for m in range(2):
                for h in range(2):
                    i = h * (SB // 2) + 2 * n + m
                    for r in range(ROUNDS):
                        first = ((m * 2 + h) * ROUNDS + r) * SB
                        out_ref[r, pl.ds(pl.multiple_of(i * SB, SB), SB), :] = turned[first : first + SB]
            return carry

        lax.fori_loop(0, SB // 4, two_stations, 0, unroll=True)


def correlate(window_starts, low, dft, lag):
    window_count = window_starts.shape[0]
    planes = low.shape[0]
    grid_spec = pltpu.PrefetchScalarGridSpec(
        num_scalar_prefetch=1,
        grid=(TILES,),
        in_specs=[
            pl.BlockSpec((planes, ROWS, LANE), lambda n, *_: (0, 0, 0)),
            pl.BlockSpec((2, FT, FOLD), lambda n, *_: (0, n, 0)),
            pl.BlockSpec((2, LAGS, BINS), lambda n, *_: (0, 0, 0)),
        ],
        out_specs=pl.BlockSpec((ROUNDS, SB * SB, LAGS), lambda n, *_: (0, 0, 0)),
        scratch_shapes=[
            pltpu.VMEM((planes, ROWS, LANE), jnp.float32),
            pltpu.VMEM((planes + 1, ROWS, LANE), jnp.float32),
            pltpu.VMEM((window_count * THEIRS, FOLD), jnp.bfloat16),
            pltpu.VMEM((window_count * THEIRS, FOLD), jnp.bfloat16),
            pltpu.VMEM((window_count * SB, FOLD), jnp.bfloat16),
            pltpu.VMEM((window_count * SB, FOLD), jnp.bfloat16),
            pltpu.VMEM((2, window_count * SB, FT), jnp.float32),
            pltpu.VMEM((FT // PACK, 2, SB, LANE), jnp.bfloat16),
            pltpu.VMEM((FT // PACK, 2 * LANE, LANE), jnp.bfloat16),
            pltpu.VMEM((BINS * SB // 2, LANE), jnp.float32),
            pltpu.VMEM((BINS * SB // 2, LANE), jnp.float32),
        ],
    )
    return pl.pallas_call(
        correlate_kernel,
        grid_spec=grid_spec,
        out_shape=jax.ShapeDtypeStruct((ROUNDS, SB * SB, LAGS), jnp.float32),
        compiler_params=pltpu.CompilerParams(vmem_limit_bytes=56 * 2**20),
    )(window_starts, low, dft, lag)


def body(raw_traces, filter_taps, station_order, window_starts, pairing):
    members = lax.axis_size("sta")
    stations, local_time = raw_traces.shape
    window_count = window_starts.shape[0]
    pieces = local_time // (LANE * DEC)
    line = members // QUAD
    in_vmem = pl.BlockSpec(memory_space=pltpu.VMEM)
    low = pl.pallas_call(
        functools.partial(gather_kernel, members),
        out_shape=jax.ShapeDtypeStruct((members * pieces, ROWS, LANE), jnp.bfloat16),
        in_specs=[
            pl.BlockSpec(memory_space=pl.ANY),
            in_vmem,
            in_vmem,
            pl.BlockSpec(memory_space=pltpu.SMEM),
        ],
        out_specs=in_vmem,
        scratch_shapes=[
            pltpu.VMEM((stations, local_time), jnp.bfloat16),
            pltpu.VMEM((stations, TAPS), jnp.bfloat16),
            pltpu.VMEM((line, pieces, stations, LANE), jnp.bfloat16),
            pltpu.VMEM((stations // SB, SB, LANE), jnp.bfloat16),
            pltpu.VMEM((3 * line * pieces, ROWS, LANE), jnp.bfloat16),
            pltpu.SemaphoreType.DMA,
            pltpu.SemaphoreType.DMA((2,)),
            pltpu.SemaphoreType.DMA((line * pieces,)),
            pltpu.SemaphoreType.DMA((line * pieces,)),
            pltpu.SemaphoreType.DMA((3 * line * pieces,)),
            pltpu.SemaphoreType.DMA((members * pieces,)),
        ],
        compiler_params=pltpu.CompilerParams(
            collective_id=0, has_side_effects=True, vmem_limit_bytes=40 * 2**20
        ),
    )(raw_traces, filter_taps.reshape(1, TAPS), station_order.reshape(1, stations), pairing)
    correlated = correlate(window_starts, low, jnp.asarray(dft_table()), jnp.asarray(lag_table(window_count)))
    return correlated.reshape(ROUNDS, SB, SB, LAGS)


def solution(mesh):
    return jax.shard_map(
        body,
        mesh=mesh,
        in_specs=(P("parts", "sta"), P(), P("parts"), P("parts"), P()),
        out_specs=P(None, ("parts", "sta"), None, None),
        check_vma=False,
    )
```

```python
import functools
import math

import jax
import jax.numpy as jnp
import ml_dtypes
import numpy as np
from jax import lax
from jax.experimental import pallas as pl
from jax.experimental.pallas import tpu as pltpu
from jax.sharding import PartitionSpec as P

SB = 16
DEC = 4
TAPS = 256
SEG = 2048
BAND = 64
LAGS = 256
ROUNDS = 4
BINS = 1024
LANE = 128
SPAN = LANE * DEC + TAPS
GROUPS = ROUNDS + 1
ROWS = GROUPS * SB
THEIRS = ROUNDS * SB
FOLD = SEG // 4
FT = 512
HT = FT // 2
TILES = BINS // FT
PACK = 8
NT = (((1,), (1,)), ((), ()))
QUAD = 4
MESH = pl.DeviceIdType.MESH


def taper_table():
    sample = np.arange(-LANE, 7 * LANE)
    return (0.5 - 0.5 * np.cos(sample * (2.0 * math.pi / SEG))).astype(np.float32).reshape(8, LANE)


def dft_table():
    sample = np.arange(FOLD)
    kinds = []
    for wave in (np.cos, lambda a: -np.sin(a)):
        for parity in range(2):
            frequency = 2 * np.arange(BINS // 2) + parity
            table = np.zeros((BINS // 2, FOLD + LANE))
            table[:, :FOLD] = wave((sample[None, :] * frequency[:, None] % SEG) * (2.0 * math.pi / SEG))
            middle = np.round(wave((frequency * FOLD % SEG) * (2.0 * math.pi / SEG)))
            if wave is np.cos:
                table[:, 0] = 0.5
                table[:, FOLD] = middle
            else:
                table[:, 0] = middle
            kinds.append(table)
    return np.stack(kinds).astype(np.float32).astype(ml_dtypes.bfloat16)


def lag_table(window_count):
    frequency = 2 * np.arange(BINS // 2).reshape(TILES, 1, HT) + np.arange(2).reshape(1, 2, 1)
    frequency = frequency.reshape(BINS)
    offset = np.arange(LAGS) - LAGS // 2 + SEG
    angles = (frequency[None, :] * offset[:, None] % SEG) * (2.0 * math.pi / SEG)
    scale = 1.0 / math.sqrt(BINS * window_count)
    both = np.stack([np.cos(angles) * scale, -np.sin(angles) * scale])
    return both.astype(np.float32).astype(ml_dtypes.bfloat16)


def gather_kernel(
    members,
    raw_ref,
    taps_ref,
    order_ref,
    pairing_ref,
    out_ref,
    raw,
    halo,
    column,
    private,
    picked,
    raw_sem,
    halo_sems,
    line_send,
    line_recv,
    pick_send,
    pick_recv,
):
    me = lax.axis_index("sta")
    stations, local_time = raw_ref.shape
    line, pieces = column.shape[:2]
    rank, lead = me // QUAD, me % QUAD
    turn = 1 - 2 * lax.rem(me, 2)
    twin = me + turn
    across = rank * QUAD + lax.rem(lead + 2, QUAD)
    others = (across, across + turn, twin)
    after, before = lax.rem(me + 1, members), lax.rem(me + members - 1, members)

    def nearest(n):
        chosen = None
        for r in range(line):
            order = sorted((x for x in range(line) if x != r), key=lambda x: abs(x - r))
            chosen = order[n] if chosen is None else jnp.where(rank == r, order[n], chosen)
        return chosen

    line_order = [nearest(n) for n in range(line - 1)]

    raw_copy = pltpu.make_async_copy(raw_ref, raw, raw_sem)
    raw_copy.start()

    barrier = pltpu.get_barrier_semaphore()
    greeted = [r * QUAD + lead for r in line_order] + list(others) + [after, before]
    for peer in greeted:
        pl.semaphore_signal(barrier, inc=1, device_id={"sta": peer}, device_id_type=MESH)

    mirror = (
        lax.broadcasted_iota(jnp.int32, (TAPS, TAPS), 0) + lax.broadcasted_iota(jnp.int32, (TAPS, TAPS), 1) == TAPS - 1
    ).astype(jnp.float32).astype(jnp.bfloat16)
    taps = jnp.broadcast_to(taps_ref[...].astype(jnp.float32), (SB, TAPS)).astype(jnp.bfloat16)
    taps = jnp.dot(taps, mirror, preferred_element_type=jnp.float32)[:1]
    banded = jnp.concatenate([taps, jnp.zeros((1, SPAN - TAPS), jnp.float32)], axis=1)
    banded = jnp.broadcast_to(banded, (LANE, SPAN))
    banded = pltpu.roll(banded, DEC, 1, stride=DEC, stride_axis=0).astype(jnp.bfloat16)
    picks = (lax.broadcasted_iota(jnp.int32, (stations, stations), 0) == order_ref[...]).astype(jnp.float32)
    picks = picks.T.astype(jnp.bfloat16)

    pl.semaphore_wait(barrier, len(greeted))

    halo_copy = pltpu.make_async_remote_copy(
        src_ref=raw_ref.at[:, local_time - TAPS :],
        dst_ref=halo,
        send_sem=halo_sems.at[0],
        recv_sem=halo_sems.at[1],
        device_id={"sta": after},
        device_id_type=MESH,
    )

    @pl.when(me < members - 1)
    def _():
        halo_copy.start()

    def line_copy(source, piece, n, peer):
        return pltpu.make_async_remote_copy(
            src_ref=column.at[source, piece],
            dst_ref=column.at[source, piece],
            send_sem=line_send.at[piece * line + n],
            recv_sem=line_recv.at[source * pieces + piece],
            device_id={"sta": peer * QUAD + lead},
            device_id_type=MESH,
        )

    at_end = (rank == 0) | (rank == line - 1)
    beside_end = (rank == 1) | (rank == line - 2)
    far_end = jnp.where(rank == 1, 0, line - 1)
    relayed = line > 3
    picks_sent = []

    def share(source, piece, samples):
        private[...] = samples.reshape(private.shape)
        plane = (source * QUAD + lead) * pieces + piece
        for k, peer in enumerate(others + (me,)):
            blocks = [pairing_ref[r, peer] for r in range(ROUNDS)] + [peer]
            slot = len(picks_sent)
            for g, block in enumerate(blocks):
                chosen = private[block]
                if k < len(others):
                    picked[slot, g * SB : (g + 1) * SB, :] = chosen
                else:
                    out_ref[plane, g * SB : (g + 1) * SB, :] = chosen
            if k < len(others):
                copy = pltpu.make_async_remote_copy(
                    src_ref=picked.at[slot],
                    dst_ref=out_ref.at[plane],
                    send_sem=pick_send.at[slot],
                    recv_sem=pick_recv.at[plane],
                    device_id={"sta": peer},
                    device_id_type=MESH,
                )
                copy.start()
                picks_sent.append(copy)

    dims = (((1,), (1,)), ((), ()))

    def filtered(piece, samples):
        summed = lax.dot_general(samples, banded, dims, preferred_element_type=jnp.float32)
        ordered = jnp.dot(picks, summed.astype(jnp.bfloat16), preferred_element_type=jnp.float32).astype(jnp.bfloat16)
        column[rank, piece] = ordered
        for n, peer in enumerate(line_order):
            if n == line - 2 and relayed:

                @pl.when(jnp.logical_not(at_end))
                def _():
                    line_copy(rank, piece, n, peer).start()
            else:
                line_copy(rank, piece, n, peer).start()
        share(rank, piece, ordered)

    raw_copy.wait()
    for piece in range(pieces - 1, 0, -1):
        first = piece * LANE * DEC - TAPS
        filtered(piece, raw[:, first : first + SPAN])

    @pl.when(me > 0)
    def _():
        halo_copy.wait_recv()

    @pl.when(me == 0)
    def _():
        halo[...] = jnp.zeros_like(halo)

    filtered(0, jnp.concatenate([halo[...], raw[:, : LANE * DEC]], axis=1))

    for n, source in enumerate(line_order):
        for piece in range(pieces - 1, -1, -1):
            line_copy(source, piece, n, source).wait_recv()
            if n == line - 2 and relayed:

                @pl.when(beside_end)
                def _():
                    line_copy(source, piece, line - 1, far_end).start()

            share(source, piece, column[source, piece])

    for source in range(line):
        for piece in range(pieces):
            for peer in others:
                plane = peer - rank * QUAD + source * QUAD
                plane = plane * pieces + piece
                pltpu.make_async_remote_copy(
                    src_ref=picked.at[0],
                    dst_ref=out_ref.at[plane],
                    send_sem=pick_send.at[0],
                    recv_sem=pick_recv.at[plane],
                    device_id={"sta": twin},
                    device_id_type=MESH,
                ).wait_recv()
    for copy in picks_sent:
        copy.wait_send()
    for piece in range(pieces):
        for n, peer in enumerate(line_order):
            if n == line - 2 and relayed:

                @pl.when(jnp.logical_not(at_end))
                def _():
                    line_copy(rank, piece, n, peer).wait_send()
            else:
                line_copy(rank, piece, n, peer).wait_send()
        if relayed:

            @pl.when(beside_end)
            def _():
                line_copy(line_order[-1], piece, line - 1, far_end).wait_send()

    @pl.when(me < members - 1)
    def _():
        halo_copy.wait_send()


def correlate_kernel(
    starts_ref,
    low_ref,
    taper_ref,
    dft_hbm,
    lag_hbm,
    out_ref,
    dft_ref,
    lag_ref,
    ahead,
    back,
    theirs,
    own,
    white_own,
    left,
    right,
    cross_real,
    cross_imag,
    dft_sems,
    lag_sem,
):
    tile = pl.program_id(0)
    planes = low_ref.shape[0]
    window_count = starts_ref.shape[0]
    lane = lax.broadcasted_iota(jnp.int32, (1, LANE), 1)
    dft_copies = [
        pltpu.make_async_copy(
            dft_hbm.at[:, n * HT : (n + 1) * HT, :], dft_ref.at[:, n * HT : (n + 1) * HT, :], dft_sems.at[n]
        )
        for n in range(TILES)
    ]
    lag_copy = pltpu.make_async_copy(lag_hbm, lag_ref, lag_sem)

    @pl.when(tile == 0)
    def _():
        for copy in dft_copies:
            copy.start()
        lag_copy.start()
        mirror = (
            lax.broadcasted_iota(jnp.int32, (LANE, LANE), 0) + lax.broadcasted_iota(jnp.int32, (LANE, LANE), 1) == LANE
        ).astype(jnp.float32).astype(jnp.bfloat16)

        def one_plane(n, carry):
            samples = low_ref[n]
            ahead[n] = samples.astype(jnp.float32)
            turned = jnp.dot(samples, mirror, preferred_element_type=jnp.float32)
            later = low_ref[jnp.minimum(n + 1, planes - 1)].astype(jnp.float32)
            later = jnp.where(n + 1 < planes, later, jnp.zeros_like(later))
            back[planes - 1 - n] = jnp.where(lane == 0, later, turned)
            return carry

        lax.fori_loop(0, planes, one_plane, 0, unroll=8)

        def one_window(w, carry):
            start = starts_ref[w]
            plane, rest = start // LANE, start % LANE
            taper = taper_ref[...]
            fore = pltpu.roll(taper, rest, 1)
            hind = pltpu.roll(taper, (LANE - rest) % LANE, 1)
            span = SEG // LANE
            rise = [jnp.where(lane >= rest, fore[p + 1 : p + 2], fore[p : p + 1]) for p in range(FOLD // LANE + 1)]
            fall = [
                jnp.where(lane < LANE - rest, hind[p + 1 : p + 2], hind[p + 2 : p + 3]) for p in range(FOLD // LANE)
            ]
            at = pl.ds(pl.multiple_of(w * THEIRS, SB), THEIRS)
            own_at = pl.ds(pl.multiple_of(w * SB, SB), SB)

            def put(kind, p, values):
                values = values.astype(jnp.bfloat16)
                lanes = slice(p * LANE, (p + 1) * LANE)
                theirs[kind, at, lanes] = values[:THEIRS]
                own[kind, own_at, lanes] = values[THEIRS:]

            last = FOLD // LANE
            a = rise[last] * ahead[plane + last]
            b = (1.0 - rise[last]) * ahead[plane + last + span // 2]
            put(0, last, a + b)
            middle = a - b
            for p in range(FOLD // LANE):
                first = ahead[plane + p]
                if p == 0:
                    first = jnp.where(lane < rest, ahead[jnp.minimum(plane + span, planes - 1)], first)
                a = rise[p] * first
                b = (1.0 - rise[p]) * ahead[plane + span // 2 + p]
                c = fall[p] * back[planes - plane - span + p]
                d = (1.0 - fall[p]) * back[planes - plane - span // 2 + p]
                same, apart = a + b, a - b
                same_turned, apart_turned = d + c, d - c
                put(0, p, same + same_turned)
                put(1, p, apart - apart_turned)
                put(2, p, same - same_turned)
                summed = apart + apart_turned
                put(3, p, jnp.where(lane == 0, middle, summed) if p == 0 else summed)
            return carry

        lax.fori_loop(0, window_count, one_window, 0, unroll=2)

    for n, copy in enumerate(dft_copies):

        @pl.when(tile == n)
        def _():
            copy.wait()

    def dot_nt(a, b):
        return lax.dot_general(a, b, NT, preferred_element_type=jnp.float32)

    bins = pl.ds(pl.multiple_of(tile * HT, HT), HT)
    depth = (FOLD + LANE, FOLD, FOLD, FOLD)
    half = LANE // 2
    wide = 2 * LANE
    first = lane < half
    slots = LANE // PACK
    turns = slots // 2
    strip = BAND // 2
    halves = HT // PACK
    for tile_pair in range(window_count * THEIRS // wide):
        at = slice(tile_pair * wide, (tile_pair + 1) * wide)
        spectra = [dot_nt(dft_ref[k, bins, : depth[k]], theirs[k, at, : depth[k]]) for k in range(4)]
        for n in range(HT // strip):
            for inner in range(wide // LANE):
                parts = [x[n * strip : (n + 1) * strip, inner * LANE : (inner + 1) * LANE] for x in spectra]
                power = sum(x * x for x in parts[1:]) + parts[0] * parts[0]
                level = jnp.sum(power, axis=0, keepdims=True)
                scale = lax.rsqrt(level * (1.0 / (2 * BAND)) + 1e-06)
                for parity in range(2):
                    real, imag = parts[parity] * scale, parts[2 + parity] * scale

                    def stacked(x, y):
                        both = [v.reshape(strip // PACK, 1, PACK, LANE) for v in (x, y)]
                        both = jnp.concatenate(both, axis=1).reshape(strip * 2, LANE)
                        return both.astype(jnp.bfloat16)

                    plain, crossed = stacked(real, imag), stacked(-imag, real)
                    turned = pltpu.roll(jnp.where(first, crossed, plain), half, 1)
                    for k, block in enumerate((jnp.where(first, plain, turned), jnp.where(first, turned, crossed))):
                        w = (tile_pair * (wide // LANE) + inner) * 2 + k
                        for m in range(strip // PACK):
                            group = n * (strip // PACK) + m
                            turn = group % slots // 2
                            row = w // turns * LANE + (w + turn) % turns * 2 * PACK
                            right[parity * halves + group, row : row + 2 * PACK, :] = block[
                                m * 2 * PACK : (m + 1) * 2 * PACK
                            ]

    spectra = [dot_nt(own[k, :, : depth[k]], dft_ref[k, bins, : depth[k]]) for k in range(4)]
    power = sum(x * x for x in spectra[1:]) + spectra[0] * spectra[0]
    same = (
        lax.broadcasted_iota(jnp.int32, (HT, HT), 0) // strip == lax.broadcasted_iota(jnp.int32, (HT, HT), 1) // strip
    ).astype(jnp.float32).astype(jnp.bfloat16)
    level = jnp.dot(power.astype(jnp.bfloat16), same, preferred_element_type=jnp.float32)
    scale = lax.rsqrt(level * (1.0 / (2 * BAND)) + 1e-06)
    for k in range(4):
        white_own[k] = (spectra[k] * scale).astype(jnp.bfloat16)

    low_slot = lane // PACK % 2 == 0
    for parity in range(2):
        for part in range(HT // LANE):
            for h in range(window_count // turns):
                moved = [[], []]
                for w in range(turns):
                    row = (h * turns + w) * SB
                    x = [
                        white_own[2 * c + parity, row : row + SB, part * LANE : (part + 1) * LANE] for c in range(2)
                    ]
                    y = (
                        jnp.where(low_slot, x[0], pltpu.roll(x[1], PACK, 1)),
                        jnp.where(low_slot, pltpu.roll(x[0], LANE - PACK, 1), x[1]),
                    )
                    for k in range(2):
                        moved[k].append(pltpu.roll(y[k], 2 * PACK * w, 1) if w else y[k])
                for slot in range(slots):
                    turn, k = slot // 2, slot % 2
                    joined = moved[k][0]
                    for w in range(1, turns):
                        joined = jnp.where(lane // (2 * PACK) == (turn + w) % turns, moved[k][w], joined)
                    left[parity * halves + part * slots + slot, h] = joined

    own_bin = lax.broadcasted_iota(jnp.int32, (PACK * SB, LANE), 0) // SB
    mask = (own_bin == lax.broadcasted_iota(jnp.int32, (PACK * SB, LANE), 1) % PACK).astype(jnp.float32).astype(
        jnp.bfloat16
    )

    def one_group(n, carry):
        masked = jnp.concatenate([jnp.concatenate([left[n, h]] * PACK, axis=0) * mask for h in range(2)], axis=1)
        product = jnp.dot(masked, right[n], preferred_element_type=jnp.float32)
        product = product.reshape(PACK, 2, SB // 2, LANE)
        a, b = product[:, 0].reshape(PACK * SB // 2, LANE), product[:, 1].reshape(PACK * SB // 2, LANE)
        turned = pltpu.roll(jnp.where(first, b, a), half, 1)
        at = pl.ds(pl.multiple_of((tile * (FT // PACK) + n) * PACK * SB // 2, PACK * SB // 2), PACK * SB // 2)
        cross_real[at, :] = jnp.where(first, a, turned)
        cross_imag[at, :] = jnp.where(first, turned, b)
        return carry

    lax.fori_loop(0, FT // PACK, one_group, 0, unroll=16)

    @pl.when(tile == pl.num_programs(0) - 1)
    def _():
        lag_copy.wait()

        def two_stations(n, carry):
            summed = None
            for k, cross in enumerate((cross_real, cross_imag)):
                columns = jnp.concatenate(
                    [cross[pl.ds(2 * n + m, BINS, stride=SB // 2), :].astype(jnp.bfloat16) for m in range(2)], axis=1
                )
                term = jnp.dot(lag_ref[k], columns, preferred_element_type=jnp.float32)
                summed = term if summed is None else summed + term
            turned = summed.T
            for m in range(2):
                for h in range(2):
                    i = h * (SB // 2) + 2 * n + m
                    for r in range(ROUNDS):
                        row = ((m * 2 + h) * ROUNDS + r) * SB
                        out_ref[r, pl.ds(pl.multiple_of(i * SB, SB), SB), :] = turned[row : row + SB]
            return carry

        lax.fori_loop(0, SB // 4, two_stations, 0, unroll=True)


def correlate(window_starts, low, taper, dft, lag):
    window_count = window_starts.shape[0]
    planes = low.shape[0]
    grid_spec = pltpu.PrefetchScalarGridSpec(
        num_scalar_prefetch=1,
        grid=(TILES,),
        in_specs=[
            pl.BlockSpec((planes, ROWS, LANE), lambda n, *_: (0, 0, 0)),
            pl.BlockSpec((8, LANE), lambda n, *_: (0, 0)),
            pl.BlockSpec(memory_space=pl.ANY),
            pl.BlockSpec(memory_space=pl.ANY),
        ],
        out_specs=pl.BlockSpec((ROUNDS, SB * SB, LAGS), lambda n, *_: (0, 0, 0)),
        scratch_shapes=[
            pltpu.VMEM(dft.shape, jnp.bfloat16),
            pltpu.VMEM(lag.shape, jnp.bfloat16),
            pltpu.VMEM((planes, ROWS, LANE), jnp.float32),
            pltpu.VMEM((planes, ROWS, LANE), jnp.float32),
            pltpu.VMEM((4, window_count * THEIRS, FOLD + LANE), jnp.bfloat16),
            pltpu.VMEM((4, window_count * SB, FOLD + LANE), jnp.bfloat16),
            pltpu.VMEM((4, window_count * SB, HT), jnp.bfloat16),
            pltpu.VMEM((FT // PACK, 2, SB, LANE), jnp.bfloat16),
            pltpu.VMEM((FT // PACK, 2 * LANE, LANE), jnp.bfloat16),
            pltpu.VMEM((BINS * SB // 2, LANE), jnp.float32),
            pltpu.VMEM((BINS * SB // 2, LANE), jnp.float32),
            pltpu.SemaphoreType.DMA((TILES,)),
            pltpu.SemaphoreType.DMA,
        ],
    )
    return pl.pallas_call(
        correlate_kernel,
        grid_spec=grid_spec,
        out_shape=jax.ShapeDtypeStruct((ROUNDS, SB * SB, LAGS), jnp.float32),
        compiler_params=pltpu.CompilerParams(vmem_limit_bytes=60 * 2**20),
    )(window_starts, low, taper, dft, lag)


def body(raw_traces, filter_taps, station_order, window_starts, pairing):
    members = lax.axis_size("sta")
    stations, local_time = raw_traces.shape
    window_count = window_starts.shape[0]
    pieces = local_time // (LANE * DEC)
    line = members // QUAD
    in_vmem = pl.BlockSpec(memory_space=pltpu.VMEM)
    low = pl.pallas_call(
        functools.partial(gather_kernel, members),
        out_shape=jax.ShapeDtypeStruct((members * pieces, ROWS, LANE), jnp.bfloat16),
        in_specs=[
            pl.BlockSpec(memory_space=pl.ANY),
            in_vmem,
            in_vmem,
            pl.BlockSpec(memory_space=pltpu.SMEM),
        ],
        out_specs=in_vmem,
        scratch_shapes=[
            pltpu.VMEM((stations, local_time), jnp.bfloat16),
            pltpu.VMEM((stations, TAPS), jnp.bfloat16),
            pltpu.VMEM((line, pieces, stations, LANE), jnp.bfloat16),
            pltpu.VMEM((stations // SB, SB, LANE), jnp.bfloat16),
            pltpu.VMEM((3 * line * pieces, ROWS, LANE), jnp.bfloat16),
            pltpu.SemaphoreType.DMA,
            pltpu.SemaphoreType.DMA((2,)),
            pltpu.SemaphoreType.DMA((line * pieces,)),
            pltpu.SemaphoreType.DMA((line * pieces,)),
            pltpu.SemaphoreType.DMA((3 * line * pieces,)),
            pltpu.SemaphoreType.DMA((members * pieces,)),
        ],
        compiler_params=pltpu.CompilerParams(
            collective_id=0, has_side_effects=True, vmem_limit_bytes=60 * 2**20
        ),
    )(raw_traces, filter_taps.reshape(1, TAPS), station_order.reshape(1, stations), pairing)
    correlated = correlate(
        window_starts,
        low,
        jnp.asarray(taper_table()),
        jnp.asarray(dft_table()),
        jnp.asarray(lag_table(window_count)),
    )
    return correlated.reshape(ROUNDS, SB, SB, LAGS)


def solution(mesh):
    return jax.shard_map(
        body,
        mesh=mesh,
        in_specs=(P("parts", "sta"), P(), P("parts"), P("parts"), P()),
        out_specs=P(None, ("parts", "sta"), None, None),
        check_vma=False,
    )
```

```python
import functools
import math

import jax
import jax.numpy as jnp
import ml_dtypes
import numpy as np
from jax import lax
from jax.experimental import pallas as pl
from jax.experimental.pallas import tpu as pltpu
from jax.sharding import PartitionSpec as P

SB = 16
DEC = 4
TAPS = 256
SEG = 2048
BAND = 64
LAGS = 256
ROUNDS = 4
BINS = 1024
LANE = 128
SPAN = LANE * DEC + TAPS
GROUPS = ROUNDS + 1
ROWS = GROUPS * SB
THEIRS = ROUNDS * SB
FOLD = SEG // 4
FT = 512
HT = FT // 2
TILES = BINS // FT
PACK = 8
NT = (((1,), (1,)), ((), ()))
QUAD = 4
MESH = pl.DeviceIdType.MESH


def taper_table():
    sample = np.arange(-LANE, 7 * LANE)
    return (0.5 - 0.5 * np.cos(sample * (2.0 * math.pi / SEG))).astype(np.float32).reshape(8, LANE)


def dft_table():
    sample = np.arange(FOLD)
    kinds = []
    for wave in (np.cos, lambda a: -np.sin(a)):
        for parity in range(2):
            frequency = 2 * np.arange(BINS // 2) + parity
            table = np.zeros((BINS // 2, FOLD + LANE))
            table[:, :FOLD] = wave((sample[None, :] * frequency[:, None] % SEG) * (2.0 * math.pi / SEG))
            middle = np.round(wave((frequency * FOLD % SEG) * (2.0 * math.pi / SEG)))
            if wave is np.cos:
                table[:, 0] = 0.5
                table[:, FOLD] = middle
            else:
                table[:, 0] = middle
            kinds.append(table)
    return np.stack(kinds).astype(np.float32).astype(ml_dtypes.bfloat16)


def lag_table(window_count):
    frequency = 2 * np.arange(BINS // 2).reshape(TILES, 1, HT) + np.arange(2).reshape(1, 2, 1)
    frequency = frequency.reshape(BINS)
    offset = np.arange(LAGS) - LAGS // 2 + SEG
    angles = (frequency[None, :] * offset[:, None] % SEG) * (2.0 * math.pi / SEG)
    scale = 1.0 / math.sqrt(BINS * window_count)
    both = np.stack([np.cos(angles) * scale, -np.sin(angles) * scale])
    return both.astype(np.float32).astype(ml_dtypes.bfloat16)


def gather_kernel(
    members,
    raw_ref,
    taps_ref,
    order_ref,
    pairing_ref,
    out_ref,
    raw,
    tail,
    halo,
    column,
    private,
    picked,
    raw_sem,
    halo_sems,
    line_send,
    line_recv,
    pick_send,
    pick_recv,
):
    me = lax.axis_index("sta")
    stations, local_time = raw_ref.shape
    line, pieces = column.shape[:2]
    rank, lead = me // QUAD, me % QUAD
    turn = 1 - 2 * lax.rem(me, 2)
    twin = me + turn
    across = rank * QUAD + lax.rem(lead + 2, QUAD)
    others = (across, across + turn, twin)
    after, before = lax.rem(me + 1, members), lax.rem(me + members - 1, members)

    def of_rank(choose):
        chosen = choose(0)
        for r in range(1, line):
            chosen = jnp.where(rank == r, choose(r), chosen)
        return chosen

    def arrivals(r):
        known = sorted((abs(x - r), -piece, x) for x in range(line) if x != r for piece in range(pieces))
        return [(x, -negative) for _, negative, x in known]

    expected = [
        (of_rank(lambda r: arrivals(r)[n][0]), of_rank(lambda r: arrivals(r)[n][1]))
        for n in range((line - 1) * pieces)
    ]

    raw_copy = pltpu.make_async_copy(raw_ref, raw, raw_sem)
    raw_copy.start()

    barrier = pltpu.get_barrier_semaphore()
    greeted = [lax.rem(rank + n, line) * QUAD + lead for n in range(1, line)] + list(others) + [after, before]
    for peer in greeted:
        pl.semaphore_signal(barrier, inc=1, device_id={"sta": peer}, device_id_type=MESH)

    mirror = (
        lax.broadcasted_iota(jnp.int32, (TAPS, TAPS), 0) + lax.broadcasted_iota(jnp.int32, (TAPS, TAPS), 1) == TAPS - 1
    ).astype(jnp.float32).astype(jnp.bfloat16)
    taps = jnp.broadcast_to(taps_ref[...].astype(jnp.float32).reshape(1, TAPS), (SB, TAPS)).astype(jnp.bfloat16)
    taps = jnp.dot(taps, mirror, preferred_element_type=jnp.float32)[:1]
    banded = jnp.concatenate([taps, jnp.zeros((1, SPAN - TAPS), jnp.float32)], axis=1)
    banded = jnp.broadcast_to(banded, (LANE, SPAN))
    banded = pltpu.roll(banded, DEC, 1, stride=DEC, stride_axis=0).astype(jnp.bfloat16)
    picks = (lax.broadcasted_iota(jnp.int32, (stations, stations), 0) == order_ref[...]).astype(jnp.float32)
    picks = picks.T.astype(jnp.bfloat16)

    dims = (((1,), (1,)), ((), ()))
    lane = lax.broadcasted_iota(jnp.int32, (1, LANE), 1)
    half = LANE // 2
    raw_copy.wait()
    spilled = lax.dot_general(
        raw[:, local_time - TAPS :], banded[:, :TAPS], dims, preferred_element_type=jnp.float32
    )
    tail[...] = jnp.where(
        lane < half, spilled[: stations // 2], pltpu.roll(spilled[stations // 2 :], half, 1)
    ).astype(jnp.bfloat16)

    pl.semaphore_wait(barrier, len(greeted))

    halo_copy = pltpu.make_async_remote_copy(
        src_ref=tail,
        dst_ref=halo,
        send_sem=halo_sems.at[0],
        recv_sem=halo_sems.at[1],
        device_id={"sta": after},
        device_id_type=MESH,
    )

    @pl.when(me < members - 1)
    def _():
        halo_copy.start()

    def line_copy(source, piece, n, peer):
        return pltpu.make_async_remote_copy(
            src_ref=column.at[source, piece],
            dst_ref=column.at[source, piece],
            send_sem=line_send.at[n],
            recv_sem=line_recv.at[source * pieces + piece],
            device_id={"sta": peer * QUAD + lead},
            device_id_type=MESH,
        )

    passed = []

    def pass_on(source, piece, ahead, there):
        copy = line_copy(source, piece, len(passed), rank + ahead)
        passed.append((copy, there))

        @pl.when(there)
        def _():
            copy.start()

    picks_sent = []

    def share(source, piece, samples):
        private[...] = samples.reshape(private.shape)
        plane = (source * QUAD + lead) * pieces + piece
        for k, peer in enumerate(others + (me,)):
            blocks = [pairing_ref[r, peer] for r in range(ROUNDS)] + [peer]
            slot = len(picks_sent)
            for g, block in enumerate(blocks):
                if k < len(others):
                    picked[slot, g * SB : (g + 1) * SB, :] = private[block]
                else:
                    out_ref[plane, g * SB : (g + 1) * SB, :] = private[block]
            if k < len(others):
                copy = pltpu.make_async_remote_copy(
                    src_ref=picked.at[slot],
                    dst_ref=out_ref.at[plane],
                    send_sem=pick_send.at[slot],
                    recv_sem=pick_recv.at[plane],
                    device_id={"sta": peer},
                    device_id_type=MESH,
                )
                copy.start()
                picks_sent.append(copy)

    def filtered(piece, first, spill=None):
        summed = lax.dot_general(
            raw[:, max(first, 0) : first + SPAN],
            banded[:, max(-first, 0) :],
            dims,
            preferred_element_type=jnp.float32,
        )
        if spill is not None:
            summed = summed + spill
        ordered = jnp.dot(picks, summed.astype(jnp.bfloat16), preferred_element_type=jnp.float32).astype(jnp.bfloat16)
        column[rank, piece] = ordered
        pass_on(rank, piece, 1, rank < line - 1)
        pass_on(rank, piece, -1, rank > 0)
        share(rank, piece, ordered)

    for piece in range(pieces - 1, 0, -1):
        filtered(piece, piece * LANE * DEC - TAPS)

    @pl.when(me > 0)
    def _():
        halo_copy.wait_recv()

    @pl.when(me == 0)
    def _():
        halo[...] = jnp.zeros_like(halo)

    spill = halo[...].astype(jnp.float32)
    spill = [jnp.where(lane < half, x, 0.0) for x in (spill, pltpu.roll(spill, half, 1))]
    filtered(0, -TAPS, jnp.concatenate(spill, axis=0))

    for source, piece in expected:
        from_below = source < rank
        line_copy(source, piece, 0, source).wait_recv()
        pass_on(
            source,
            piece,
            jnp.where(from_below, 1, -1),
            (from_below & (rank < line - 1)) | (jnp.logical_not(from_below) & (rank > 0)),
        )
        share(source, piece, column[source, piece])

    for source in range(line):
        for piece in range(pieces):
            for peer in others:
                plane = peer - rank * QUAD + source * QUAD
                plane = plane * pieces + piece
                pltpu.make_async_remote_copy(
                    src_ref=picked.at[0],
                    dst_ref=out_ref.at[plane],
                    send_sem=pick_send.at[0],
                    recv_sem=pick_recv.at[plane],
                    device_id={"sta": twin},
                    device_id_type=MESH,
                ).wait_recv()
    for copy in picks_sent:
        copy.wait_send()
    for copy, there in passed:

        @pl.when(there)
        def _():
            copy.wait_send()

    @pl.when(me < members - 1)
    def _():
        halo_copy.wait_send()


def correlate_kernel(
    starts_ref,
    low_ref,
    taper_ref,
    dft_hbm,
    lag_hbm,
    out_ref,
    dft_ref,
    lag_ref,
    ahead,
    back,
    theirs,
    own,
    white_own,
    left,
    right,
    cross_real,
    cross_imag,
    dft_sems,
    lag_sem,
):
    tile = pl.program_id(0)
    planes = low_ref.shape[0]
    window_count = starts_ref.shape[0]
    lane = lax.broadcasted_iota(jnp.int32, (1, LANE), 1)
    dft_copies = [
        pltpu.make_async_copy(
            dft_hbm.at[:, n * HT : (n + 1) * HT, :], dft_ref.at[:, n * HT : (n + 1) * HT, :], dft_sems.at[n]
        )
        for n in range(TILES)
    ]
    lag_copy = pltpu.make_async_copy(lag_hbm, lag_ref, lag_sem)

    @pl.when(tile == 0)
    def _():
        for copy in dft_copies:
            copy.start()
        lag_copy.start()
        mirror = (
            lax.broadcasted_iota(jnp.int32, (LANE, LANE), 0) + lax.broadcasted_iota(jnp.int32, (LANE, LANE), 1) == LANE
        ).astype(jnp.float32).astype(jnp.bfloat16)

        def one_plane(n, carry):
            samples = low_ref[n]
            ahead[n] = samples.astype(jnp.float32)
            turned = jnp.dot(samples, mirror, preferred_element_type=jnp.float32)
            later = low_ref[jnp.minimum(n + 1, planes - 1)].astype(jnp.float32)
            later = jnp.where(n + 1 < planes, later, jnp.zeros_like(later))
            back[planes - 1 - n] = jnp.where(lane == 0, later, turned)
            return carry

        lax.fori_loop(0, planes, one_plane, 0, unroll=8)

        def one_window(w, carry):
            start = starts_ref[w]
            plane, rest = start // LANE, start % LANE
            taper = taper_ref[...]
            fore = pltpu.roll(taper, rest, 1)
            hind = pltpu.roll(taper, (LANE - rest) % LANE, 1)
            span = SEG // LANE
            rise = [jnp.where(lane >= rest, fore[p + 1 : p + 2], fore[p : p + 1]) for p in range(FOLD // LANE + 1)]
            fall = [
                jnp.where(lane < LANE - rest, hind[p + 1 : p + 2], hind[p + 2 : p + 3]) for p in range(FOLD // LANE)
            ]
            at = pl.ds(pl.multiple_of(w * THEIRS, SB), THEIRS)
            own_at = pl.ds(pl.multiple_of(w * SB, SB), SB)

            def put(kind, p, values):
                values = values.astype(jnp.bfloat16)
                lanes = slice(p * LANE, (p + 1) * LANE)
                theirs[kind, at, lanes] = values[:THEIRS]
                own[kind, own_at, lanes] = values[THEIRS:]

            last = FOLD // LANE
            a = rise[last] * ahead[plane + last]
            b = (1.0 - rise[last]) * ahead[plane + last + span // 2]
            put(0, last, a + b)
            middle = a - b
            for p in range(FOLD // LANE):
                first = ahead[plane + p]
                if p == 0:
                    first = jnp.where(lane < rest, ahead[jnp.minimum(plane + span, planes - 1)], first)
                a = rise[p] * first
                b = (1.0 - rise[p]) * ahead[plane + span // 2 + p]
                c = fall[p] * back[planes - plane - span + p]
                d = (1.0 - fall[p]) * back[planes - plane - span // 2 + p]
                same, apart = a + b, a - b
                same_turned, apart_turned = d + c, d - c
                put(0, p, same + same_turned)
                put(1, p, apart - apart_turned)
                put(2, p, same - same_turned)
                summed = apart + apart_turned
                put(3, p, jnp.where(lane == 0, middle, summed) if p == 0 else summed)
            return carry

        lax.fori_loop(0, window_count, one_window, 0, unroll=2)

    for n, copy in enumerate(dft_copies):

        @pl.when(tile == n)
        def _():
            copy.wait()

    def dot_nt(a, b):
        return lax.dot_general(a, b, NT, preferred_element_type=jnp.float32)

    bins = pl.ds(pl.multiple_of(tile * HT, HT), HT)
    depth = (FOLD + LANE, FOLD, FOLD, FOLD)
    half = LANE // 2
    wide = 2 * LANE
    first = lane < half
    slots = LANE // PACK
    turns = slots // 2
    strip = BAND // 2
    halves = HT // PACK
    for tile_pair in range(window_count * THEIRS // wide):
        at = slice(tile_pair * wide, (tile_pair + 1) * wide)
        spectra = [dot_nt(dft_ref[k, bins, : depth[k]], theirs[k, at, : depth[k]]) for k in range(4)]
        for n in range(HT // strip):
            for inner in range(wide // LANE):
                parts = [x[n * strip : (n + 1) * strip, inner * LANE : (inner + 1) * LANE] for x in spectra]
                power = sum(x * x for x in parts[1:]) + parts[0] * parts[0]
                level = jnp.sum(power, axis=0, keepdims=True)
                scale = lax.rsqrt(level * (1.0 / (2 * BAND)) + 1e-06)
                for parity in range(2):
                    real, imag = parts[parity] * scale, parts[2 + parity] * scale

                    def stacked(x, y):
                        both = [v.reshape(strip // PACK, 1, PACK, LANE) for v in (x, y)]
                        both = jnp.concatenate(both, axis=1).reshape(strip * 2, LANE)
                        return both.astype(jnp.bfloat16)

                    plain, crossed = stacked(real, imag), stacked(-imag, real)
                    turned = pltpu.roll(jnp.where(first, crossed, plain), half, 1)
                    for k, block in enumerate((jnp.where(first, plain, turned), jnp.where(first, turned, crossed))):
                        w = (tile_pair * (wide // LANE) + inner) * 2 + k
                        for m in range(strip // PACK):
                            group = n * (strip // PACK) + m
                            turn = group % slots // 2
                            row = w // turns * LANE + (w + turn) % turns * 2 * PACK
                            right[parity * halves + group, row : row + 2 * PACK, :] = block[
                                m * 2 * PACK : (m + 1) * 2 * PACK
                            ]

    spectra = [dot_nt(own[k, :, : depth[k]], dft_ref[k, bins, : depth[k]]) for k in range(4)]
    power = sum(x * x for x in spectra[1:]) + spectra[0] * spectra[0]
    same = (
        lax.broadcasted_iota(jnp.int32, (HT, HT), 0) // strip == lax.broadcasted_iota(jnp.int32, (HT, HT), 1) // strip
    ).astype(jnp.float32).astype(jnp.bfloat16)
    level = jnp.dot(power.astype(jnp.bfloat16), same, preferred_element_type=jnp.float32)
    scale = lax.rsqrt(level * (1.0 / (2 * BAND)) + 1e-06)
    for k in range(4):
        white_own[k] = (spectra[k] * scale).astype(jnp.bfloat16)

    low_slot = lane // PACK % 2 == 0
    for parity in range(2):
        for part in range(HT // LANE):
            for h in range(window_count // turns):
                moved = [[], []]
                for w in range(turns):
                    row = (h * turns + w) * SB
                    x = [
                        white_own[2 * c + parity, row : row + SB, part * LANE : (part + 1) * LANE] for c in range(2)
                    ]
                    y = (
                        jnp.where(low_slot, x[0], pltpu.roll(x[1], PACK, 1)),
                        jnp.where(low_slot, pltpu.roll(x[0], LANE - PACK, 1), x[1]),
                    )
                    for k in range(2):
                        moved[k].append(pltpu.roll(y[k], 2 * PACK * w, 1) if w else y[k])
                for slot in range(slots):
                    turn, k = slot // 2, slot % 2
                    joined = moved[k][0]
                    for w in range(1, turns):
                        joined = jnp.where(lane // (2 * PACK) == (turn + w) % turns, moved[k][w], joined)
                    left[parity * halves + part * slots + slot, h] = joined

    own_bin = lax.broadcasted_iota(jnp.int32, (PACK * SB, LANE), 0) // SB
    mask = (own_bin == lax.broadcasted_iota(jnp.int32, (PACK * SB, LANE), 1) % PACK).astype(jnp.float32).astype(
        jnp.bfloat16
    )

    def one_group(n, carry):
        masked = jnp.concatenate([jnp.concatenate([left[n, h]] * PACK, axis=0) * mask for h in range(2)], axis=1)
        product = jnp.dot(masked, right[n], preferred_element_type=jnp.float32)
        product = product.reshape(PACK, 2, SB // 2, LANE)
        a, b = product[:, 0].reshape(PACK * SB // 2, LANE), product[:, 1].reshape(PACK * SB // 2, LANE)
        turned = pltpu.roll(jnp.where(first, b, a), half, 1)
        at = pl.ds(pl.multiple_of((tile * (FT // PACK) + n) * PACK * SB // 2, PACK * SB // 2), PACK * SB // 2)
        cross_real[at, :] = jnp.where(first, a, turned)
        cross_imag[at, :] = jnp.where(first, turned, b)
        return carry

    lax.fori_loop(0, FT // PACK, one_group, 0, unroll=16)

    @pl.when(tile == pl.num_programs(0) - 1)
    def _():
        lag_copy.wait()

        def two_stations(n, carry):
            summed = None
            for k, cross in enumerate((cross_real, cross_imag)):
                columns = jnp.concatenate(
                    [cross[pl.ds(2 * n + m, BINS, stride=SB // 2), :].astype(jnp.bfloat16) for m in range(2)], axis=1
                )
                term = jnp.dot(lag_ref[k], columns, preferred_element_type=jnp.float32)
                summed = term if summed is None else summed + term
            turned = summed.T
            for m in range(2):
                for h in range(2):
                    i = h * (SB // 2) + 2 * n + m
                    for r in range(ROUNDS):
                        row = ((m * 2 + h) * ROUNDS + r) * SB
                        out_ref[r, pl.ds(pl.multiple_of(i * SB, SB), SB), :] = turned[row : row + SB]
            return carry

        lax.fori_loop(0, SB // 4, two_stations, 0, unroll=True)


def correlate(window_starts, low, taper, dft, lag):
    window_count = window_starts.shape[0]
    planes = low.shape[0]
    grid_spec = pltpu.PrefetchScalarGridSpec(
        num_scalar_prefetch=1,
        grid=(TILES,),
        in_specs=[
            pl.BlockSpec((planes, ROWS, LANE), lambda n, *_: (0, 0, 0)),
            pl.BlockSpec((8, LANE), lambda n, *_: (0, 0)),
            pl.BlockSpec(memory_space=pl.ANY),
            pl.BlockSpec(memory_space=pl.ANY),
        ],
        out_specs=pl.BlockSpec((ROUNDS, SB * SB, LAGS), lambda n, *_: (0, 0, 0)),
        scratch_shapes=[
            pltpu.VMEM(dft.shape, jnp.bfloat16),
            pltpu.VMEM(lag.shape, jnp.bfloat16),
            pltpu.VMEM((planes, ROWS, LANE), jnp.float32),
            pltpu.VMEM((planes, ROWS, LANE), jnp.float32),
            pltpu.VMEM((4, window_count * THEIRS, FOLD + LANE), jnp.bfloat16),
            pltpu.VMEM((4, window_count * SB, FOLD + LANE), jnp.bfloat16),
            pltpu.VMEM((4, window_count * SB, HT), jnp.bfloat16),
            pltpu.VMEM((FT // PACK, 2, SB, LANE), jnp.bfloat16),
            pltpu.VMEM((FT // PACK, 2 * LANE, LANE), jnp.bfloat16),
            pltpu.VMEM((BINS * SB // 2, LANE), jnp.float32),
            pltpu.VMEM((BINS * SB // 2, LANE), jnp.float32),
            pltpu.SemaphoreType.DMA((TILES,)),
            pltpu.SemaphoreType.DMA,
        ],
    )
    return pl.pallas_call(
        correlate_kernel,
        grid_spec=grid_spec,
        out_shape=jax.ShapeDtypeStruct((ROUNDS, SB * SB, LAGS), jnp.float32),
        compiler_params=pltpu.CompilerParams(vmem_limit_bytes=60 * 2**20),
    )(window_starts, low, taper, dft, lag)


def body(raw_traces, filter_taps, station_order, window_starts, pairing):
    members = lax.axis_size("sta")
    stations, local_time = raw_traces.shape
    window_count = window_starts.shape[0]
    pieces = local_time // (LANE * DEC)
    line = members // QUAD
    in_vmem = pl.BlockSpec(memory_space=pltpu.VMEM)
    low = pl.pallas_call(
        functools.partial(gather_kernel, members),
        out_shape=jax.ShapeDtypeStruct((members * pieces, ROWS, LANE), jnp.bfloat16),
        in_specs=[
            pl.BlockSpec(memory_space=pl.ANY),
            in_vmem,
            in_vmem,
            pl.BlockSpec(memory_space=pltpu.SMEM),
        ],
        out_specs=in_vmem,
        scratch_shapes=[
            pltpu.VMEM((stations, local_time), jnp.bfloat16),
            pltpu.VMEM((stations // 2, LANE), jnp.bfloat16),
            pltpu.VMEM((stations // 2, LANE), jnp.bfloat16),
            pltpu.VMEM((line, pieces, stations, LANE), jnp.bfloat16),
            pltpu.VMEM((stations // SB, SB, LANE), jnp.bfloat16),
            pltpu.VMEM((3 * line * pieces, ROWS, LANE), jnp.bfloat16),
            pltpu.SemaphoreType.DMA,
            pltpu.SemaphoreType.DMA((2,)),
            pltpu.SemaphoreType.DMA(((line + 1) * pieces,)),
            pltpu.SemaphoreType.DMA((line * pieces,)),
            pltpu.SemaphoreType.DMA((3 * line * pieces,)),
            pltpu.SemaphoreType.DMA((members * pieces,)),
        ],
        compiler_params=pltpu.CompilerParams(
            collective_id=0, has_side_effects=True, vmem_limit_bytes=60 * 2**20
        ),
    )(raw_traces, filter_taps, station_order.reshape(1, stations), pairing)
    correlated = correlate(
        window_starts,
        low,
        jnp.asarray(taper_table()),
        jnp.asarray(dft_table()),
        jnp.asarray(lag_table(window_count)),
    )
    return correlated.reshape(ROUNDS, SB, SB, LAGS)


def solution(mesh):
    return jax.shard_map(
        body,
        mesh=mesh,
        in_specs=(P("parts", "sta"), P(), P("parts"), P("parts"), P()),
        out_specs=P(None, ("parts", "sta"), None, None),
        check_vma=False,
    )
```

```python
import functools
import math

import jax
import jax.numpy as jnp
import ml_dtypes
import numpy as np
from jax import lax
from jax.experimental import pallas as pl
from jax.experimental.pallas import tpu as pltpu
from jax.sharding import PartitionSpec as P

SB = 16
DEC = 4
TAPS = 256
SEG = 2048
BAND = 64
LAGS = 256
ROUNDS = 4
BINS = 1024
LANE = 128
SPAN = LANE * DEC + TAPS
GROUPS = ROUNDS + 1
ROWS = GROUPS * SB
THEIRS = ROUNDS * SB
FOLD = SEG // 4
FT = 512
HT = FT // 2
TILES = BINS // FT
PACK = 8
NT = (((1,), (1,)), ((), ()))
QUAD = 4
MESH = pl.DeviceIdType.MESH


def taper_table():
    sample = np.arange(-LANE, 7 * LANE)
    return (0.5 - 0.5 * np.cos(sample * (2.0 * math.pi / SEG))).astype(np.float32).reshape(8, LANE)


def dft_table():
    sample = np.arange(FOLD)
    kinds = []
    for wave in (np.cos, lambda a: -np.sin(a)):
        for parity in range(2):
            frequency = 2 * np.arange(BINS // 2) + parity
            table = np.zeros((BINS // 2, FOLD + LANE))
            table[:, :FOLD] = wave((sample[None, :] * frequency[:, None] % SEG) * (2.0 * math.pi / SEG))
            middle = np.round(wave((frequency * FOLD % SEG) * (2.0 * math.pi / SEG)))
            if wave is np.cos:
                table[:, 0] = 0.5
                table[:, FOLD] = middle
            else:
                table[:, 0] = middle
            kinds.append(table)
    return np.stack(kinds).astype(np.float32).astype(ml_dtypes.bfloat16)


def lag_table(window_count):
    frequency = 2 * np.arange(BINS // 2).reshape(TILES, 1, HT) + np.arange(2).reshape(1, 2, 1)
    frequency = frequency.reshape(BINS)
    offset = np.arange(LAGS) - LAGS // 2 + SEG
    angles = (frequency[None, :] * offset[:, None] % SEG) * (2.0 * math.pi / SEG)
    scale = 1.0 / math.sqrt(BINS * window_count)
    both = np.stack([np.cos(angles) * scale, -np.sin(angles) * scale])
    return both.astype(np.float32).astype(ml_dtypes.bfloat16)


def gather_kernel(
    members,
    raw_ref,
    taps_ref,
    order_ref,
    pairing_ref,
    out_ref,
    raw,
    tail,
    halo,
    column,
    private,
    picked,
    raw_sem,
    halo_sems,
    line_send,
    line_recv,
    pick_send,
    pick_recv,
):
    me = lax.axis_index("sta")
    stations, local_time = raw_ref.shape
    line, pieces = column.shape[:2]
    rank, lead = me // QUAD, me % QUAD
    turn = 1 - 2 * lax.rem(me, 2)
    twin = me + turn
    across = rank * QUAD + lax.rem(lead + 2, QUAD)
    others = (across, across + turn, twin)
    after, before = lax.rem(me + 1, members), lax.rem(me + members - 1, members)

    def of_rank(choose):
        chosen = choose(0)
        for r in range(1, line):
            chosen = jnp.where(rank == r, choose(r), chosen)
        return chosen

    def arrivals(r):
        known = sorted((abs(x - r), -piece, x) for x in range(line) if x != r for piece in range(pieces))
        return [(x, -negative) for _, negative, x in known]

    expected = [
        (of_rank(lambda r: arrivals(r)[n][0]), of_rank(lambda r: arrivals(r)[n][1]))
        for n in range((line - 1) * pieces)
    ]

    raw_copy = pltpu.make_async_copy(raw_ref, raw, raw_sem)
    raw_copy.start()

    barrier = pltpu.get_barrier_semaphore()
    greeted = [lax.rem(rank + n, line) * QUAD + lead for n in range(1, line)] + list(others) + [after, before]
    for peer in greeted:
        pl.semaphore_signal(barrier, inc=1, device_id={"sta": peer}, device_id_type=MESH)

    mirror = (
        lax.broadcasted_iota(jnp.int32, (TAPS, TAPS), 0) + lax.broadcasted_iota(jnp.int32, (TAPS, TAPS), 1) == TAPS - 1
    ).astype(jnp.float32).astype(jnp.bfloat16)
    taps = jnp.broadcast_to(taps_ref[...].astype(jnp.float32).reshape(1, TAPS), (SB, TAPS)).astype(jnp.bfloat16)
    taps = jnp.dot(taps, mirror, preferred_element_type=jnp.float32)[:1]
    banded = jnp.concatenate([taps, jnp.zeros((1, SPAN - TAPS), jnp.float32)], axis=1)
    banded = jnp.broadcast_to(banded, (LANE, SPAN))
    banded = pltpu.roll(banded, DEC, 1, stride=DEC, stride_axis=0).astype(jnp.bfloat16)
    picks = (lax.broadcasted_iota(jnp.int32, (stations, stations), 0) == order_ref[...]).astype(jnp.float32)
    picks = picks.T.astype(jnp.bfloat16)

    dims = (((1,), (1,)), ((), ()))
    lane = lax.broadcasted_iota(jnp.int32, (1, LANE), 1)
    half = LANE // 2
    raw_copy.wait()
    spilled = lax.dot_general(
        raw[:, local_time - TAPS :], banded[:, :TAPS], dims, preferred_element_type=jnp.float32
    )
    tail[...] = jnp.where(
        lane < half, spilled[: stations // 2], pltpu.roll(spilled[stations // 2 :], half, 1)
    ).astype(jnp.bfloat16)

    pl.semaphore_wait(barrier, len(greeted))

    halo_copy = pltpu.make_async_remote_copy(
        src_ref=tail,
        dst_ref=halo,
        send_sem=halo_sems.at[0],
        recv_sem=halo_sems.at[1],
        device_id={"sta": after},
        device_id_type=MESH,
    )

    @pl.when(me < members - 1)
    def _():
        halo_copy.start()

    def line_copy(source, piece, n, peer):
        return pltpu.make_async_remote_copy(
            src_ref=column.at[source, piece],
            dst_ref=column.at[source, piece],
            send_sem=line_send.at[n],
            recv_sem=line_recv.at[source * pieces + piece],
            device_id={"sta": peer * QUAD + lead},
            device_id_type=MESH,
        )

    passed = []

    def pass_on(source, piece, ahead, there):
        copy = line_copy(source, piece, len(passed), rank + ahead)
        passed.append((copy, there))

        @pl.when(there)
        def _():
            copy.start()

    picks_sent = []

    def share(source, piece, samples):
        private[...] = samples.reshape(private.shape)
        plane = (source * QUAD + lead) * pieces + piece
        for k, peer in enumerate(others + (me,)):
            blocks = [pairing_ref[r, peer] for r in range(ROUNDS)] + [peer]
            slot = len(picks_sent)
            for g, block in enumerate(blocks):
                if k < len(others):
                    picked[slot, g * SB : (g + 1) * SB, :] = private[block]
                else:
                    out_ref[plane, g * SB : (g + 1) * SB, :] = private[block]
            if k < len(others):
                copy = pltpu.make_async_remote_copy(
                    src_ref=picked.at[slot],
                    dst_ref=out_ref.at[plane],
                    send_sem=pick_send.at[slot],
                    recv_sem=pick_recv.at[plane],
                    device_id={"sta": peer},
                    device_id_type=MESH,
                )
                copy.start()
                picks_sent.append(copy)

    def filtered(piece, first, spill=None):
        summed = lax.dot_general(
            raw[:, max(first, 0) : first + SPAN],
            banded[:, max(-first, 0) :],
            dims,
            preferred_element_type=jnp.float32,
        )
        if spill is not None:
            summed = summed + spill
        ordered = jnp.dot(picks, summed.astype(jnp.bfloat16), preferred_element_type=jnp.float32).astype(jnp.bfloat16)
        column[rank, piece] = ordered
        pass_on(rank, piece, 1, rank < line - 1)
        pass_on(rank, piece, -1, rank > 0)
        share(rank, piece, ordered)

    for piece in range(pieces - 1, 0, -1):
        filtered(piece, piece * LANE * DEC - TAPS)

    @pl.when(me > 0)
    def _():
        halo_copy.wait_recv()

    @pl.when(me == 0)
    def _():
        halo[...] = jnp.zeros_like(halo)

    spill = halo[...].astype(jnp.float32)
    spill = [jnp.where(lane < half, x, 0.0) for x in (spill, pltpu.roll(spill, half, 1))]
    filtered(0, -TAPS, jnp.concatenate(spill, axis=0))

    for source, piece in expected:
        from_below = source < rank
        line_copy(source, piece, 0, source).wait_recv()
        pass_on(
            source,
            piece,
            jnp.where(from_below, 1, -1),
            (from_below & (rank < line - 1)) | (jnp.logical_not(from_below) & (rank > 0)),
        )
        share(source, piece, column[source, piece])

    for source in range(line):
        for piece in range(pieces):
            for peer in others:
                plane = peer - rank * QUAD + source * QUAD
                plane = plane * pieces + piece
                pltpu.make_async_remote_copy(
                    src_ref=picked.at[0],
                    dst_ref=out_ref.at[plane],
                    send_sem=pick_send.at[0],
                    recv_sem=pick_recv.at[plane],
                    device_id={"sta": twin},
                    device_id_type=MESH,
                ).wait_recv()
    for copy in picks_sent:
        copy.wait_send()
    for copy, there in passed:

        @pl.when(there)
        def _():
            copy.wait_send()

    @pl.when(me < members - 1)
    def _():
        halo_copy.wait_send()


def correlate_kernel(
    starts_ref,
    low_ref,
    taper_ref,
    dft_hbm,
    lag_hbm,
    out_hbm,
    out_ref,
    dft_ref,
    lag_ref,
    ahead,
    back,
    theirs,
    own,
    white_own,
    left,
    right,
    cross_real,
    cross_imag,
    dft_sems,
    lag_sem,
    out_sems,
):
    planes = low_ref.shape[0]
    window_count = starts_ref.shape[0]
    lane = lax.broadcasted_iota(jnp.int32, (1, LANE), 1)
    dft_copies = [
        pltpu.make_async_copy(
            dft_hbm.at[:, n * HT : (n + 1) * HT, :], dft_ref.at[:, n * HT : (n + 1) * HT, :], dft_sems.at[n]
        )
        for n in range(TILES)
    ]
    lag_copy = pltpu.make_async_copy(lag_hbm, lag_ref, lag_sem)

    for copy in dft_copies:
        copy.start()
    lag_copy.start()
    mirror = (
        lax.broadcasted_iota(jnp.int32, (LANE, LANE), 0) + lax.broadcasted_iota(jnp.int32, (LANE, LANE), 1) == LANE
    ).astype(jnp.float32).astype(jnp.bfloat16)

    def one_plane(n, carry):
        samples = low_ref[n]
        ahead[n] = samples.astype(jnp.float32)
        turned = jnp.dot(samples, mirror, preferred_element_type=jnp.float32)
        later = low_ref[jnp.minimum(n + 1, planes - 1)].astype(jnp.float32)
        later = jnp.where(n + 1 < planes, later, jnp.zeros_like(later))
        back[planes - 1 - n] = jnp.where(lane == 0, later, turned)
        return carry

    lax.fori_loop(0, planes, one_plane, 0, unroll=16)

    def one_window(w, carry):
        start = starts_ref[w]
        plane, rest = start // LANE, start % LANE
        taper = taper_ref[...]
        fore = pltpu.roll(taper, rest, 1)
        hind = pltpu.roll(taper, (LANE - rest) % LANE, 1)
        span = SEG // LANE
        rise = [jnp.where(lane >= rest, fore[p + 1 : p + 2], fore[p : p + 1]) for p in range(FOLD // LANE + 1)]
        fall = [
            jnp.where(lane < LANE - rest, hind[p + 1 : p + 2], hind[p + 2 : p + 3]) for p in range(FOLD // LANE)
        ]
        at = pl.ds(pl.multiple_of(w * THEIRS, SB), THEIRS)
        own_at = pl.ds(pl.multiple_of(w * SB, SB), SB)

        def put(kind, p, values):
            values = values.astype(jnp.bfloat16)
            lanes = slice(p * LANE, (p + 1) * LANE)
            theirs[kind, at, lanes] = values[:THEIRS]
            own[kind, own_at, lanes] = values[THEIRS:]

        last = FOLD // LANE
        a = rise[last] * ahead[plane + last]
        b = (1.0 - rise[last]) * ahead[plane + last + span // 2]
        put(0, last, a + b)
        middle = a - b
        for p in range(FOLD // LANE):
            first = ahead[plane + p]
            if p == 0:
                first = jnp.where(lane < rest, ahead[jnp.minimum(plane + span, planes - 1)], first)
            a = rise[p] * first
            b = (1.0 - rise[p]) * ahead[plane + span // 2 + p]
            c = fall[p] * back[planes - plane - span + p]
            d = (1.0 - fall[p]) * back[planes - plane - span // 2 + p]
            same, apart = a + b, a - b
            same_turned, apart_turned = d + c, d - c
            put(0, p, same + same_turned)
            put(1, p, apart - apart_turned)
            put(2, p, same - same_turned)
            summed = apart + apart_turned
            put(3, p, jnp.where(lane == 0, middle, summed) if p == 0 else summed)
        return carry

    lax.fori_loop(0, window_count, one_window, 0, unroll=8)

    def dot_nt(a, b):
        return lax.dot_general(a, b, NT, preferred_element_type=jnp.float32)

    depth = (FOLD + LANE, FOLD, FOLD, FOLD)
    half = LANE // 2
    wide = 2 * LANE
    first = lane < half
    slots = LANE // PACK
    turns = slots // 2
    strip = BAND // 2
    halves = HT // PACK
    own_bin = lax.broadcasted_iota(jnp.int32, (PACK * SB, LANE), 0) // SB
    mask = (own_bin == lax.broadcasted_iota(jnp.int32, (PACK * SB, LANE), 1) % PACK).astype(jnp.float32).astype(
        jnp.bfloat16
    )

    def one_group(tile, n):
        masked = jnp.concatenate([jnp.concatenate([left[tile, n, h]] * PACK, axis=0) * mask for h in range(2)], axis=1)
        product = jnp.dot(masked, right[tile, n], preferred_element_type=jnp.float32)
        product = product.reshape(PACK, 2, SB // 2, LANE)
        a, b = product[:, 0].reshape(PACK * SB // 2, LANE), product[:, 1].reshape(PACK * SB // 2, LANE)
        turned = pltpu.roll(jnp.where(first, b, a), half, 1)
        row = (tile * (FT // PACK) + n) * PACK * SB // 2
        at = pl.ds(row if isinstance(n, int) else pl.multiple_of(row, PACK * SB // 2), PACK * SB // 2)
        cross_real[at, :] = jnp.where(first, a, turned)
        cross_imag[at, :] = jnp.where(first, turned, b)

    def transforms(tile):
        dft_copies[tile].wait()
        bins = slice(tile * HT, (tile + 1) * HT)
        for tile_pair in range(window_count * THEIRS // wide):
            at = slice(tile_pair * wide, (tile_pair + 1) * wide)
            spectra = [dot_nt(dft_ref[k, bins, : depth[k]], theirs[k, at, : depth[k]]) for k in range(4)]
            for n in range(HT // strip):
                for inner in range(wide // LANE):
                    parts = [x[n * strip : (n + 1) * strip, inner * LANE : (inner + 1) * LANE] for x in spectra]
                    power = sum(x * x for x in parts[1:]) + parts[0] * parts[0]
                    level = jnp.sum(power, axis=0, keepdims=True)
                    scale = lax.rsqrt(level * (1.0 / (2 * BAND)) + 1e-06)
                    for parity in range(2):
                        real, imag = parts[parity] * scale, parts[2 + parity] * scale

                        def stacked(x, y):
                            both = [v.reshape(strip // PACK, 1, PACK, LANE) for v in (x, y)]
                            both = jnp.concatenate(both, axis=1).reshape(strip * 2, LANE)
                            return both.astype(jnp.bfloat16)

                        plain, crossed = stacked(real, imag), stacked(-imag, real)
                        turned = pltpu.roll(jnp.where(first, crossed, plain), half, 1)
                        for k, block in enumerate((jnp.where(first, plain, turned), jnp.where(first, turned, crossed))):
                            w = (tile_pair * (wide // LANE) + inner) * 2 + k
                            for m in range(strip // PACK):
                                group = n * (strip // PACK) + m
                                turn = group % slots // 2
                                row = w // turns * LANE + (w + turn) % turns * 2 * PACK
                                right[tile, parity * halves + group, row : row + 2 * PACK, :] = block[
                                    m * 2 * PACK : (m + 1) * 2 * PACK
                                ]

        spectra = [dot_nt(own[k, :, : depth[k]], dft_ref[k, bins, : depth[k]]) for k in range(4)]
        power = sum(x * x for x in spectra[1:]) + spectra[0] * spectra[0]
        same = (
            lax.broadcasted_iota(jnp.int32, (HT, HT), 0) // strip == lax.broadcasted_iota(jnp.int32, (HT, HT), 1) // strip
        ).astype(jnp.float32).astype(jnp.bfloat16)
        level = jnp.dot(power.astype(jnp.bfloat16), same, preferred_element_type=jnp.float32)
        scale = lax.rsqrt(level * (1.0 / (2 * BAND)) + 1e-06)
        for k in range(4):
            white_own[tile, k] = (spectra[k] * scale).astype(jnp.bfloat16)

        low_slot = lane // PACK % 2 == 0
        for parity in range(2):
            for part in range(HT // LANE):
                for h in range(window_count // turns):
                    moved = [[], []]
                    for w in range(turns):
                        row = (h * turns + w) * SB
                        x = [
                            white_own[tile, 2 * c + parity, row : row + SB, part * LANE : (part + 1) * LANE] for c in range(2)
                        ]
                        y = (
                            jnp.where(low_slot, x[0], pltpu.roll(x[1], PACK, 1)),
                            jnp.where(low_slot, pltpu.roll(x[0], LANE - PACK, 1), x[1]),
                        )
                        for k in range(2):
                            moved[k].append(pltpu.roll(y[k], 2 * PACK * w, 1) if w else y[k])
                    for slot in range(slots):
                        turn, k = slot // 2, slot % 2
                        joined = moved[k][0]
                        for w in range(1, turns):
                            joined = jnp.where(lane // (2 * PACK) == (turn + w) % turns, moved[k][w], joined)
                        left[tile, parity * halves + part * slots + slot, h] = joined

    def products(tile):
        def several(n, carry):
            one_group(tile, n)
            return carry

        lax.fori_loop(0, FT // PACK, several, 0, unroll=32)

    for tile in range(TILES):
        transforms(tile)
        if tile:
            products(tile - 1)
    products(TILES - 1)

    lag_copy.wait()
    out_copies = []
    for n in range(SB // 4):
        summed = None
        for k, cross in enumerate((cross_real, cross_imag)):
            columns = jnp.concatenate(
                [cross[pl.ds(2 * n + m, BINS, stride=SB // 2), :].astype(jnp.bfloat16) for m in range(2)], axis=1
            )
            term = jnp.dot(lag_ref[k], columns, preferred_element_type=jnp.float32)
            summed = term if summed is None else summed + term
        turned = summed.T
        for h in range(2):
            station = h * (SB // 2) + 2 * n
            for m in range(2):
                for r in range(ROUNDS):
                    row = ((m * 2 + h) * ROUNDS + r) * SB
                    out_ref[r, (station + m) * SB : (station + m + 1) * SB, :] = turned[row : row + SB]
            rows = slice(station * SB, (station + 2) * SB)
            copy = pltpu.make_async_copy(
                out_ref.at[:, rows, :], out_hbm.at[:, rows, :], out_sems.at[len(out_copies)]
            )
            copy.start()
            out_copies.append(copy)
    for copy in out_copies:
        copy.wait()


def correlate(window_starts, low, taper, dft, lag):
    window_count = window_starts.shape[0]
    planes = low.shape[0]
    in_vmem = pl.BlockSpec(memory_space=pltpu.VMEM)
    anywhere = pl.BlockSpec(memory_space=pl.ANY)
    return pl.pallas_call(
        correlate_kernel,
        in_specs=[pl.BlockSpec(memory_space=pltpu.SMEM), in_vmem, in_vmem, anywhere, anywhere],
        out_specs=anywhere,
        out_shape=jax.ShapeDtypeStruct((ROUNDS, SB * SB, LAGS), jnp.float32),
        scratch_shapes=[
            pltpu.VMEM((ROUNDS, SB * SB, LAGS), jnp.float32),
            pltpu.VMEM(dft.shape, jnp.bfloat16),
            pltpu.VMEM(lag.shape, jnp.bfloat16),
            pltpu.VMEM((planes, ROWS, LANE), jnp.float32),
            pltpu.VMEM((planes, ROWS, LANE), jnp.float32),
            pltpu.VMEM((4, window_count * THEIRS, FOLD + LANE), jnp.bfloat16),
            pltpu.VMEM((4, window_count * SB, FOLD + LANE), jnp.bfloat16),
            pltpu.VMEM((TILES, 4, window_count * SB, HT), jnp.bfloat16),
            pltpu.VMEM((TILES, FT // PACK, 2, SB, LANE), jnp.bfloat16),
            pltpu.VMEM((TILES, FT // PACK, 2 * LANE, LANE), jnp.bfloat16),
            pltpu.VMEM((BINS * SB // 2, LANE), jnp.float32),
            pltpu.VMEM((BINS * SB // 2, LANE), jnp.float32),
            pltpu.SemaphoreType.DMA((TILES,)),
            pltpu.SemaphoreType.DMA,
            pltpu.SemaphoreType.DMA((SB // 2,)),
        ],
        compiler_params=pltpu.CompilerParams(vmem_limit_bytes=60 * 2**20),
    )(window_starts, low, taper, dft, lag)


def body(raw_traces, filter_taps, station_order, window_starts, pairing):
    members = lax.axis_size("sta")
    stations, local_time = raw_traces.shape
    window_count = window_starts.shape[0]
    pieces = local_time // (LANE * DEC)
    line = members // QUAD
    in_vmem = pl.BlockSpec(memory_space=pltpu.VMEM)
    low = pl.pallas_call(
        functools.partial(gather_kernel, members),
        out_shape=jax.ShapeDtypeStruct((members * pieces, ROWS, LANE), jnp.bfloat16),
        in_specs=[
            pl.BlockSpec(memory_space=pl.ANY),
            in_vmem,
            in_vmem,
            pl.BlockSpec(memory_space=pltpu.SMEM),
        ],
        out_specs=in_vmem,
        scratch_shapes=[
            pltpu.VMEM((stations, local_time), jnp.bfloat16),
            pltpu.VMEM((stations // 2, LANE), jnp.bfloat16),
            pltpu.VMEM((stations // 2, LANE), jnp.bfloat16),
            pltpu.VMEM((line, pieces, stations, LANE), jnp.bfloat16),
            pltpu.VMEM((stations // SB, SB, LANE), jnp.bfloat16),
            pltpu.VMEM((3 * line * pieces, ROWS, LANE), jnp.bfloat16),
            pltpu.SemaphoreType.DMA,
            pltpu.SemaphoreType.DMA((2,)),
            pltpu.SemaphoreType.DMA(((line + 1) * pieces,)),
            pltpu.SemaphoreType.DMA((line * pieces,)),
            pltpu.SemaphoreType.DMA((3 * line * pieces,)),
            pltpu.SemaphoreType.DMA((members * pieces,)),
        ],
        compiler_params=pltpu.CompilerParams(
            collective_id=0, has_side_effects=True, vmem_limit_bytes=60 * 2**20
        ),
    )(raw_traces, filter_taps, station_order.reshape(1, stations), pairing)
    correlated = correlate(
        window_starts,
        low,
        jnp.asarray(taper_table()),
        jnp.asarray(dft_table()),
        jnp.asarray(lag_table(window_count)),
    )
    return correlated.reshape(ROUNDS, SB, SB, LAGS)


def solution(mesh):
    return jax.shard_map(
        body,
        mesh=mesh,
        in_specs=(P("parts", "sta"), P(), P("parts"), P("parts"), P()),
        out_specs=P(None, ("parts", "sta"), None, None),
        check_vma=False,
    )
```

```python
import functools
import math

import jax
import jax.numpy as jnp
import ml_dtypes
import numpy as np
from jax import lax
from jax.experimental import pallas as pl
from jax.experimental.pallas import tpu as pltpu
from jax.sharding import PartitionSpec as P

SB = 16
DEC = 4
TAPS = 256
SEG = 2048
BAND = 64
LAGS = 256
ROUNDS = 4
BINS = 1024
LANE = 128
SPAN = LANE * DEC + TAPS
GROUPS = ROUNDS + 1
ROWS = GROUPS * SB
THEIRS = ROUNDS * SB
FOLD = SEG // 4
FT = 512
HT = FT // 2
TILES = BINS // FT
PACK = 8
NT = (((1,), (1,)), ((), ()))
QUAD = 4
MESH = pl.DeviceIdType.MESH


def taper_table():
    sample = np.arange(-LANE, 7 * LANE)
    return (0.5 - 0.5 * np.cos(sample * (2.0 * math.pi / SEG))).astype(np.float32).reshape(8, LANE)


def dft_table():
    sample = np.arange(FOLD)
    kinds = []
    for wave in (np.cos, lambda a: -np.sin(a)):
        for parity in range(2):
            frequency = 2 * np.arange(BINS // 2) + parity
            table = np.zeros((BINS // 2, FOLD + LANE))
            table[:, :FOLD] = wave((sample[None, :] * frequency[:, None] % SEG) * (2.0 * math.pi / SEG))
            middle = np.round(wave((frequency * FOLD % SEG) * (2.0 * math.pi / SEG)))
            if wave is np.cos:
                table[:, 0] = 0.5
                table[:, FOLD] = middle
            else:
                table[:, 0] = middle
            kinds.append(table)
    return np.stack(kinds).astype(np.float32).astype(ml_dtypes.bfloat16)


def lag_table(window_count):
    frequency = 2 * np.arange(BINS // 2).reshape(TILES, 1, HT) + np.arange(2).reshape(1, 2, 1)
    frequency = frequency.reshape(BINS)
    offset = np.arange(LAGS) - LAGS // 2 + SEG
    angles = (frequency[None, :] * offset[:, None] % SEG) * (2.0 * math.pi / SEG)
    scale = 1.0 / math.sqrt(BINS * window_count)
    both = np.stack([np.cos(angles) * scale, -np.sin(angles) * scale])
    return both.astype(np.float32).astype(ml_dtypes.bfloat16)


def gather_kernel(
    members,
    raw_ref,
    taps_ref,
    order_ref,
    pairing_ref,
    out_ref,
    raw,
    tail,
    halo,
    column,
    private,
    picked,
    raw_sem,
    halo_sems,
    line_send,
    line_recv,
    pick_send,
    pick_recv,
):
    me = lax.axis_index("sta")
    stations, local_time = raw_ref.shape
    line, pieces = column.shape[:2]
    rank, lead = me // QUAD, me % QUAD
    turn = 1 - 2 * lax.rem(me, 2)
    twin = me + turn
    across = rank * QUAD + lax.rem(lead + 2, QUAD)
    others = (across, across + turn, twin)
    after, before = lax.rem(me + 1, members), lax.rem(me + members - 1, members)

    def of_rank(choose):
        chosen = choose(0)
        for r in range(1, line):
            chosen = jnp.where(rank == r, choose(r), chosen)
        return chosen

    def arrivals(r):
        known = sorted((abs(x - r), -piece, x) for x in range(line) if x != r for piece in range(pieces))
        return [(x, -negative) for _, negative, x in known]

    expected = [
        (of_rank(lambda r: arrivals(r)[n][0]), of_rank(lambda r: arrivals(r)[n][1]))
        for n in range((line - 1) * pieces)
    ]

    raw_copy = pltpu.make_async_copy(raw_ref, raw, raw_sem)
    raw_copy.start()

    barrier = pltpu.get_barrier_semaphore()
    greeted = [lax.rem(rank + n, line) * QUAD + lead for n in range(1, line)] + list(others) + [after, before]
    for peer in greeted:
        pl.semaphore_signal(barrier, inc=1, device_id={"sta": peer}, device_id_type=MESH)

    relayed = line > 3
    at_end = (rank == 0) | (rank == line - 1)
    beside_end = (rank == 1) | (rank == line - 2)
    joined = rank + jnp.where((rank == 0) | (rank == line - 2), 1, -1)
    near_end = at_end | beside_end
    if relayed:

        @pl.when(near_end)
        def _():
            for n in range(1, QUAD):
                peer = joined * QUAD + lax.rem(lead + n, QUAD)
                pl.semaphore_signal(barrier, inc=1, device_id={"sta": peer}, device_id_type=MESH)

    mirror = (
        lax.broadcasted_iota(jnp.int32, (TAPS, TAPS), 0) + lax.broadcasted_iota(jnp.int32, (TAPS, TAPS), 1) == TAPS - 1
    ).astype(jnp.float32).astype(jnp.bfloat16)
    taps = jnp.broadcast_to(taps_ref[...].astype(jnp.float32).reshape(1, TAPS), (SB, TAPS)).astype(jnp.bfloat16)
    taps = jnp.dot(taps, mirror, preferred_element_type=jnp.float32)[:1]
    banded = jnp.concatenate([taps, jnp.zeros((1, SPAN - TAPS), jnp.float32)], axis=1)
    banded = jnp.broadcast_to(banded, (LANE, SPAN))
    banded = pltpu.roll(banded, DEC, 1, stride=DEC, stride_axis=0).astype(jnp.bfloat16)
    picks = (lax.broadcasted_iota(jnp.int32, (stations, stations), 0) == order_ref[...]).astype(jnp.float32)
    picks = picks.T.astype(jnp.bfloat16)

    dims = (((1,), (1,)), ((), ()))
    lane = lax.broadcasted_iota(jnp.int32, (1, LANE), 1)
    half = LANE // 2
    raw_copy.wait()
    spilled = lax.dot_general(
        raw[:, local_time - TAPS :], banded[:, :TAPS], dims, preferred_element_type=jnp.float32
    )
    tail[...] = jnp.where(
        lane < half, spilled[: stations // 2], pltpu.roll(spilled[stations // 2 :], half, 1)
    ).astype(jnp.bfloat16)

    pl.semaphore_wait(barrier, len(greeted) + (jnp.where(near_end, QUAD - 1, 0) if relayed else 0))

    halo_copy = pltpu.make_async_remote_copy(
        src_ref=tail,
        dst_ref=halo,
        send_sem=halo_sems.at[0],
        recv_sem=halo_sems.at[1],
        device_id={"sta": after},
        device_id_type=MESH,
    )

    @pl.when(me < members - 1)
    def _():
        halo_copy.start()

    def line_copy(source, piece, n, peer):
        return pltpu.make_async_remote_copy(
            src_ref=column.at[source, piece],
            dst_ref=column.at[source, piece],
            send_sem=line_send.at[n],
            recv_sem=line_recv.at[source * pieces + piece],
            device_id={"sta": peer * QUAD + lead},
            device_id_type=MESH,
        )

    passed = []

    def pass_on(source, piece, ahead, there):
        copy = line_copy(source, piece, len(passed), rank + ahead)
        passed.append((copy, there))

        @pl.when(there)
        def _():
            copy.start()

    picks_sent = []

    def share(source, piece, samples, peers, there):
        private[...] = samples.reshape(private.shape)
        plane = (source * QUAD + lead) * pieces + piece
        for peer in peers:
            slot = len(picks_sent)
            for g, block in enumerate([pairing_ref[r, peer] for r in range(ROUNDS)] + [peer]):
                picked[slot, g * SB : (g + 1) * SB, :] = private[block]
            copy = pltpu.make_async_remote_copy(
                src_ref=picked.at[slot],
                dst_ref=out_ref.at[plane],
                send_sem=pick_send.at[slot],
                recv_sem=pick_recv.at[plane],
                device_id={"sta": peer},
                device_id_type=MESH,
            )
            copy.start()
            picks_sent.append(there)

    def keep(source, piece):
        plane = (source * QUAD + lead) * pieces + piece
        for g, block in enumerate([pairing_ref[r, me] for r in range(ROUNDS)] + [me]):
            out_ref[plane, g * SB : (g + 1) * SB, :] = private[block]

    def filtered(piece, first, spill=None):
        summed = lax.dot_general(
            raw[:, max(first, 0) : first + SPAN],
            banded[:, max(-first, 0) :],
            dims,
            preferred_element_type=jnp.float32,
        )
        if spill is not None:
            summed = summed + spill
        ordered = jnp.dot(picks, summed.astype(jnp.bfloat16), preferred_element_type=jnp.float32).astype(jnp.bfloat16)
        column[rank, piece] = ordered
        pass_on(rank, piece, 1, rank < line - 1)
        pass_on(rank, piece, -1, rank > 0)
        share(rank, piece, ordered, others, None)
        keep(rank, piece)

    for piece in range(pieces - 1, 0, -1):
        filtered(piece, piece * LANE * DEC - TAPS)

    @pl.when(me > 0)
    def _():
        halo_copy.wait_recv()

    @pl.when(me == 0)
    def _():
        halo[...] = jnp.zeros_like(halo)

    spill = halo[...].astype(jnp.float32)
    spill = [jnp.where(lane < half, x, 0.0) for x in (spill, pltpu.roll(spill, half, 1))]
    filtered(0, -TAPS, jnp.concatenate(spill, axis=0))

    for n, (source, piece) in enumerate(expected):
        from_below = source < rank
        there = (from_below & (rank < line - 1)) | (jnp.logical_not(from_below) & (rank > 0))
        ahead = jnp.where(from_below, 1, -1)
        if relayed and n >= len(expected) - pieces:
            inside = jnp.logical_not(at_end)

            @pl.when(inside)
            def _():
                line_copy(source, piece, 0, source).wait_recv()

            pass_on(source, piece, ahead, there & jnp.logical_not(near_end))

            @pl.when(beside_end)
            def _():
                ends = [joined * QUAD + lax.rem(lead + k, QUAD) for k in range(QUAD)]
                share(source, piece, column[source, piece], ends, beside_end)

            @pl.when(inside)
            def _():
                share(source, piece, column[source, piece], others, inside)
                keep(source, piece)
        else:
            line_copy(source, piece, 0, source).wait_recv()
            pass_on(source, piece, ahead, there)
            share(source, piece, column[source, piece], others, None)
            keep(source, piece)

    def landed(plane):
        pltpu.make_async_remote_copy(
            src_ref=picked.at[0],
            dst_ref=out_ref.at[plane],
            send_sem=pick_send.at[0],
            recv_sem=pick_recv.at[plane],
            device_id={"sta": twin},
            device_id_type=MESH,
        ).wait_recv()

    for source in range(line):
        for piece in range(pieces):
            for peer in others:
                landed((peer - rank * QUAD + source * QUAD) * pieces + piece)
    if relayed:

        @pl.when(at_end)
        def _():
            for piece in range(pieces):
                landed(((line - 1 - rank) * QUAD + lead) * pieces + piece)

    leaving = [
        (
            pltpu.make_async_remote_copy(
                src_ref=picked.at[slot],
                dst_ref=out_ref.at[0],
                send_sem=pick_send.at[slot],
                recv_sem=pick_recv.at[0],
                device_id={"sta": twin},
                device_id_type=MESH,
            ),
            there,
        )
        for slot, there in enumerate(picks_sent)
    ]
    for copy, there in leaving + passed:
        if there is None:
            copy.wait_send()
        else:

            @pl.when(there)
            def _():
                copy.wait_send()

    @pl.when(me < members - 1)
    def _():
        halo_copy.wait_send()


def correlate_kernel(
    starts_ref,
    low_ref,
    taper_ref,
    dft_hbm,
    lag_hbm,
    out_hbm,
    out_ref,
    dft_ref,
    lag_ref,
    ahead,
    back,
    theirs,
    own,
    white_own,
    left,
    right,
    cross_real,
    cross_imag,
    dft_sems,
    lag_sem,
    out_sems,
):
    planes = low_ref.shape[0]
    window_count = starts_ref.shape[0]
    lane = lax.broadcasted_iota(jnp.int32, (1, LANE), 1)
    dft_copies = [
        pltpu.make_async_copy(
            dft_hbm.at[:, n * HT : (n + 1) * HT, :], dft_ref.at[:, n * HT : (n + 1) * HT, :], dft_sems.at[n]
        )
        for n in range(TILES)
    ]
    lag_copy = pltpu.make_async_copy(lag_hbm, lag_ref, lag_sem)

    for copy in dft_copies:
        copy.start()
    lag_copy.start()
    mirror = (
        lax.broadcasted_iota(jnp.int32, (LANE, LANE), 0) + lax.broadcasted_iota(jnp.int32, (LANE, LANE), 1) == LANE
    ).astype(jnp.float32).astype(jnp.bfloat16)

    def one_plane(n, carry):
        samples = low_ref[n]
        ahead[n] = samples.astype(jnp.float32)
        turned = jnp.dot(samples, mirror, preferred_element_type=jnp.float32)
        later = low_ref[jnp.minimum(n + 1, planes - 1)].astype(jnp.float32)
        later = jnp.where(n + 1 < planes, later, jnp.zeros_like(later))
        back[planes - 1 - n] = jnp.where(lane == 0, later, turned)
        return carry

    lax.fori_loop(0, planes, one_plane, 0, unroll=16)

    def one_window(w, carry):
        start = starts_ref[w]
        plane, rest = start // LANE, start % LANE
        taper = taper_ref[...]
        fore = pltpu.roll(taper, rest, 1)
        hind = pltpu.roll(taper, (LANE - rest) % LANE, 1)
        span = SEG // LANE
        rise = [jnp.where(lane >= rest, fore[p + 1 : p + 2], fore[p : p + 1]) for p in range(FOLD // LANE + 1)]
        fall = [
            jnp.where(lane < LANE - rest, hind[p + 1 : p + 2], hind[p + 2 : p + 3]) for p in range(FOLD // LANE)
        ]
        at = pl.ds(pl.multiple_of(w * THEIRS, SB), THEIRS)
        own_at = pl.ds(pl.multiple_of(w * SB, SB), SB)

        def put(kind, p, values):
            values = values.astype(jnp.bfloat16)
            lanes = slice(p * LANE, (p + 1) * LANE)
            theirs[kind, at, lanes] = values[:THEIRS]
            own[kind, own_at, lanes] = values[THEIRS:]

        last = FOLD // LANE
        a = rise[last] * ahead[plane + last]
        b = (1.0 - rise[last]) * ahead[plane + last + span // 2]
        put(0, last, a + b)
        middle = a - b
        for p in range(FOLD // LANE):
            first = ahead[plane + p]
            if p == 0:
                first = jnp.where(lane < rest, ahead[jnp.minimum(plane + span, planes - 1)], first)
            a = rise[p] * first
            b = (1.0 - rise[p]) * ahead[plane + span // 2 + p]
            c = fall[p] * back[planes - plane - span + p]
            d = (1.0 - fall[p]) * back[planes - plane - span // 2 + p]
            same, apart = a + b, a - b
            same_turned, apart_turned = d + c, d - c
            put(0, p, same + same_turned)
            put(1, p, apart - apart_turned)
            put(2, p, same - same_turned)
            summed = apart + apart_turned
            put(3, p, jnp.where(lane == 0, middle, summed) if p == 0 else summed)
        return carry

    lax.fori_loop(0, window_count, one_window, 0, unroll=8)

    def dot_nt(a, b):
        return lax.dot_general(a, b, NT, preferred_element_type=jnp.float32)

    depth = (FOLD + LANE, FOLD, FOLD, FOLD)
    half = LANE // 2
    wide = 2 * LANE
    first = lane < half
    slots = LANE // PACK
    turns = slots // 2
    strip = BAND // 2
    halves = HT // PACK
    own_bin = lax.broadcasted_iota(jnp.int32, (PACK * SB, LANE), 0) // SB
    mask = (own_bin == lax.broadcasted_iota(jnp.int32, (PACK * SB, LANE), 1) % PACK).astype(jnp.float32).astype(
        jnp.bfloat16
    )

    def one_group(tile, n):
        masked = jnp.concatenate([jnp.concatenate([left[tile, n, h]] * PACK, axis=0) * mask for h in range(2)], axis=1)
        product = jnp.dot(masked, right[tile, n], preferred_element_type=jnp.float32)
        product = product.reshape(PACK, 2, SB // 2, LANE)
        a, b = product[:, 0].reshape(PACK * SB // 2, LANE), product[:, 1].reshape(PACK * SB // 2, LANE)
        turned = pltpu.roll(jnp.where(first, b, a), half, 1)
        row = (tile * (FT // PACK) + n) * PACK * SB // 2
        at = pl.ds(row if isinstance(n, int) else pl.multiple_of(row, PACK * SB // 2), PACK * SB // 2)
        cross_real[at, :] = jnp.where(first, a, turned)
        cross_imag[at, :] = jnp.where(first, turned, b)

    def transforms(tile):
        dft_copies[tile].wait()
        bins = slice(tile * HT, (tile + 1) * HT)
        for tile_pair in range(window_count * THEIRS // wide):
            at = slice(tile_pair * wide, (tile_pair + 1) * wide)
            spectra = [dot_nt(dft_ref[k, bins, : depth[k]], theirs[k, at, : depth[k]]) for k in range(4)]
            for n in range(HT // strip):
                for inner in range(wide // LANE):
                    parts = [x[n * strip : (n + 1) * strip, inner * LANE : (inner + 1) * LANE] for x in spectra]
                    power = sum(x * x for x in parts[1:]) + parts[0] * parts[0]
                    level = jnp.sum(power, axis=0, keepdims=True)
                    scale = lax.rsqrt(level * (1.0 / (2 * BAND)) + 1e-06)
                    for parity in range(2):
                        real, imag = parts[parity] * scale, parts[2 + parity] * scale

                        def stacked(x, y):
                            both = [v.reshape(strip // PACK, 1, PACK, LANE) for v in (x, y)]
                            both = jnp.concatenate(both, axis=1).reshape(strip * 2, LANE)
                            return both.astype(jnp.bfloat16)

                        plain, crossed = stacked(real, imag), stacked(-imag, real)
                        turned = pltpu.roll(jnp.where(first, crossed, plain), half, 1)
                        for k, block in enumerate((jnp.where(first, plain, turned), jnp.where(first, turned, crossed))):
                            w = (tile_pair * (wide // LANE) + inner) * 2 + k
                            for m in range(strip // PACK):
                                group = n * (strip // PACK) + m
                                turn = group % slots // 2
                                row = w // turns * LANE + (w + turn) % turns * 2 * PACK
                                right[tile, parity * halves + group, row : row + 2 * PACK, :] = block[
                                    m * 2 * PACK : (m + 1) * 2 * PACK
                                ]

        spectra = [dot_nt(own[k, :, : depth[k]], dft_ref[k, bins, : depth[k]]) for k in range(4)]
        power = sum(x * x for x in spectra[1:]) + spectra[0] * spectra[0]
        same = (
            lax.broadcasted_iota(jnp.int32, (HT, HT), 0) // strip == lax.broadcasted_iota(jnp.int32, (HT, HT), 1) // strip
        ).astype(jnp.float32).astype(jnp.bfloat16)
        level = jnp.dot(power.astype(jnp.bfloat16), same, preferred_element_type=jnp.float32)
        scale = lax.rsqrt(level * (1.0 / (2 * BAND)) + 1e-06)
        for k in range(4):
            white_own[tile, k] = (spectra[k] * scale).astype(jnp.bfloat16)

        low_slot = lane // PACK % 2 == 0
        for parity in range(2):
            for part in range(HT // LANE):
                for h in range(window_count // turns):
                    moved = [[], []]
                    for w in range(turns):
                        row = (h * turns + w) * SB
                        x = [
                            white_own[tile, 2 * c + parity, row : row + SB, part * LANE : (part + 1) * LANE] for c in range(2)
                        ]
                        y = (
                            jnp.where(low_slot, x[0], pltpu.roll(x[1], PACK, 1)),
                            jnp.where(low_slot, pltpu.roll(x[0], LANE - PACK, 1), x[1]),
                        )
                        for k in range(2):
                            moved[k].append(pltpu.roll(y[k], 2 * PACK * w, 1) if w else y[k])
                    for slot in range(slots):
                        turn, k = slot // 2, slot % 2
                        joined = moved[k][0]
                        for w in range(1, turns):
                            joined = jnp.where(lane // (2 * PACK) == (turn + w) % turns, moved[k][w], joined)
                        left[tile, parity * halves + part * slots + slot, h] = joined

    def products(tile):
        def several(n, carry):
            one_group(tile, n)
            return carry

        lax.fori_loop(0, FT // PACK, several, 0, unroll=32)

    for tile in range(TILES):
        transforms(tile)
        if tile:
            products(tile - 1)
    products(TILES - 1)

    lag_copy.wait()
    out_copies = []
    for n in range(SB // 4):
        summed = None
        for k, cross in enumerate((cross_real, cross_imag)):
            columns = jnp.concatenate(
                [cross[pl.ds(2 * n + m, BINS, stride=SB // 2), :].astype(jnp.bfloat16) for m in range(2)], axis=1
            )
            term = jnp.dot(lag_ref[k], columns, preferred_element_type=jnp.float32)
            summed = term if summed is None else summed + term
        turned = summed.T
        for h in range(2):
            station = h * (SB // 2) + 2 * n
            for m in range(2):
                for r in range(ROUNDS):
                    row = ((m * 2 + h) * ROUNDS + r) * SB
                    out_ref[r, (station + m) * SB : (station + m + 1) * SB, :] = turned[row : row + SB]
            rows = slice(station * SB, (station + 2) * SB)
            copy = pltpu.make_async_copy(
                out_ref.at[:, rows, :], out_hbm.at[:, rows, :], out_sems.at[len(out_copies)]
            )
            copy.start()
            out_copies.append(copy)
    for copy in out_copies:
        copy.wait()


def correlate(window_starts, low, taper, dft, lag):
    window_count = window_starts.shape[0]
    planes = low.shape[0]
    in_vmem = pl.BlockSpec(memory_space=pltpu.VMEM)
    anywhere = pl.BlockSpec(memory_space=pl.ANY)
    return pl.pallas_call(
        correlate_kernel,
        in_specs=[pl.BlockSpec(memory_space=pltpu.SMEM), in_vmem, in_vmem, anywhere, anywhere],
        out_specs=anywhere,
        out_shape=jax.ShapeDtypeStruct((ROUNDS, SB * SB, LAGS), jnp.float32),
        scratch_shapes=[
            pltpu.VMEM((ROUNDS, SB * SB, LAGS), jnp.float32),
            pltpu.VMEM(dft.shape, jnp.bfloat16),
            pltpu.VMEM(lag.shape, jnp.bfloat16),
            pltpu.VMEM((planes, ROWS, LANE), jnp.float32),
            pltpu.VMEM((planes, ROWS, LANE), jnp.float32),
            pltpu.VMEM((4, window_count * THEIRS, FOLD + LANE), jnp.bfloat16),
            pltpu.VMEM((4, window_count * SB, FOLD + LANE), jnp.bfloat16),
            pltpu.VMEM((TILES, 4, window_count * SB, HT), jnp.bfloat16),
            pltpu.VMEM((TILES, FT // PACK, 2, SB, LANE), jnp.bfloat16),
            pltpu.VMEM((TILES, FT // PACK, 2 * LANE, LANE), jnp.bfloat16),
            pltpu.VMEM((BINS * SB // 2, LANE), jnp.float32),
            pltpu.VMEM((BINS * SB // 2, LANE), jnp.float32),
            pltpu.SemaphoreType.DMA((TILES,)),
            pltpu.SemaphoreType.DMA,
            pltpu.SemaphoreType.DMA((SB // 2,)),
        ],
        compiler_params=pltpu.CompilerParams(vmem_limit_bytes=60 * 2**20),
    )(window_starts, low, taper, dft, lag)


def body(raw_traces, filter_taps, station_order, window_starts, pairing):
    members = lax.axis_size("sta")
    stations, local_time = raw_traces.shape
    window_count = window_starts.shape[0]
    pieces = local_time // (LANE * DEC)
    line = members // QUAD
    in_vmem = pl.BlockSpec(memory_space=pltpu.VMEM)
    low = pl.pallas_call(
        functools.partial(gather_kernel, members),
        out_shape=jax.ShapeDtypeStruct((members * pieces, ROWS, LANE), jnp.bfloat16),
        in_specs=[
            pl.BlockSpec(memory_space=pl.ANY),
            in_vmem,
            in_vmem,
            pl.BlockSpec(memory_space=pltpu.SMEM),
        ],
        out_specs=in_vmem,
        scratch_shapes=[
            pltpu.VMEM((stations, local_time), jnp.bfloat16),
            pltpu.VMEM((stations // 2, LANE), jnp.bfloat16),
            pltpu.VMEM((stations // 2, LANE), jnp.bfloat16),
            pltpu.VMEM((line, pieces, stations, LANE), jnp.bfloat16),
            pltpu.VMEM((stations // SB, SB, LANE), jnp.bfloat16),
            pltpu.VMEM(((3 * line + QUAD) * pieces, ROWS, LANE), jnp.bfloat16),
            pltpu.SemaphoreType.DMA,
            pltpu.SemaphoreType.DMA((2,)),
            pltpu.SemaphoreType.DMA(((line + 1) * pieces,)),
            pltpu.SemaphoreType.DMA((line * pieces,)),
            pltpu.SemaphoreType.DMA(((3 * line + QUAD) * pieces,)),
            pltpu.SemaphoreType.DMA((members * pieces,)),
        ],
        compiler_params=pltpu.CompilerParams(
            collective_id=0, has_side_effects=True, vmem_limit_bytes=60 * 2**20
        ),
    )(raw_traces, filter_taps, station_order.reshape(1, stations), pairing)
    correlated = correlate(
        window_starts,
        low,
        jnp.asarray(taper_table()),
        jnp.asarray(dft_table()),
        jnp.asarray(lag_table(window_count)),
    )
    return correlated.reshape(ROUNDS, SB, SB, LAGS)


def solution(mesh):
    return jax.shard_map(
        body,
        mesh=mesh,
        in_specs=(P("parts", "sta"), P(), P("parts"), P("parts"), P()),
        out_specs=P(None, ("parts", "sta"), None, None),
        check_vma=False,
    )
```

```python
import functools
import math

import jax
import jax.numpy as jnp
import ml_dtypes
import numpy as np
from jax import lax
from jax.experimental import pallas as pl
from jax.experimental.pallas import tpu as pltpu
from jax.sharding import PartitionSpec as P

SB = 16
DEC = 4
TAPS = 256
SEG = 2048
BAND = 64
LAGS = 256
ROUNDS = 4
BINS = 1024
LANE = 128
SPAN = LANE * DEC + TAPS
GROUPS = ROUNDS + 1
ROWS = GROUPS * SB
THEIRS = ROUNDS * SB
FOLD = SEG // 4
FT = 512
HT = FT // 2
TILES = BINS // FT
PACK = 8
NT = (((1,), (1,)), ((), ()))
QUAD = 4
MESH = pl.DeviceIdType.MESH


def taper_table():
    sample = np.arange(-LANE, 7 * LANE)
    return (0.5 - 0.5 * np.cos(sample * (2.0 * math.pi / SEG))).astype(np.float32).reshape(8, LANE)


def dft_table():
    sample = np.arange(FOLD)
    kinds = []
    for wave in (np.cos, lambda a: -np.sin(a)):
        for parity in range(2):
            frequency = 2 * np.arange(BINS // 2) + parity
            table = np.zeros((BINS // 2, FOLD + LANE))
            table[:, :FOLD] = wave((sample[None, :] * frequency[:, None] % SEG) * (2.0 * math.pi / SEG))
            middle = np.round(wave((frequency * FOLD % SEG) * (2.0 * math.pi / SEG)))
            if wave is np.cos:
                table[:, 0] = 0.5
                table[:, FOLD] = middle
            else:
                table[:, 0] = middle
            kinds.append(table)
    return np.stack(kinds).astype(np.float32).astype(ml_dtypes.bfloat16)


def lag_table(window_count):
    frequency = 2 * np.arange(BINS // 2).reshape(TILES, 1, HT) + np.arange(2).reshape(1, 2, 1)
    frequency = frequency.reshape(BINS)
    offset = np.arange(LAGS) - LAGS // 2 + SEG
    angles = (frequency[None, :] * offset[:, None] % SEG) * (2.0 * math.pi / SEG)
    scale = 1.0 / math.sqrt(BINS * window_count)
    both = np.stack([np.cos(angles) * scale, -np.sin(angles) * scale])
    return both.astype(np.float32).astype(ml_dtypes.bfloat16)


def gather_kernel(
    members,
    raw_ref,
    taps_ref,
    order_ref,
    pairing_ref,
    out_ref,
    raw,
    tail,
    halo,
    column,
    private,
    picked,
    kept,
    keep_sems,
    raw_sem,
    halo_sems,
    line_send,
    line_recv,
    pick_send,
    pick_recv,
):
    me = lax.axis_index("sta")
    stations, local_time = raw_ref.shape
    line, pieces = column.shape[:2]
    rank, lead = me // QUAD, me % QUAD
    turn = 1 - 2 * lax.rem(me, 2)
    twin = me + turn
    across = rank * QUAD + lax.rem(lead + 2, QUAD)
    others = (across, across + turn, twin)
    after, before = lax.rem(me + 1, members), lax.rem(me + members - 1, members)

    def of_rank(choose):
        chosen = choose(0)
        for r in range(1, line):
            chosen = jnp.where(rank == r, choose(r), chosen)
        return chosen

    def arrivals(r):
        known = sorted((abs(x - r), -piece, x) for x in range(line) if x != r for piece in range(pieces))
        return [(x, -negative) for _, negative, x in known]

    expected = [
        (of_rank(lambda r: arrivals(r)[n][0]), of_rank(lambda r: arrivals(r)[n][1]))
        for n in range((line - 1) * pieces)
    ]

    raw_copy = pltpu.make_async_copy(raw_ref, raw, raw_sem)
    raw_copy.start()

    barrier = pltpu.get_barrier_semaphore()
    greeted = [lax.rem(rank + n, line) * QUAD + lead for n in range(1, line)] + list(others) + [after, before]
    for peer in greeted:
        pl.semaphore_signal(barrier, inc=1, device_id={"sta": peer}, device_id_type=MESH)

    relayed = line > 3
    at_end = (rank == 0) | (rank == line - 1)
    beside_end = (rank == 1) | (rank == line - 2)
    joined = rank + jnp.where((rank == 0) | (rank == line - 2), 1, -1)
    near_end = at_end | beside_end
    if relayed:

        @pl.when(near_end)
        def _():
            for n in range(1, QUAD):
                peer = joined * QUAD + lax.rem(lead + n, QUAD)
                pl.semaphore_signal(barrier, inc=1, device_id={"sta": peer}, device_id_type=MESH)

    mirror = (
        lax.broadcasted_iota(jnp.int32, (TAPS, TAPS), 0) + lax.broadcasted_iota(jnp.int32, (TAPS, TAPS), 1) == TAPS - 1
    ).astype(jnp.float32).astype(jnp.bfloat16)
    taps = jnp.broadcast_to(taps_ref[...].astype(jnp.float32).reshape(1, TAPS), (SB, TAPS)).astype(jnp.bfloat16)
    taps = jnp.dot(taps, mirror, preferred_element_type=jnp.float32)[:1]
    banded = jnp.concatenate([taps, jnp.zeros((1, SPAN - TAPS), jnp.float32)], axis=1)
    banded = jnp.broadcast_to(banded, (LANE, SPAN))
    banded = pltpu.roll(banded, DEC, 1, stride=DEC, stride_axis=0).astype(jnp.bfloat16)
    picks = (lax.broadcasted_iota(jnp.int32, (stations, stations), 0) == order_ref[...]).astype(jnp.float32)
    picks = picks.T.astype(jnp.bfloat16)

    dims = (((1,), (1,)), ((), ()))
    lane = lax.broadcasted_iota(jnp.int32, (1, LANE), 1)
    half = LANE // 2
    raw_copy.wait()
    spilled = lax.dot_general(
        raw[:, local_time - TAPS :], banded[:, :TAPS], dims, preferred_element_type=jnp.float32
    )
    tail[...] = jnp.where(
        lane < half, spilled[: stations // 2], pltpu.roll(spilled[stations // 2 :], half, 1)
    ).astype(jnp.bfloat16)

    pl.semaphore_wait(barrier, len(greeted) + (jnp.where(near_end, QUAD - 1, 0) if relayed else 0))

    halo_copy = pltpu.make_async_remote_copy(
        src_ref=tail,
        dst_ref=halo,
        send_sem=halo_sems.at[0],
        recv_sem=halo_sems.at[1],
        device_id={"sta": after},
        device_id_type=MESH,
    )

    @pl.when(me < members - 1)
    def _():
        halo_copy.start()

    def line_copy(source, piece, n, peer):
        return pltpu.make_async_remote_copy(
            src_ref=column.at[source, piece],
            dst_ref=column.at[source, piece],
            send_sem=line_send.at[n],
            recv_sem=line_recv.at[source * pieces + piece],
            device_id={"sta": peer * QUAD + lead},
            device_id_type=MESH,
        )

    passed = []

    def pass_on(source, piece, ahead, there):
        copy = line_copy(source, piece, len(passed), rank + ahead)
        passed.append((copy, there))

        @pl.when(there)
        def _():
            copy.start()

    picks_sent = []

    def share(source, piece, samples, peers, there):
        private[...] = samples.reshape(private.shape)
        plane = (source * QUAD + lead) * pieces + piece
        for peer in peers:
            slot = len(picks_sent)
            for g, block in enumerate([pairing_ref[r, peer] for r in range(ROUNDS)] + [peer]):
                picked[slot, g * SB : (g + 1) * SB, :] = private[block]
            copy = pltpu.make_async_remote_copy(
                src_ref=picked.at[slot],
                dst_ref=out_ref.at[plane],
                send_sem=pick_send.at[slot],
                recv_sem=pick_recv.at[plane],
                device_id={"sta": peer},
                device_id_type=MESH,
            )
            copy.start()
            picks_sent.append(there)

    kept_there = []

    def keep(source, piece, there):
        slot = len(kept_there)
        plane = (source * QUAD + lead) * pieces + piece
        for g, block in enumerate([pairing_ref[r, me] for r in range(ROUNDS)] + [me]):
            kept[slot, g * SB : (g + 1) * SB, :] = private[block]
        pltpu.make_async_copy(kept.at[slot], out_ref.at[plane], keep_sems.at[slot]).start()
        kept_there.append(there)

    def filtered(piece, first, spill=None):
        summed = lax.dot_general(
            raw[:, max(first, 0) : first + SPAN],
            banded[:, max(-first, 0) :],
            dims,
            preferred_element_type=jnp.float32,
        )
        if spill is not None:
            summed = summed + spill
        ordered = jnp.dot(picks, summed.astype(jnp.bfloat16), preferred_element_type=jnp.float32).astype(jnp.bfloat16)
        column[rank, piece] = ordered
        pass_on(rank, piece, 1, rank < line - 1)
        pass_on(rank, piece, -1, rank > 0)
        share(rank, piece, ordered, others, None)
        keep(rank, piece, None)

    for piece in range(pieces - 1, 0, -1):
        filtered(piece, piece * LANE * DEC - TAPS)

    @pl.when(me > 0)
    def _():
        halo_copy.wait_recv()

    @pl.when(me == 0)
    def _():
        halo[...] = jnp.zeros_like(halo)

    spill = halo[...].astype(jnp.float32)
    spill = [jnp.where(lane < half, x, 0.0) for x in (spill, pltpu.roll(spill, half, 1))]
    filtered(0, -TAPS, jnp.concatenate(spill, axis=0))

    for n, (source, piece) in enumerate(expected):
        from_below = source < rank
        there = (from_below & (rank < line - 1)) | (jnp.logical_not(from_below) & (rank > 0))
        ahead = jnp.where(from_below, 1, -1)
        if relayed and n >= len(expected) - pieces:
            inside = jnp.logical_not(at_end)

            @pl.when(inside)
            def _():
                line_copy(source, piece, 0, source).wait_recv()

            pass_on(source, piece, ahead, there & jnp.logical_not(near_end))

            @pl.when(beside_end)
            def _():
                ends = [joined * QUAD + lax.rem(lead + k, QUAD) for k in range(QUAD)]
                share(source, piece, column[source, piece], ends, beside_end)

            @pl.when(inside)
            def _():
                share(source, piece, column[source, piece], others, inside)
                keep(source, piece, inside)
        else:
            line_copy(source, piece, 0, source).wait_recv()
            pass_on(source, piece, ahead, there)
            share(source, piece, column[source, piece], others, None)
            keep(source, piece, None)

    def landed(plane):
        pltpu.make_async_remote_copy(
            src_ref=picked.at[0],
            dst_ref=out_ref.at[plane],
            send_sem=pick_send.at[0],
            recv_sem=pick_recv.at[plane],
            device_id={"sta": twin},
            device_id_type=MESH,
        ).wait_recv()

    for source in range(line):
        for piece in range(pieces):
            for peer in others:
                landed((peer - rank * QUAD + source * QUAD) * pieces + piece)
    if relayed:

        @pl.when(at_end)
        def _():
            for piece in range(pieces):
                landed(((line - 1 - rank) * QUAD + lead) * pieces + piece)

    leaving = [
        (
            pltpu.make_async_remote_copy(
                src_ref=picked.at[slot],
                dst_ref=out_ref.at[0],
                send_sem=pick_send.at[slot],
                recv_sem=pick_recv.at[0],
                device_id={"sta": twin},
                device_id_type=MESH,
            ),
            there,
        )
        for slot, there in enumerate(picks_sent)
    ]
    def kept_done(slot):
        pltpu.make_async_copy(kept.at[slot], out_ref.at[0], keep_sems.at[slot]).wait()

    for slot, there in enumerate(kept_there):
        if there is None:
            kept_done(slot)
        else:

            @pl.when(there)
            def _():
                kept_done(slot)

    for copy, there in leaving + passed:
        if there is None:
            copy.wait_send()
        else:

            @pl.when(there)
            def _():
                copy.wait_send()

    @pl.when(me < members - 1)
    def _():
        halo_copy.wait_send()


def correlate_kernel(
    starts_ref,
    low_ref,
    taper_ref,
    dft_hbm,
    lag_hbm,
    out_hbm,
    out_ref,
    dft_ref,
    lag_ref,
    ahead,
    back,
    theirs,
    own,
    white_own,
    left,
    right,
    cross_real,
    cross_imag,
    dft_sems,
    lag_sem,
    out_sems,
):
    planes = low_ref.shape[0]
    window_count = starts_ref.shape[0]
    lane = lax.broadcasted_iota(jnp.int32, (1, LANE), 1)
    dft_copies = [
        pltpu.make_async_copy(
            dft_hbm.at[:, n * HT : (n + 1) * HT, :], dft_ref.at[:, n * HT : (n + 1) * HT, :], dft_sems.at[n]
        )
        for n in range(TILES)
    ]
    lag_copy = pltpu.make_async_copy(lag_hbm, lag_ref, lag_sem)

    for copy in dft_copies:
        copy.start()
    lag_copy.start()
    mirror = (
        lax.broadcasted_iota(jnp.int32, (LANE, LANE), 0) + lax.broadcasted_iota(jnp.int32, (LANE, LANE), 1) == LANE
    ).astype(jnp.float32).astype(jnp.bfloat16)

    def one_plane(n, carry):
        samples = low_ref[n]
        ahead[n] = samples.astype(jnp.float32)
        turned = jnp.dot(samples, mirror, preferred_element_type=jnp.float32)
        later = low_ref[jnp.minimum(n + 1, planes - 1)].astype(jnp.float32)
        later = jnp.where(n + 1 < planes, later, jnp.zeros_like(later))
        back[planes - 1 - n] = jnp.where(lane == 0, later, turned)
        return carry

    lax.fori_loop(0, planes, one_plane, 0, unroll=16)

    def one_window(w, carry):
        start = starts_ref[w]
        plane, rest = start // LANE, start % LANE
        taper = taper_ref[...]
        fore = pltpu.roll(taper, rest, 1)
        hind = pltpu.roll(taper, (LANE - rest) % LANE, 1)
        span = SEG // LANE
        rise = [jnp.where(lane >= rest, fore[p + 1 : p + 2], fore[p : p + 1]) for p in range(FOLD // LANE + 1)]
        fall = [
            jnp.where(lane < LANE - rest, hind[p + 1 : p + 2], hind[p + 2 : p + 3]) for p in range(FOLD // LANE)
        ]
        at = pl.ds(pl.multiple_of(w * THEIRS, SB), THEIRS)
        own_at = pl.ds(pl.multiple_of(w * SB, SB), SB)

        def put(kind, p, values):
            values = values.astype(jnp.bfloat16)
            lanes = slice(p * LANE, (p + 1) * LANE)
            theirs[kind, at, lanes] = values[:THEIRS]
            own[kind, own_at, lanes] = values[THEIRS:]

        last = FOLD // LANE
        a = rise[last] * ahead[plane + last]
        b = (1.0 - rise[last]) * ahead[plane + last + span // 2]
        put(0, last, a + b)
        middle = a - b
        for p in range(FOLD // LANE):
            first = ahead[plane + p]
            if p == 0:
                first = jnp.where(lane < rest, ahead[jnp.minimum(plane + span, planes - 1)], first)
            a = rise[p] * first
            b = (1.0 - rise[p]) * ahead[plane + span // 2 + p]
            c = fall[p] * back[planes - plane - span + p]
            d = (1.0 - fall[p]) * back[planes - plane - span // 2 + p]
            same, apart = a + b, a - b
            same_turned, apart_turned = d + c, d - c
            put(0, p, same + same_turned)
            put(1, p, apart - apart_turned)
            put(2, p, same - same_turned)
            summed = apart + apart_turned
            put(3, p, jnp.where(lane == 0, middle, summed) if p == 0 else summed)
        return carry

    lax.fori_loop(0, window_count, one_window, 0, unroll=8)

    def dot_nt(a, b):
        return lax.dot_general(a, b, NT, preferred_element_type=jnp.float32)

    depth = (FOLD + LANE, FOLD, FOLD, FOLD)
    half = LANE // 2
    wide = 2 * LANE
    first = lane < half
    slots = LANE // PACK
    turns = slots // 2
    strip = BAND // 2
    halves = HT // PACK
    own_bin = lax.broadcasted_iota(jnp.int32, (PACK * SB, LANE), 0) // SB
    mask = (own_bin == lax.broadcasted_iota(jnp.int32, (PACK * SB, LANE), 1) % PACK).astype(jnp.float32).astype(
        jnp.bfloat16
    )

    def one_group(tile, n):
        masked = jnp.concatenate([jnp.concatenate([left[tile, n, h]] * PACK, axis=0) * mask for h in range(2)], axis=1)
        product = jnp.dot(masked, right[tile, n], preferred_element_type=jnp.float32)
        product = product.reshape(PACK, 2, SB // 2, LANE)
        a, b = product[:, 0].reshape(PACK * SB // 2, LANE), product[:, 1].reshape(PACK * SB // 2, LANE)
        turned = pltpu.roll(jnp.where(first, b, a), half, 1)
        row = (tile * (FT // PACK) + n) * PACK * SB // 2
        at = pl.ds(row if isinstance(n, int) else pl.multiple_of(row, PACK * SB // 2), PACK * SB // 2)
        cross_real[at, :] = jnp.where(first, a, turned)
        cross_imag[at, :] = jnp.where(first, turned, b)

    def transforms(tile):
        dft_copies[tile].wait()
        bins = slice(tile * HT, (tile + 1) * HT)
        for tile_pair in range(window_count * THEIRS // wide):
            at = slice(tile_pair * wide, (tile_pair + 1) * wide)
            spectra = [dot_nt(dft_ref[k, bins, : depth[k]], theirs[k, at, : depth[k]]) for k in range(4)]
            for n in range(HT // strip):
                for inner in range(wide // LANE):
                    parts = [x[n * strip : (n + 1) * strip, inner * LANE : (inner + 1) * LANE] for x in spectra]
                    power = sum(x * x for x in parts[1:]) + parts[0] * parts[0]
                    level = jnp.sum(power, axis=0, keepdims=True)
                    scale = lax.rsqrt(level * (1.0 / (2 * BAND)) + 1e-06)
                    for parity in range(2):
                        real, imag = parts[parity] * scale, parts[2 + parity] * scale

                        def stacked(x, y):
                            both = [v.reshape(strip // PACK, 1, PACK, LANE) for v in (x, y)]
                            both = jnp.concatenate(both, axis=1).reshape(strip * 2, LANE)
                            return both.astype(jnp.bfloat16)

                        plain, crossed = stacked(real, imag), stacked(-imag, real)
                        turned = pltpu.roll(jnp.where(first, crossed, plain), half, 1)
                        for k, block in enumerate((jnp.where(first, plain, turned), jnp.where(first, turned, crossed))):
                            w = (tile_pair * (wide // LANE) + inner) * 2 + k
                            for m in range(strip // PACK):
                                group = n * (strip // PACK) + m
                                turn = group % slots // 2
                                row = w // turns * LANE + (w + turn) % turns * 2 * PACK
                                right[tile, parity * halves + group, row : row + 2 * PACK, :] = block[
                                    m * 2 * PACK : (m + 1) * 2 * PACK
                                ]

        spectra = [dot_nt(own[k, :, : depth[k]], dft_ref[k, bins, : depth[k]]) for k in range(4)]
        power = sum(x * x for x in spectra[1:]) + spectra[0] * spectra[0]
        same = (
            lax.broadcasted_iota(jnp.int32, (HT, HT), 0) // strip == lax.broadcasted_iota(jnp.int32, (HT, HT), 1) // strip
        ).astype(jnp.float32).astype(jnp.bfloat16)
        level = jnp.dot(power.astype(jnp.bfloat16), same, preferred_element_type=jnp.float32)
        scale = lax.rsqrt(level * (1.0 / (2 * BAND)) + 1e-06)
        for k in range(4):
            white_own[tile, k] = (spectra[k] * scale).astype(jnp.bfloat16)

        low_slot = lane // PACK % 2 == 0
        for parity in range(2):
            for part in range(HT // LANE):
                for h in range(window_count // turns):
                    moved = [[], []]
                    for w in range(turns):
                        row = (h * turns + w) * SB
                        x = [
                            white_own[tile, 2 * c + parity, row : row + SB, part * LANE : (part + 1) * LANE] for c in range(2)
                        ]
                        y = (
                            jnp.where(low_slot, x[0], pltpu.roll(x[1], PACK, 1)),
                            jnp.where(low_slot, pltpu.roll(x[0], LANE - PACK, 1), x[1]),
                        )
                        for k in range(2):
                            moved[k].append(pltpu.roll(y[k], 2 * PACK * w, 1) if w else y[k])
                    for slot in range(slots):
                        turn, k = slot // 2, slot % 2
                        joined = moved[k][0]
                        for w in range(1, turns):
                            joined = jnp.where(lane // (2 * PACK) == (turn + w) % turns, moved[k][w], joined)
                        left[tile, parity * halves + part * slots + slot, h] = joined

    def products(tile):
        def several(n, carry):
            one_group(tile, n)
            return carry

        lax.fori_loop(0, FT // PACK, several, 0, unroll=32)

    for tile in range(TILES):
        transforms(tile)
        if tile:
            products(tile - 1)
    products(TILES - 1)

    lag_copy.wait()
    out_copies = []
    for n in range(SB // 4):
        summed = None
        for k, cross in enumerate((cross_real, cross_imag)):
            columns = jnp.concatenate(
                [cross[pl.ds(2 * n + m, BINS, stride=SB // 2), :].astype(jnp.bfloat16) for m in range(2)], axis=1
            )
            term = jnp.dot(lag_ref[k], columns, preferred_element_type=jnp.float32)
            summed = term if summed is None else summed + term
        turned = summed.T
        for h in range(2):
            station = h * (SB // 2) + 2 * n
            for m in range(2):
                for r in range(ROUNDS):
                    row = ((m * 2 + h) * ROUNDS + r) * SB
                    out_ref[r, (station + m) * SB : (station + m + 1) * SB, :] = turned[row : row + SB]
            rows = slice(station * SB, (station + 2) * SB)
            copy = pltpu.make_async_copy(
                out_ref.at[:, rows, :], out_hbm.at[:, rows, :], out_sems.at[len(out_copies)]
            )
            copy.start()
            out_copies.append(copy)
    for copy in out_copies:
        copy.wait()


def correlate(window_starts, low, taper, dft, lag):
    window_count = window_starts.shape[0]
    planes = low.shape[0]
    in_vmem = pl.BlockSpec(memory_space=pltpu.VMEM)
    anywhere = pl.BlockSpec(memory_space=pl.ANY)
    return pl.pallas_call(
        correlate_kernel,
        in_specs=[pl.BlockSpec(memory_space=pltpu.SMEM), in_vmem, in_vmem, anywhere, anywhere],
        out_specs=anywhere,
        out_shape=jax.ShapeDtypeStruct((ROUNDS, SB * SB, LAGS), jnp.float32),
        scratch_shapes=[
            pltpu.VMEM((ROUNDS, SB * SB, LAGS), jnp.float32),
            pltpu.VMEM(dft.shape, jnp.bfloat16),
            pltpu.VMEM(lag.shape, jnp.bfloat16),
            pltpu.VMEM((planes, ROWS, LANE), jnp.float32),
            pltpu.VMEM((planes, ROWS, LANE), jnp.float32),
            pltpu.VMEM((4, window_count * THEIRS, FOLD + LANE), jnp.bfloat16),
            pltpu.VMEM((4, window_count * SB, FOLD + LANE), jnp.bfloat16),
            pltpu.VMEM((TILES, 4, window_count * SB, HT), jnp.bfloat16),
            pltpu.VMEM((TILES, FT // PACK, 2, SB, LANE), jnp.bfloat16),
            pltpu.VMEM((TILES, FT // PACK, 2 * LANE, LANE), jnp.bfloat16),
            pltpu.VMEM((BINS * SB // 2, LANE), jnp.float32),
            pltpu.VMEM((BINS * SB // 2, LANE), jnp.float32),
            pltpu.SemaphoreType.DMA((TILES,)),
            pltpu.SemaphoreType.DMA,
            pltpu.SemaphoreType.DMA((SB // 2,)),
        ],
        compiler_params=pltpu.CompilerParams(vmem_limit_bytes=60 * 2**20),
    )(window_starts, low, taper, dft, lag)


def body(raw_traces, filter_taps, station_order, window_starts, pairing):
    members = lax.axis_size("sta")
    stations, local_time = raw_traces.shape
    window_count = window_starts.shape[0]
    pieces = local_time // (LANE * DEC)
    line = members // QUAD
    in_vmem = pl.BlockSpec(memory_space=pltpu.VMEM)
    low = pl.pallas_call(
        functools.partial(gather_kernel, members),
        out_shape=jax.ShapeDtypeStruct((members * pieces, ROWS, LANE), jnp.bfloat16),
        in_specs=[
            pl.BlockSpec(memory_space=pl.ANY),
            in_vmem,
            in_vmem,
            pl.BlockSpec(memory_space=pltpu.SMEM),
        ],
        out_specs=pl.BlockSpec(memory_space=pl.ANY),
        scratch_shapes=[
            pltpu.VMEM((stations, local_time), jnp.bfloat16),
            pltpu.VMEM((stations // 2, LANE), jnp.bfloat16),
            pltpu.VMEM((stations // 2, LANE), jnp.bfloat16),
            pltpu.VMEM((line, pieces, stations, LANE), jnp.bfloat16),
            pltpu.VMEM((stations // SB, SB, LANE), jnp.bfloat16),
            pltpu.VMEM(((3 * line + QUAD) * pieces, ROWS, LANE), jnp.bfloat16),
            pltpu.VMEM((line * pieces, ROWS, LANE), jnp.bfloat16),
            pltpu.SemaphoreType.DMA((line * pieces,)),
            pltpu.SemaphoreType.DMA,
            pltpu.SemaphoreType.DMA((2,)),
            pltpu.SemaphoreType.DMA(((line + 1) * pieces,)),
            pltpu.SemaphoreType.DMA((line * pieces,)),
            pltpu.SemaphoreType.DMA(((3 * line + QUAD) * pieces,)),
            pltpu.SemaphoreType.DMA((members * pieces,)),
        ],
        compiler_params=pltpu.CompilerParams(
            collective_id=0, has_side_effects=True, vmem_limit_bytes=60 * 2**20
        ),
    )(raw_traces, filter_taps, station_order.reshape(1, stations), pairing)
    correlated = correlate(
        window_starts,
        low,
        jnp.asarray(taper_table()),
        jnp.asarray(dft_table()),
        jnp.asarray(lag_table(window_count)),
    )
    return correlated.reshape(ROUNDS, SB, SB, LAGS)


def solution(mesh):
    return jax.shard_map(
        body,
        mesh=mesh,
        in_specs=(P("parts", "sta"), P(), P("parts"), P("parts"), P()),
        out_specs=P(None, ("parts", "sta"), None, None),
        check_vma=False,
    )
```

```python
import functools
import math

import jax
import jax.numpy as jnp
import ml_dtypes
import numpy as np
from jax import lax
from jax.experimental import pallas as pl
from jax.experimental.pallas import tpu as pltpu
from jax.sharding import PartitionSpec as P

SB = 16
DEC = 4
TAPS = 256
SEG = 2048
BAND = 64
LAGS = 256
ROUNDS = 4
BINS = 1024
LANE = 128
SPAN = LANE * DEC + TAPS
GROUPS = ROUNDS + 1
ROWS = GROUPS * SB
THEIRS = ROUNDS * SB
FOLD = SEG // 4
FT = 512
HT = FT // 2
TILES = BINS // FT
PACK = 8
NT = (((1,), (1,)), ((), ()))
QUAD = 4
MESH = pl.DeviceIdType.MESH


def taper_table():
    sample = np.arange(-LANE, 7 * LANE)
    return (0.5 - 0.5 * np.cos(sample * (2.0 * math.pi / SEG))).astype(np.float32).reshape(8, LANE)


def dft_table():
    sample = np.arange(FOLD)
    kinds = []
    for wave in (np.cos, lambda a: -np.sin(a)):
        for parity in range(2):
            frequency = 2 * np.arange(BINS // 2) + parity
            table = np.zeros((BINS // 2, FOLD + LANE))
            table[:, :FOLD] = wave((sample[None, :] * frequency[:, None] % SEG) * (2.0 * math.pi / SEG))
            middle = np.round(wave((frequency * FOLD % SEG) * (2.0 * math.pi / SEG)))
            if wave is np.cos:
                table[:, 0] = 0.5
                table[:, FOLD] = middle
            else:
                table[:, 0] = middle
            kinds.append(table)
    return np.stack(kinds).astype(np.float32).astype(ml_dtypes.bfloat16)


def lag_table(window_count):
    frequency = 2 * np.arange(BINS // 2).reshape(TILES, 1, HT) + np.arange(2).reshape(1, 2, 1)
    frequency = frequency.reshape(BINS)
    offset = np.arange(LAGS) - LAGS // 2 + SEG
    angles = (frequency[None, :] * offset[:, None] % SEG) * (2.0 * math.pi / SEG)
    scale = 1.0 / math.sqrt(BINS * window_count)
    both = np.stack([np.cos(angles) * scale, -np.sin(angles) * scale])
    return both.astype(np.float32).astype(ml_dtypes.bfloat16)


def gather_kernel(
    members,
    raw_ref,
    taps_ref,
    order_ref,
    pairing_ref,
    out_ref,
    raw,
    tail,
    halo,
    column,
    private,
    picked,
    kept,
    keep_sems,
    raw_sem,
    halo_sems,
    line_send,
    line_recv,
    pick_send,
    pick_recv,
):
    me = lax.axis_index("sta")
    stations, local_time = raw_ref.shape
    line, pieces = column.shape[:2]
    rank, lead = me // QUAD, me % QUAD
    turn = 1 - 2 * lax.rem(me, 2)
    twin = me + turn
    across = rank * QUAD + lax.rem(lead + 2, QUAD)
    others = (across, across + turn, twin)
    after = lax.rem(me + 1, members)

    def of_rank(choose):
        chosen = choose(0)
        for r in range(1, line):
            chosen = jnp.where(rank == r, choose(r), chosen)
        return chosen

    def arrivals(r):
        known = sorted((abs(x - r), -piece, x) for x in range(line) if x != r for piece in range(pieces))
        return [(x, -negative) for _, negative, x in known]

    expected = [
        (of_rank(lambda r: arrivals(r)[n][0]), of_rank(lambda r: arrivals(r)[n][1]))
        for n in range((line - 1) * pieces)
    ]

    raw_copy = pltpu.make_async_copy(raw_ref, raw, raw_sem)
    raw_copy.start()

    barrier = pltpu.get_barrier_semaphore()
    for peer in others:
        pl.semaphore_signal(barrier, inc=1, device_id={"sta": peer}, device_id_type=MESH)
    greeters = len(others)
    for ahead, there in ((QUAD, rank < line - 1), (-QUAD, rank > 0), (1, me < members - 1), (-1, me > 0)):
        greeters = greeters + jnp.where(there, 1, 0)

        @pl.when(there)
        def _():
            pl.semaphore_signal(barrier, inc=1, device_id={"sta": me + ahead}, device_id_type=MESH)

    relayed = line > 3
    at_end = (rank == 0) | (rank == line - 1)
    beside_end = (rank == 1) | (rank == line - 2)
    joined = rank + jnp.where((rank == 0) | (rank == line - 2), 1, -1)
    near_end = at_end | beside_end
    if relayed:

        @pl.when(near_end)
        def _():
            for n in range(1, QUAD):
                peer = joined * QUAD + lax.rem(lead + n, QUAD)
                pl.semaphore_signal(barrier, inc=1, device_id={"sta": peer}, device_id_type=MESH)

    mirror = (
        lax.broadcasted_iota(jnp.int32, (TAPS, TAPS), 0) + lax.broadcasted_iota(jnp.int32, (TAPS, TAPS), 1) == TAPS - 1
    ).astype(jnp.float32).astype(jnp.bfloat16)
    taps = jnp.broadcast_to(taps_ref[...].astype(jnp.float32).reshape(1, TAPS), (SB, TAPS)).astype(jnp.bfloat16)
    taps = jnp.dot(taps, mirror, preferred_element_type=jnp.float32)[:1]
    banded = jnp.concatenate([taps, jnp.zeros((1, SPAN - TAPS), jnp.float32)], axis=1)
    banded = jnp.broadcast_to(banded, (LANE, SPAN))
    banded = pltpu.roll(banded, DEC, 1, stride=DEC, stride_axis=0).astype(jnp.bfloat16)
    picks = (lax.broadcasted_iota(jnp.int32, (stations, stations), 0) == order_ref[...]).astype(jnp.float32)
    picks = picks.T.astype(jnp.bfloat16)

    dims = (((1,), (1,)), ((), ()))
    lane = lax.broadcasted_iota(jnp.int32, (1, LANE), 1)
    half = LANE // 2
    raw_copy.wait()
    spilled = lax.dot_general(
        raw[:, local_time - TAPS :], banded[:, :TAPS], dims, preferred_element_type=jnp.float32
    )
    tail[...] = jnp.where(
        lane < half, spilled[: stations // 2], pltpu.roll(spilled[stations // 2 :], half, 1)
    ).astype(jnp.bfloat16)

    pl.semaphore_wait(barrier, greeters + (jnp.where(near_end, QUAD - 1, 0) if relayed else 0))

    halo_copy = pltpu.make_async_remote_copy(
        src_ref=tail,
        dst_ref=halo,
        send_sem=halo_sems.at[0],
        recv_sem=halo_sems.at[1],
        device_id={"sta": after},
        device_id_type=MESH,
    )

    @pl.when(me < members - 1)
    def _():
        halo_copy.start()

    def line_copy(source, piece, n, peer):
        return pltpu.make_async_remote_copy(
            src_ref=column.at[source, piece],
            dst_ref=column.at[source, piece],
            send_sem=line_send.at[n],
            recv_sem=line_recv.at[source * pieces + piece],
            device_id={"sta": peer * QUAD + lead},
            device_id_type=MESH,
        )

    passed = []

    def pass_on(source, piece, ahead, there):
        copy = line_copy(source, piece, len(passed), rank + ahead)
        passed.append((copy, there))

        @pl.when(there)
        def _():
            copy.start()

    picks_sent = []

    def share(source, piece, samples, peers, there):
        private[...] = samples.reshape(private.shape)
        plane = (source * QUAD + lead) * pieces + piece
        for peer in peers:
            slot = len(picks_sent)
            for g, block in enumerate([pairing_ref[r, peer] for r in range(ROUNDS)] + [peer]):
                picked[slot, g * SB : (g + 1) * SB, :] = private[block]
            copy = pltpu.make_async_remote_copy(
                src_ref=picked.at[slot],
                dst_ref=out_ref.at[plane],
                send_sem=pick_send.at[slot],
                recv_sem=pick_recv.at[plane],
                device_id={"sta": peer},
                device_id_type=MESH,
            )
            copy.start()
            picks_sent.append(there)

    kept_there = []

    def keep(source, piece, there):
        slot = len(kept_there)
        plane = (source * QUAD + lead) * pieces + piece
        for g, block in enumerate([pairing_ref[r, me] for r in range(ROUNDS)] + [me]):
            kept[slot, g * SB : (g + 1) * SB, :] = private[block]
        pltpu.make_async_copy(kept.at[slot], out_ref.at[plane], keep_sems.at[slot]).start()
        kept_there.append(there)

    def filtered(piece, first, spill=None):
        summed = lax.dot_general(
            raw[:, max(first, 0) : first + SPAN],
            banded[:, max(-first, 0) :],
            dims,
            preferred_element_type=jnp.float32,
        )
        if spill is not None:
            summed = summed + spill
        ordered = jnp.dot(picks, summed.astype(jnp.bfloat16), preferred_element_type=jnp.float32).astype(jnp.bfloat16)
        column[rank, piece] = ordered
        pass_on(rank, piece, 1, rank < line - 1)
        pass_on(rank, piece, -1, rank > 0)
        share(rank, piece, ordered, others, None)
        keep(rank, piece, None)

    for piece in range(pieces - 1, 0, -1):
        filtered(piece, piece * LANE * DEC - TAPS)

    @pl.when(me > 0)
    def _():
        halo_copy.wait_recv()

    @pl.when(me == 0)
    def _():
        halo[...] = jnp.zeros_like(halo)

    spill = halo[...].astype(jnp.float32)
    spill = [jnp.where(lane < half, x, 0.0) for x in (spill, pltpu.roll(spill, half, 1))]
    filtered(0, -TAPS, jnp.concatenate(spill, axis=0))

    for n, (source, piece) in enumerate(expected):
        from_below = source < rank
        there = (from_below & (rank < line - 1)) | (jnp.logical_not(from_below) & (rank > 0))
        ahead = jnp.where(from_below, 1, -1)
        if relayed and n >= len(expected) - pieces:
            inside = jnp.logical_not(at_end)

            @pl.when(inside)
            def _():
                line_copy(source, piece, 0, source).wait_recv()

            pass_on(source, piece, ahead, there & jnp.logical_not(near_end))

            @pl.when(beside_end)
            def _():
                ends = [joined * QUAD + lax.rem(lead + k, QUAD) for k in range(QUAD)]
                share(source, piece, column[source, piece], ends, beside_end)

            @pl.when(inside)
            def _():
                share(source, piece, column[source, piece], others, inside)
                keep(source, piece, inside)
        else:
            line_copy(source, piece, 0, source).wait_recv()
            pass_on(source, piece, ahead, there)
            share(source, piece, column[source, piece], others, None)
            keep(source, piece, None)

    def landed(plane):
        pltpu.make_async_remote_copy(
            src_ref=picked.at[0],
            dst_ref=out_ref.at[plane],
            send_sem=pick_send.at[0],
            recv_sem=pick_recv.at[plane],
            device_id={"sta": twin},
            device_id_type=MESH,
        ).wait_recv()

    for source in range(line):
        for piece in range(pieces):
            for peer in others:
                landed((peer - rank * QUAD + source * QUAD) * pieces + piece)
    if relayed:

        @pl.when(at_end)
        def _():
            for piece in range(pieces):
                landed(((line - 1 - rank) * QUAD + lead) * pieces + piece)

    leaving = [
        (
            pltpu.make_async_remote_copy(
                src_ref=picked.at[slot],
                dst_ref=out_ref.at[0],
                send_sem=pick_send.at[slot],
                recv_sem=pick_recv.at[0],
                device_id={"sta": twin},
                device_id_type=MESH,
            ),
            there,
        )
        for slot, there in enumerate(picks_sent)
    ]
    def kept_done(slot):
        pltpu.make_async_copy(kept.at[slot], out_ref.at[0], keep_sems.at[slot]).wait()

    for slot, there in enumerate(kept_there):
        if there is None:
            kept_done(slot)
        else:

            @pl.when(there)
            def _():
                kept_done(slot)

    for copy, there in leaving + passed:
        if there is None:
            copy.wait_send()
        else:

            @pl.when(there)
            def _():
                copy.wait_send()

    @pl.when(me < members - 1)
    def _():
        halo_copy.wait_send()


def correlate_kernel(
    starts_ref,
    low_ref,
    taper_ref,
    dft_hbm,
    lag_hbm,
    out_hbm,
    out_ref,
    dft_ref,
    lag_ref,
    ahead,
    back,
    theirs,
    own,
    white_own,
    left,
    right,
    cross_real,
    cross_imag,
    dft_sems,
    lag_sem,
    out_sems,
):
    planes = low_ref.shape[0]
    window_count = starts_ref.shape[0]
    lane = lax.broadcasted_iota(jnp.int32, (1, LANE), 1)
    dft_copies = [
        pltpu.make_async_copy(
            dft_hbm.at[:, n * HT : (n + 1) * HT, :], dft_ref.at[:, n * HT : (n + 1) * HT, :], dft_sems.at[n]
        )
        for n in range(TILES)
    ]
    lag_copy = pltpu.make_async_copy(lag_hbm, lag_ref, lag_sem)

    for copy in dft_copies:
        copy.start()
    lag_copy.start()
    mirror = (
        lax.broadcasted_iota(jnp.int32, (LANE, LANE), 0) + lax.broadcasted_iota(jnp.int32, (LANE, LANE), 1) == LANE
    ).astype(jnp.float32).astype(jnp.bfloat16)

    def one_plane(n, carry):
        samples = low_ref[n]
        ahead[n] = samples.astype(jnp.float32)
        turned = jnp.dot(samples, mirror, preferred_element_type=jnp.float32)
        later = low_ref[jnp.minimum(n + 1, planes - 1)].astype(jnp.float32)
        later = jnp.where(n + 1 < planes, later, jnp.zeros_like(later))
        back[planes - 1 - n] = jnp.where(lane == 0, later, turned)
        return carry

    lax.fori_loop(0, planes, one_plane, 0, unroll=16)

    def one_window(w, carry):
        start = starts_ref[w]
        plane, rest = start // LANE, start % LANE
        taper = taper_ref[...]
        fore = pltpu.roll(taper, rest, 1)
        hind = pltpu.roll(taper, (LANE - rest) % LANE, 1)
        span = SEG // LANE
        rise = [jnp.where(lane >= rest, fore[p + 1 : p + 2], fore[p : p + 1]) for p in range(FOLD // LANE + 1)]
        fall = [
            jnp.where(lane < LANE - rest, hind[p + 1 : p + 2], hind[p + 2 : p + 3]) for p in range(FOLD // LANE)
        ]
        at = pl.ds(pl.multiple_of(w * THEIRS, SB), THEIRS)
        own_at = pl.ds(pl.multiple_of(w * SB, SB), SB)

        def put(kind, p, values):
            values = values.astype(jnp.bfloat16)
            lanes = slice(p * LANE, (p + 1) * LANE)
            theirs[kind, at, lanes] = values[:THEIRS]
            own[kind, own_at, lanes] = values[THEIRS:]

        last = FOLD // LANE
        a = rise[last] * ahead[plane + last]
        b = (1.0 - rise[last]) * ahead[plane + last + span // 2]
        put(0, last, a + b)
        middle = a - b
        for p in range(FOLD // LANE):
            first = ahead[plane + p]
            if p == 0:
                first = jnp.where(lane < rest, ahead[jnp.minimum(plane + span, planes - 1)], first)
            a = rise[p] * first
            b = (1.0 - rise[p]) * ahead[plane + span // 2 + p]
            c = fall[p] * back[planes - plane - span + p]
            d = (1.0 - fall[p]) * back[planes - plane - span // 2 + p]
            same, apart = a + b, a - b
            same_turned, apart_turned = d + c, d - c
            put(0, p, same + same_turned)
            put(1, p, apart - apart_turned)
            put(2, p, same - same_turned)
            summed = apart + apart_turned
            put(3, p, jnp.where(lane == 0, middle, summed) if p == 0 else summed)
        return carry

    lax.fori_loop(0, window_count, one_window, 0, unroll=8)

    def dot_nt(a, b):
        return lax.dot_general(a, b, NT, preferred_element_type=jnp.float32)

    depth = (FOLD + LANE, FOLD, FOLD, FOLD)
    half = LANE // 2
    wide = 2 * LANE
    first = lane < half
    slots = LANE // PACK
    turns = slots // 2
    strip = BAND // 2
    halves = HT // PACK
    own_bin = lax.broadcasted_iota(jnp.int32, (PACK * SB, LANE), 0) // SB
    mask = (own_bin == lax.broadcasted_iota(jnp.int32, (PACK * SB, LANE), 1) % PACK).astype(jnp.float32).astype(
        jnp.bfloat16
    )

    def one_group(tile, n):
        masked = jnp.concatenate([jnp.concatenate([left[tile, n, h]] * PACK, axis=0) * mask for h in range(2)], axis=1)
        product = jnp.dot(masked, right[tile, n], preferred_element_type=jnp.float32)
        product = product.reshape(PACK, 2, SB // 2, LANE)
        a, b = product[:, 0].reshape(PACK * SB // 2, LANE), product[:, 1].reshape(PACK * SB // 2, LANE)
        turned = pltpu.roll(jnp.where(first, b, a), half, 1)
        row = (tile * (FT // PACK) + n) * PACK * SB // 2
        at = pl.ds(row if isinstance(n, int) else pl.multiple_of(row, PACK * SB // 2), PACK * SB // 2)
        cross_real[at, :] = jnp.where(first, a, turned)
        cross_imag[at, :] = jnp.where(first, turned, b)

    def transforms(tile):
        dft_copies[tile].wait()
        bins = slice(tile * HT, (tile + 1) * HT)
        for tile_pair in range(window_count * THEIRS // wide):
            at = slice(tile_pair * wide, (tile_pair + 1) * wide)
            spectra = [dot_nt(dft_ref[k, bins, : depth[k]], theirs[k, at, : depth[k]]) for k in range(4)]
            for n in range(HT // strip):
                for inner in range(wide // LANE):
                    parts = [x[n * strip : (n + 1) * strip, inner * LANE : (inner + 1) * LANE] for x in spectra]
                    power = sum(x * x for x in parts[1:]) + parts[0] * parts[0]
                    level = jnp.sum(power, axis=0, keepdims=True)
                    scale = lax.rsqrt(level * (1.0 / (2 * BAND)) + 1e-06)
                    for parity in range(2):
                        real, imag = parts[parity] * scale, parts[2 + parity] * scale

                        def stacked(x, y):
                            both = [v.reshape(strip // PACK, 1, PACK, LANE) for v in (x, y)]
                            both = jnp.concatenate(both, axis=1).reshape(strip * 2, LANE)
                            return both.astype(jnp.bfloat16)

                        plain, crossed = stacked(real, imag), stacked(-imag, real)
                        turned = pltpu.roll(jnp.where(first, crossed, plain), half, 1)
                        for k, block in enumerate((jnp.where(first, plain, turned), jnp.where(first, turned, crossed))):
                            w = (tile_pair * (wide // LANE) + inner) * 2 + k
                            for m in range(strip // PACK):
                                group = n * (strip // PACK) + m
                                turn = group % slots // 2
                                row = w // turns * LANE + (w + turn) % turns * 2 * PACK
                                right[tile, parity * halves + group, row : row + 2 * PACK, :] = block[
                                    m * 2 * PACK : (m + 1) * 2 * PACK
                                ]

        spectra = [dot_nt(own[k, :, : depth[k]], dft_ref[k, bins, : depth[k]]) for k in range(4)]
        power = sum(x * x for x in spectra[1:]) + spectra[0] * spectra[0]
        same = (
            lax.broadcasted_iota(jnp.int32, (HT, HT), 0) // strip == lax.broadcasted_iota(jnp.int32, (HT, HT), 1) // strip
        ).astype(jnp.float32).astype(jnp.bfloat16)
        level = jnp.dot(power.astype(jnp.bfloat16), same, preferred_element_type=jnp.float32)
        scale = lax.rsqrt(level * (1.0 / (2 * BAND)) + 1e-06)
        for k in range(4):
            white_own[tile, k] = (spectra[k] * scale).astype(jnp.bfloat16)

        low_slot = lane // PACK % 2 == 0
        for parity in range(2):
            for part in range(HT // LANE):
                for h in range(window_count // turns):
                    moved = [[], []]
                    for w in range(turns):
                        row = (h * turns + w) * SB
                        x = [
                            white_own[tile, 2 * c + parity, row : row + SB, part * LANE : (part + 1) * LANE] for c in range(2)
                        ]
                        y = (
                            jnp.where(low_slot, x[0], pltpu.roll(x[1], PACK, 1)),
                            jnp.where(low_slot, pltpu.roll(x[0], LANE - PACK, 1), x[1]),
                        )
                        for k in range(2):
                            moved[k].append(pltpu.roll(y[k], 2 * PACK * w, 1) if w else y[k])
                    for slot in range(slots):
                        turn, k = slot // 2, slot % 2
                        joined = moved[k][0]
                        for w in range(1, turns):
                            joined = jnp.where(lane // (2 * PACK) == (turn + w) % turns, moved[k][w], joined)
                        left[tile, parity * halves + part * slots + slot, h] = joined

    def products(tile):
        def several(n, carry):
            one_group(tile, n)
            return carry

        lax.fori_loop(0, FT // PACK, several, 0, unroll=32)

    for tile in range(TILES):
        transforms(tile)
        if tile:
            products(tile - 1)
    products(TILES - 1)

    lag_copy.wait()
    out_copies = []
    for n in range(SB // 4):
        summed = None
        for k, cross in enumerate((cross_real, cross_imag)):
            columns = jnp.concatenate(
                [cross[pl.ds(2 * n + m, BINS, stride=SB // 2), :].astype(jnp.bfloat16) for m in range(2)], axis=1
            )
            term = jnp.dot(lag_ref[k], columns, preferred_element_type=jnp.float32)
            summed = term if summed is None else summed + term
        turned = summed.T
        for h in range(2):
            station = h * (SB // 2) + 2 * n
            for m in range(2):
                for r in range(ROUNDS):
                    row = ((m * 2 + h) * ROUNDS + r) * SB
                    out_ref[r, (station + m) * SB : (station + m + 1) * SB, :] = turned[row : row + SB]
            rows = slice(station * SB, (station + 2) * SB)
            copy = pltpu.make_async_copy(
                out_ref.at[:, rows, :], out_hbm.at[:, rows, :], out_sems.at[len(out_copies)]
            )
            copy.start()
            out_copies.append(copy)
    for copy in out_copies:
        copy.wait()


def correlate(window_starts, low, taper, dft, lag):
    window_count = window_starts.shape[0]
    planes = low.shape[0]
    in_vmem = pl.BlockSpec(memory_space=pltpu.VMEM)
    anywhere = pl.BlockSpec(memory_space=pl.ANY)
    return pl.pallas_call(
        correlate_kernel,
        in_specs=[pl.BlockSpec(memory_space=pltpu.SMEM), in_vmem, in_vmem, anywhere, anywhere],
        out_specs=anywhere,
        out_shape=jax.ShapeDtypeStruct((ROUNDS, SB * SB, LAGS), jnp.float32),
        scratch_shapes=[
            pltpu.VMEM((ROUNDS, SB * SB, LAGS), jnp.float32),
            pltpu.VMEM(dft.shape, jnp.bfloat16),
            pltpu.VMEM(lag.shape, jnp.bfloat16),
            pltpu.VMEM((planes, ROWS, LANE), jnp.float32),
            pltpu.VMEM((planes, ROWS, LANE), jnp.float32),
            pltpu.VMEM((4, window_count * THEIRS, FOLD + LANE), jnp.bfloat16),
            pltpu.VMEM((4, window_count * SB, FOLD + LANE), jnp.bfloat16),
            pltpu.VMEM((TILES, 4, window_count * SB, HT), jnp.bfloat16),
            pltpu.VMEM((TILES, FT // PACK, 2, SB, LANE), jnp.bfloat16),
            pltpu.VMEM((TILES, FT // PACK, 2 * LANE, LANE), jnp.bfloat16),
            pltpu.VMEM((BINS * SB // 2, LANE), jnp.float32),
            pltpu.VMEM((BINS * SB // 2, LANE), jnp.float32),
            pltpu.SemaphoreType.DMA((TILES,)),
            pltpu.SemaphoreType.DMA,
            pltpu.SemaphoreType.DMA((SB // 2,)),
        ],
        compiler_params=pltpu.CompilerParams(vmem_limit_bytes=60 * 2**20),
    )(window_starts, low, taper, dft, lag)


def body(raw_traces, filter_taps, station_order, window_starts, pairing):
    members = lax.axis_size("sta")
    stations, local_time = raw_traces.shape
    window_count = window_starts.shape[0]
    pieces = local_time // (LANE * DEC)
    line = members // QUAD
    in_vmem = pl.BlockSpec(memory_space=pltpu.VMEM)
    low = pl.pallas_call(
        functools.partial(gather_kernel, members),
        out_shape=jax.ShapeDtypeStruct((members * pieces, ROWS, LANE), jnp.bfloat16),
        in_specs=[
            pl.BlockSpec(memory_space=pl.ANY),
            in_vmem,
            in_vmem,
            pl.BlockSpec(memory_space=pltpu.SMEM),
        ],
        out_specs=pl.BlockSpec(memory_space=pl.ANY),
        scratch_shapes=[
            pltpu.VMEM((stations, local_time), jnp.bfloat16),
            pltpu.VMEM((stations // 2, LANE), jnp.bfloat16),
            pltpu.VMEM((stations // 2, LANE), jnp.bfloat16),
            pltpu.VMEM((line, pieces, stations, LANE), jnp.bfloat16),
            pltpu.VMEM((stations // SB, SB, LANE), jnp.bfloat16),
            pltpu.VMEM(((3 * line + QUAD) * pieces, ROWS, LANE), jnp.bfloat16),
            pltpu.VMEM((line * pieces, ROWS, LANE), jnp.bfloat16),
            pltpu.SemaphoreType.DMA((line * pieces,)),
            pltpu.SemaphoreType.DMA,
            pltpu.SemaphoreType.DMA((2,)),
            pltpu.SemaphoreType.DMA(((line + 1) * pieces,)),
            pltpu.SemaphoreType.DMA((line * pieces,)),
            pltpu.SemaphoreType.DMA(((3 * line + QUAD) * pieces,)),
            pltpu.SemaphoreType.DMA((members * pieces,)),
        ],
        compiler_params=pltpu.CompilerParams(
            collective_id=0, has_side_effects=True, vmem_limit_bytes=60 * 2**20
        ),
    )(raw_traces, filter_taps, station_order.reshape(1, stations), pairing)
    correlated = correlate(
        window_starts,
        low,
        jnp.asarray(taper_table()),
        jnp.asarray(dft_table()),
        jnp.asarray(lag_table(window_count)),
    )
    return correlated.reshape(ROUNDS, SB, SB, LAGS)


def solution(mesh):
    return jax.shard_map(
        body,
        mesh=mesh,
        in_specs=(P("parts", "sta"), P(), P("parts"), P("parts"), P()),
        out_specs=P(None, ("parts", "sta"), None, None),
        check_vma=False,
    )
```

```python
import functools
import math

import jax
import jax.numpy as jnp
import ml_dtypes
import numpy as np
from jax import lax
from jax.experimental import pallas as pl
from jax.experimental.pallas import tpu as pltpu
from jax.sharding import PartitionSpec as P

SB = 16
DEC = 4
TAPS = 256
SEG = 2048
BAND = 64
LAGS = 256
ROUNDS = 4
BINS = 1024
LANE = 128
SPAN = LANE * DEC + TAPS
GROUPS = ROUNDS + 1
ROWS = GROUPS * SB
THEIRS = ROUNDS * SB
FOLD = SEG // 4
FT = 512
HT = FT // 2
TILES = BINS // FT
PACK = 8
NT = (((1,), (1,)), ((), ()))
QUAD = 4
MESH = pl.DeviceIdType.MESH


def taper_table():
    sample = np.arange(-LANE, 7 * LANE)
    return (0.5 - 0.5 * np.cos(sample * (2.0 * math.pi / SEG))).astype(np.float32).reshape(8, LANE)


def dft_table():
    sample = np.arange(FOLD)
    kinds = []
    for wave in (np.cos, lambda a: -np.sin(a)):
        for parity in range(2):
            frequency = 2 * np.arange(BINS // 2) + parity
            table = np.zeros((BINS // 2, FOLD + LANE))
            table[:, :FOLD] = wave((sample[None, :] * frequency[:, None] % SEG) * (2.0 * math.pi / SEG))
            middle = np.round(wave((frequency * FOLD % SEG) * (2.0 * math.pi / SEG)))
            if wave is np.cos:
                table[:, 0] = 0.5
                table[:, FOLD] = middle
            else:
                table[:, 0] = middle
            kinds.append(table)
    return np.stack(kinds).astype(np.float32).astype(ml_dtypes.bfloat16)


def lag_table(window_count):
    frequency = 2 * np.arange(BINS // 2).reshape(TILES, 1, HT) + np.arange(2).reshape(1, 2, 1)
    frequency = frequency.reshape(BINS)
    offset = np.arange(LAGS) - LAGS // 2 + SEG
    angles = (frequency[None, :] * offset[:, None] % SEG) * (2.0 * math.pi / SEG)
    scale = 1.0 / math.sqrt(BINS * window_count)
    both = np.stack([np.cos(angles) * scale, -np.sin(angles) * scale])
    return both.astype(np.float32).astype(ml_dtypes.bfloat16)


def gather_kernel(
    members,
    raw_ref,
    taps_ref,
    order_ref,
    pairing_ref,
    out_ref,
    raw,
    tail,
    halo,
    column,
    private,
    picked,
    kept,
    keep_sems,
    raw_sem,
    halo_sems,
    line_send,
    line_recv,
    pick_send,
    pick_recv,
):
    me = lax.axis_index("sta")
    stations, local_time = raw_ref.shape
    line, pieces = column.shape[:2]
    rank, lead = me // QUAD, me % QUAD
    turn = 1 - 2 * lax.rem(me, 2)
    twin = me + turn
    across = rank * QUAD + lax.rem(lead + 2, QUAD)
    others = (across, across + turn, twin)
    after = lax.rem(me + 1, members)

    def of_rank(choose):
        chosen = choose(0)
        for r in range(1, line):
            chosen = jnp.where(rank == r, choose(r), chosen)
        return chosen

    def arrivals(r):
        known = sorted((abs(x - r), -piece, x) for x in range(line) if x != r for piece in range(pieces))
        return [(x, -negative) for _, negative, x in known]

    expected = [
        (of_rank(lambda r: arrivals(r)[n][0]), of_rank(lambda r: arrivals(r)[n][1]))
        for n in range((line - 1) * pieces)
    ]

    raw_copy = pltpu.make_async_copy(raw_ref, raw, raw_sem)
    raw_copy.start()

    barrier = pltpu.get_barrier_semaphore()
    for peer in others:
        pl.semaphore_signal(barrier, inc=1, device_id={"sta": peer}, device_id_type=MESH)
    greeters = len(others)
    for ahead, there in ((QUAD, rank < line - 1), (-QUAD, rank > 0), (1, me < members - 1), (-1, me > 0)):
        greeters = greeters + jnp.where(there, 1, 0)

        @pl.when(there)
        def _():
            pl.semaphore_signal(barrier, inc=1, device_id={"sta": me + ahead}, device_id_type=MESH)

    relayed = line > 3
    at_end = (rank == 0) | (rank == line - 1)
    beside_end = (rank == 1) | (rank == line - 2)
    joined = rank + jnp.where((rank == 0) | (rank == line - 2), 1, -1)
    near_end = at_end | beside_end
    if relayed:

        @pl.when(near_end)
        def _():
            for n in range(1, QUAD):
                peer = joined * QUAD + lax.rem(lead + n, QUAD)
                pl.semaphore_signal(barrier, inc=1, device_id={"sta": peer}, device_id_type=MESH)

    mirror = (
        lax.broadcasted_iota(jnp.int32, (TAPS, TAPS), 0) + lax.broadcasted_iota(jnp.int32, (TAPS, TAPS), 1) == TAPS - 1
    ).astype(jnp.float32).astype(jnp.bfloat16)
    taps = jnp.broadcast_to(taps_ref[...].astype(jnp.float32).reshape(1, TAPS), (SB, TAPS)).astype(jnp.bfloat16)
    taps = jnp.dot(taps, mirror, preferred_element_type=jnp.float32)[:1]
    banded = jnp.concatenate([taps, jnp.zeros((1, SPAN - TAPS), jnp.float32)], axis=1)
    banded = jnp.broadcast_to(banded, (LANE, SPAN))
    banded = pltpu.roll(banded, DEC, 1, stride=DEC, stride_axis=0).astype(jnp.bfloat16)
    picks = (lax.broadcasted_iota(jnp.int32, (stations, stations), 0) == order_ref[...]).astype(jnp.float32)
    picks = picks.T.astype(jnp.bfloat16)

    dims = (((1,), (1,)), ((), ()))
    lane = lax.broadcasted_iota(jnp.int32, (1, LANE), 1)
    half = LANE // 2
    raw_copy.wait()
    spilled = lax.dot_general(
        raw[:, local_time - TAPS :], banded[:, :TAPS], dims, preferred_element_type=jnp.float32
    )
    tail[...] = jnp.where(
        lane < half, spilled[: stations // 2], pltpu.roll(spilled[stations // 2 :], half, 1)
    ).astype(jnp.bfloat16)

    pl.semaphore_wait(barrier, greeters + (jnp.where(near_end, QUAD - 1, 0) if relayed else 0))

    halo_copy = pltpu.make_async_remote_copy(
        src_ref=tail,
        dst_ref=halo,
        send_sem=halo_sems.at[0],
        recv_sem=halo_sems.at[1],
        device_id={"sta": after},
        device_id_type=MESH,
    )

    @pl.when(me < members - 1)
    def _():
        halo_copy.start()

    def line_copy(source, piece, n, peer):
        return pltpu.make_async_remote_copy(
            src_ref=column.at[source, piece],
            dst_ref=column.at[source, piece],
            send_sem=line_send.at[n],
            recv_sem=line_recv.at[source * pieces + piece],
            device_id={"sta": peer * QUAD + lead},
            device_id_type=MESH,
        )

    passed = []

    def pass_on(source, piece, ahead, there):
        copy = line_copy(source, piece, len(passed), rank + ahead)
        passed.append((copy, there))

        @pl.when(there)
        def _():
            copy.start()

    picks_sent = []

    def share(source, piece, samples, peers, there):
        private[...] = samples.reshape(private.shape)
        plane = (source * QUAD + lead) * pieces + piece
        for peer in peers:
            slot = len(picks_sent)
            for g, block in enumerate([pairing_ref[r, peer] for r in range(ROUNDS)] + [peer]):
                picked[slot, g * SB : (g + 1) * SB, :] = private[block]
            copy = pltpu.make_async_remote_copy(
                src_ref=picked.at[slot],
                dst_ref=out_ref.at[plane],
                send_sem=pick_send.at[slot],
                recv_sem=pick_recv.at[plane],
                device_id={"sta": peer},
                device_id_type=MESH,
            )
            copy.start()
            picks_sent.append(there)

    kept_there = []

    def keep(source, piece, there):
        slot = len(kept_there)
        plane = (source * QUAD + lead) * pieces + piece
        for g, block in enumerate([pairing_ref[r, me] for r in range(ROUNDS)] + [me]):
            kept[slot, g * SB : (g + 1) * SB, :] = private[block]
        pltpu.make_async_copy(kept.at[slot], out_ref.at[plane], keep_sems.at[slot]).start()
        kept_there.append(there)

    def filtered(piece, first, spill=None):
        summed = lax.dot_general(
            raw[:, max(first, 0) : first + SPAN],
            banded[:, max(-first, 0) :],
            dims,
            preferred_element_type=jnp.float32,
        )
        if spill is not None:
            summed = summed + spill
        ordered = jnp.dot(picks, summed.astype(jnp.bfloat16), preferred_element_type=jnp.float32).astype(jnp.bfloat16)
        column[rank, piece] = ordered
        pass_on(rank, piece, 1, rank < line - 1)
        pass_on(rank, piece, -1, rank > 0)
        share(rank, piece, ordered, others, None)
        keep(rank, piece, None)

    for piece in range(pieces - 1, 0, -1):
        filtered(piece, piece * LANE * DEC - TAPS)

    @pl.when(me > 0)
    def _():
        halo_copy.wait_recv()

    @pl.when(me == 0)
    def _():
        halo[...] = jnp.zeros_like(halo)

    spill = halo[...].astype(jnp.float32)
    spill = [jnp.where(lane < half, x, 0.0) for x in (spill, pltpu.roll(spill, half, 1))]
    filtered(0, -TAPS, jnp.concatenate(spill, axis=0))

    for n, (source, piece) in enumerate(expected):
        from_below = source < rank
        there = (from_below & (rank < line - 1)) | (jnp.logical_not(from_below) & (rank > 0))
        ahead = jnp.where(from_below, 1, -1)
        if relayed and n >= len(expected) - pieces:
            inside = jnp.logical_not(at_end)

            @pl.when(inside)
            def _():
                line_copy(source, piece, 0, source).wait_recv()

            pass_on(source, piece, ahead, there & jnp.logical_not(near_end))

            @pl.when(beside_end)
            def _():
                ends = [joined * QUAD + lax.rem(lead + k, QUAD) for k in range(QUAD)]
                share(source, piece, column[source, piece], ends, beside_end)

            @pl.when(inside)
            def _():
                share(source, piece, column[source, piece], others, inside)
                keep(source, piece, inside)
        else:
            line_copy(source, piece, 0, source).wait_recv()
            pass_on(source, piece, ahead, there)
            share(source, piece, column[source, piece], others, None)
            keep(source, piece, None)

    def landed(plane):
        pltpu.make_async_remote_copy(
            src_ref=picked.at[0],
            dst_ref=out_ref.at[plane],
            send_sem=pick_send.at[0],
            recv_sem=pick_recv.at[plane],
            device_id={"sta": twin},
            device_id_type=MESH,
        ).wait_recv()

    for source in range(line):
        for piece in range(pieces):
            for peer in others:
                landed((peer - rank * QUAD + source * QUAD) * pieces + piece)
    if relayed:

        @pl.when(at_end)
        def _():
            for piece in range(pieces):
                landed(((line - 1 - rank) * QUAD + lead) * pieces + piece)

    leaving = [
        (
            pltpu.make_async_remote_copy(
                src_ref=picked.at[slot],
                dst_ref=out_ref.at[0],
                send_sem=pick_send.at[slot],
                recv_sem=pick_recv.at[0],
                device_id={"sta": twin},
                device_id_type=MESH,
            ),
            there,
        )
        for slot, there in enumerate(picks_sent)
    ]
    def kept_done(slot):
        pltpu.make_async_copy(kept.at[slot], out_ref.at[0], keep_sems.at[slot]).wait()

    for slot, there in enumerate(kept_there):
        if there is None:
            kept_done(slot)
        else:

            @pl.when(there)
            def _():
                kept_done(slot)

    for copy, there in leaving + passed:
        if there is None:
            copy.wait_send()
        else:

            @pl.when(there)
            def _():
                copy.wait_send()

    @pl.when(me < members - 1)
    def _():
        halo_copy.wait_send()


def correlate_kernel(
    starts_ref,
    low_ref,
    taper_ref,
    dft_hbm,
    lag_hbm,
    out_hbm,
    out_ref,
    dft_ref,
    lag_ref,
    ahead,
    back,
    theirs,
    own,
    white_own,
    left,
    right,
    cross_real,
    cross_imag,
    dft_sems,
    lag_sem,
    out_sems,
):
    planes = low_ref.shape[0]
    window_count = starts_ref.shape[0]
    lane = lax.broadcasted_iota(jnp.int32, (1, LANE), 1)
    dft_copies = [
        pltpu.make_async_copy(
            dft_hbm.at[:, n * HT : (n + 1) * HT, :], dft_ref.at[:, n * HT : (n + 1) * HT, :], dft_sems.at[n]
        )
        for n in range(TILES)
    ]
    lag_copy = pltpu.make_async_copy(lag_hbm, lag_ref, lag_sem)

    for copy in dft_copies:
        copy.start()
    lag_copy.start()
    mirror = (
        lax.broadcasted_iota(jnp.int32, (LANE, LANE), 0) + lax.broadcasted_iota(jnp.int32, (LANE, LANE), 1) == LANE
    ).astype(jnp.float32).astype(jnp.bfloat16)

    def one_plane(n, carry):
        samples = low_ref[n]
        ahead[n] = samples.astype(jnp.float32)
        turned = jnp.dot(samples, mirror, preferred_element_type=jnp.float32)
        later = low_ref[jnp.minimum(n + 1, planes - 1)].astype(jnp.float32)
        later = jnp.where(n + 1 < planes, later, jnp.zeros_like(later))
        back[planes - 1 - n] = jnp.where(lane == 0, later, turned)
        return carry

    lax.fori_loop(0, planes, one_plane, 0, unroll=32)

    def one_window(w, carry):
        start = starts_ref[w]
        plane, rest = start // LANE, start % LANE
        taper = taper_ref[...]
        fore = pltpu.roll(taper, rest, 1)
        hind = pltpu.roll(taper, (LANE - rest) % LANE, 1)
        span = SEG // LANE
        rise = [jnp.where(lane >= rest, fore[p + 1 : p + 2], fore[p : p + 1]) for p in range(FOLD // LANE + 1)]
        fall = [
            jnp.where(lane < LANE - rest, hind[p + 1 : p + 2], hind[p + 2 : p + 3]) for p in range(FOLD // LANE)
        ]
        at = pl.ds(pl.multiple_of(w * THEIRS, SB), THEIRS)
        own_at = pl.ds(pl.multiple_of(w * SB, SB), SB)

        def put(kind, p, values):
            values = values.astype(jnp.bfloat16)
            lanes = slice(p * LANE, (p + 1) * LANE)
            theirs[kind, at, lanes] = values[:THEIRS]
            own[kind, own_at, lanes] = values[THEIRS:]

        last = FOLD // LANE
        a = rise[last] * ahead[plane + last]
        b = (1.0 - rise[last]) * ahead[plane + last + span // 2]
        put(0, last, a + b)
        middle = a - b
        for p in range(FOLD // LANE):
            first = ahead[plane + p]
            if p == 0:
                first = jnp.where(lane < rest, ahead[jnp.minimum(plane + span, planes - 1)], first)
            a = rise[p] * first
            b = (1.0 - rise[p]) * ahead[plane + span // 2 + p]
            c = fall[p] * back[planes - plane - span + p]
            d = (1.0 - fall[p]) * back[planes - plane - span // 2 + p]
            same, apart = a + b, a - b
            same_turned, apart_turned = d + c, d - c
            put(0, p, same + same_turned)
            put(1, p, apart - apart_turned)
            put(2, p, same - same_turned)
            summed = apart + apart_turned
            put(3, p, jnp.where(lane == 0, middle, summed) if p == 0 else summed)
        return carry

    lax.fori_loop(0, window_count, one_window, 0, unroll=16)

    def dot_nt(a, b):
        return lax.dot_general(a, b, NT, preferred_element_type=jnp.float32)

    depth = (FOLD + LANE, FOLD, FOLD, FOLD)
    half = LANE // 2
    wide = 2 * LANE
    first = lane < half
    slots = LANE // PACK
    turns = slots // 2
    strip = BAND // 2
    halves = HT // PACK
    own_bin = lax.broadcasted_iota(jnp.int32, (PACK * SB, LANE), 0) // SB
    mask = (own_bin == lax.broadcasted_iota(jnp.int32, (PACK * SB, LANE), 1) % PACK).astype(jnp.float32).astype(
        jnp.bfloat16
    )

    def one_group(tile, n):
        masked = jnp.concatenate([jnp.concatenate([left[tile, n, h]] * PACK, axis=0) * mask for h in range(2)], axis=1)
        product = jnp.dot(masked, right[tile, n], preferred_element_type=jnp.float32)
        product = product.reshape(PACK, 2, SB // 2, LANE)
        a, b = product[:, 0].reshape(PACK * SB // 2, LANE), product[:, 1].reshape(PACK * SB // 2, LANE)
        turned = pltpu.roll(jnp.where(first, b, a), half, 1)
        row = (tile * (FT // PACK) + n) * PACK * SB // 2
        at = pl.ds(row if isinstance(n, int) else pl.multiple_of(row, PACK * SB // 2), PACK * SB // 2)
        cross_real[at, :] = jnp.where(first, a, turned)
        cross_imag[at, :] = jnp.where(first, turned, b)

    def transforms(tile):
        dft_copies[tile].wait()
        bins = slice(tile * HT, (tile + 1) * HT)
        for tile_pair in range(window_count * THEIRS // wide):
            at = slice(tile_pair * wide, (tile_pair + 1) * wide)
            spectra = [dot_nt(dft_ref[k, bins, : depth[k]], theirs[k, at, : depth[k]]) for k in range(4)]
            for n in range(HT // strip):
                for inner in range(wide // LANE):
                    parts = [x[n * strip : (n + 1) * strip, inner * LANE : (inner + 1) * LANE] for x in spectra]
                    power = sum(x * x for x in parts[1:]) + parts[0] * parts[0]
                    level = jnp.sum(power, axis=0, keepdims=True)
                    scale = lax.rsqrt(level * (1.0 / (2 * BAND)) + 1e-06)
                    for parity in range(2):
                        real, imag = parts[parity] * scale, parts[2 + parity] * scale

                        def stacked(x, y):
                            both = [v.reshape(strip // PACK, 1, PACK, LANE) for v in (x, y)]
                            both = jnp.concatenate(both, axis=1).reshape(strip * 2, LANE)
                            return both.astype(jnp.bfloat16)

                        plain, crossed = stacked(real, imag), stacked(-imag, real)
                        turned = pltpu.roll(jnp.where(first, crossed, plain), half, 1)
                        for k, block in enumerate((jnp.where(first, plain, turned), jnp.where(first, turned, crossed))):
                            w = (tile_pair * (wide // LANE) + inner) * 2 + k
                            for m in range(strip // PACK):
                                group = n * (strip // PACK) + m
                                turn = group % slots // 2
                                row = w // turns * LANE + (w + turn) % turns * 2 * PACK
                                right[tile, parity * halves + group, row : row + 2 * PACK, :] = block[
                                    m * 2 * PACK : (m + 1) * 2 * PACK
                                ]

        spectra = [dot_nt(own[k, :, : depth[k]], dft_ref[k, bins, : depth[k]]) for k in range(4)]
        power = sum(x * x for x in spectra[1:]) + spectra[0] * spectra[0]
        same = (
            lax.broadcasted_iota(jnp.int32, (HT, HT), 0) // strip == lax.broadcasted_iota(jnp.int32, (HT, HT), 1) // strip
        ).astype(jnp.float32).astype(jnp.bfloat16)
        level = jnp.dot(power.astype(jnp.bfloat16), same, preferred_element_type=jnp.float32)
        scale = lax.rsqrt(level * (1.0 / (2 * BAND)) + 1e-06)
        for k in range(4):
            white_own[tile, k] = (spectra[k] * scale).astype(jnp.bfloat16)

        low_slot = lane // PACK % 2 == 0
        for parity in range(2):
            for part in range(HT // LANE):
                for h in range(window_count // turns):
                    moved = [[], []]
                    for w in range(turns):
                        row = (h * turns + w) * SB
                        x = [
                            white_own[tile, 2 * c + parity, row : row + SB, part * LANE : (part + 1) * LANE] for c in range(2)
                        ]
                        y = (
                            jnp.where(low_slot, x[0], pltpu.roll(x[1], PACK, 1)),
                            jnp.where(low_slot, pltpu.roll(x[0], LANE - PACK, 1), x[1]),
                        )
                        for k in range(2):
                            moved[k].append(pltpu.roll(y[k], 2 * PACK * w, 1) if w else y[k])
                    for slot in range(slots):
                        turn, k = slot // 2, slot % 2
                        joined = moved[k][0]
                        for w in range(1, turns):
                            joined = jnp.where(lane // (2 * PACK) == (turn + w) % turns, moved[k][w], joined)
                        left[tile, parity * halves + part * slots + slot, h] = joined

    def products(tile):
        def several(n, carry):
            one_group(tile, n)
            return carry

        lax.fori_loop(0, FT // PACK, several, 0, unroll=32)

    for tile in range(TILES):
        transforms(tile)
        if tile:
            products(tile - 1)
    products(TILES - 1)

    lag_copy.wait()
    out_copies = []
    for n in range(SB // 4):
        summed = None
        for k, cross in enumerate((cross_real, cross_imag)):
            columns = jnp.concatenate(
                [cross[pl.ds(2 * n + m, BINS, stride=SB // 2), :].astype(jnp.bfloat16) for m in range(2)], axis=1
            )
            term = jnp.dot(lag_ref[k], columns, preferred_element_type=jnp.float32)
            summed = term if summed is None else summed + term
        turned = summed.T
        for h in range(2):
            station = h * (SB // 2) + 2 * n
            for m in range(2):
                for r in range(ROUNDS):
                    row = ((m * 2 + h) * ROUNDS + r) * SB
                    out_ref[r, (station + m) * SB : (station + m + 1) * SB, :] = turned[row : row + SB]
            rows = slice(station * SB, (station + 2) * SB)
            copy = pltpu.make_async_copy(
                out_ref.at[:, rows, :], out_hbm.at[:, rows, :], out_sems.at[len(out_copies)]
            )
            copy.start()
            out_copies.append(copy)
    for copy in out_copies:
        copy.wait()


def correlate(window_starts, low, taper, dft, lag):
    window_count = window_starts.shape[0]
    planes = low.shape[0]
    in_vmem = pl.BlockSpec(memory_space=pltpu.VMEM)
    anywhere = pl.BlockSpec(memory_space=pl.ANY)
    return pl.pallas_call(
        correlate_kernel,
        in_specs=[pl.BlockSpec(memory_space=pltpu.SMEM), in_vmem, in_vmem, anywhere, anywhere],
        out_specs=anywhere,
        out_shape=jax.ShapeDtypeStruct((ROUNDS, SB * SB, LAGS), jnp.float32),
        scratch_shapes=[
            pltpu.VMEM((ROUNDS, SB * SB, LAGS), jnp.float32),
            pltpu.VMEM(dft.shape, jnp.bfloat16),
            pltpu.VMEM(lag.shape, jnp.bfloat16),
            pltpu.VMEM((planes, ROWS, LANE), jnp.float32),
            pltpu.VMEM((planes, ROWS, LANE), jnp.float32),
            pltpu.VMEM((4, window_count * THEIRS, FOLD + LANE), jnp.bfloat16),
            pltpu.VMEM((4, window_count * SB, FOLD + LANE), jnp.bfloat16),
            pltpu.VMEM((TILES, 4, window_count * SB, HT), jnp.bfloat16),
            pltpu.VMEM((TILES, FT // PACK, 2, SB, LANE), jnp.bfloat16),
            pltpu.VMEM((TILES, FT // PACK, 2 * LANE, LANE), jnp.bfloat16),
            pltpu.VMEM((BINS * SB // 2, LANE), jnp.float32),
            pltpu.VMEM((BINS * SB // 2, LANE), jnp.float32),
            pltpu.SemaphoreType.DMA((TILES,)),
            pltpu.SemaphoreType.DMA,
            pltpu.SemaphoreType.DMA((SB // 2,)),
        ],
        compiler_params=pltpu.CompilerParams(vmem_limit_bytes=60 * 2**20),
    )(window_starts, low, taper, dft, lag)


def body(raw_traces, filter_taps, station_order, window_starts, pairing):
    members = lax.axis_size("sta")
    stations, local_time = raw_traces.shape
    window_count = window_starts.shape[0]
    pieces = local_time // (LANE * DEC)
    line = members // QUAD
    in_vmem = pl.BlockSpec(memory_space=pltpu.VMEM)
    low = pl.pallas_call(
        functools.partial(gather_kernel, members),
        out_shape=jax.ShapeDtypeStruct((members * pieces, ROWS, LANE), jnp.bfloat16),
        in_specs=[
            pl.BlockSpec(memory_space=pl.ANY),
            in_vmem,
            in_vmem,
            pl.BlockSpec(memory_space=pltpu.SMEM),
        ],
        out_specs=pl.BlockSpec(memory_space=pl.ANY),
        scratch_shapes=[
            pltpu.VMEM((stations, local_time), jnp.bfloat16),
            pltpu.VMEM((stations // 2, LANE), jnp.bfloat16),
            pltpu.VMEM((stations // 2, LANE), jnp.bfloat16),
            pltpu.VMEM((line, pieces, stations, LANE), jnp.bfloat16),
            pltpu.VMEM((stations // SB, SB, LANE), jnp.bfloat16),
            pltpu.VMEM(((3 * line + QUAD) * pieces, ROWS, LANE), jnp.bfloat16),
            pltpu.VMEM((line * pieces, ROWS, LANE), jnp.bfloat16),
            pltpu.SemaphoreType.DMA((line * pieces,)),
            pltpu.SemaphoreType.DMA,
            pltpu.SemaphoreType.DMA((2,)),
            pltpu.SemaphoreType.DMA(((line + 1) * pieces,)),
            pltpu.SemaphoreType.DMA((line * pieces,)),
            pltpu.SemaphoreType.DMA(((3 * line + QUAD) * pieces,)),
            pltpu.SemaphoreType.DMA((members * pieces,)),
        ],
        compiler_params=pltpu.CompilerParams(
            collective_id=0, has_side_effects=True, vmem_limit_bytes=60 * 2**20
        ),
    )(raw_traces, filter_taps, station_order.reshape(1, stations), pairing)
    correlated = correlate(
        window_starts,
        low,
        jnp.asarray(taper_table()),
        jnp.asarray(dft_table()),
        jnp.asarray(lag_table(window_count)),
    )
    return correlated.reshape(ROUNDS, SB, SB, LAGS)


def solution(mesh):
    return jax.shard_map(
        body,
        mesh=mesh,
        in_specs=(P("parts", "sta"), P(), P("parts"), P("parts"), P()),
        out_specs=P(None, ("parts", "sta"), None, None),
        check_vma=False,
    )
```
